512 devices in a mesh: dp: 4 (over z_lo), seq: 16 (over y, z_hi), tensor: 8 (over x, core).
Axes of the slice: x: 4, y: 8, z: 8 (z_hi: 2, z_lo: 4; z = z_hi * 4 + z_lo), core: 2. Of those that a mesh axis runs over, the one named last changes fastest.
Arguments:
- inputs: bfloat16 [4, 4096, 1536], P('dp', 'seq', 'tensor'), may hold values from -6 to 6
- targets: bfloat16 [4, 4096, 1536], P('dp', 'seq', 'tensor'), may hold values from -6 to 6
- block_mix: bfloat16 [256, 256], replicated, may hold values from -0.375 to 0.375
- cross_mix: bfloat16 [16, 16], replicated, may hold values from -1.5 to 1.5
- twiddle_in: float32 [16, 256], P('seq'), may hold values from 0.5 to 1.5
- twiddle_out: float32 [16, 256], P(None, 'seq'), may hold values from 0.5 to 1.5
- norm_gain: float32 [1536], replicated, may hold values from 0.3 to 2.8
- w_gate: bfloat16 [1536, 3072], P(None, 'tensor'), may hold values from -0.15625 to 0.15625
- w_up: bfloat16 [1536, 3072], P(None, 'tensor'), may hold values from -0.15625 to 0.15625
- w_down: bfloat16 [1536, 3072], P(None, 'tensor'), may hold values from -0.109375 to 0.109375
Outputs:
- output: bfloat16 [4, 4096, 1536], P('dp', 'seq', 'tensor')
- d_input: bfloat16 [4, 4096, 1536], P('dp', 'seq', 'tensor')
- grad_down: float32 [1536, 3072], P(('dp', 'seq'), 'tensor')
The draws below stay inside these ranges and needn't reach their ends.
All inputs are finite; a program needn't handle non-finite values.
Results may differ from the reference program's by a relative error of at most 0.022.
Values may be sent and summed in bfloat16 or wider, within the bound.
A program may use at most 64 MiB of HBM per device.

```python
import jax
import jax.numpy as jnp
from jax import lax

D = 1536
FFN = 3072
BLOCK = 256
NBLK = 16
TOKENS = 4096
SEQS = 4
N_TENSOR = 8


def draw_norm_gain(key, part):
    key = jax.random.fold_in(key, 7)
    ramp = jnp.arange(D, dtype=jnp.float32) / (D - 1)
    base = 0.6 + 1.2 * ramp
    spread = jax.random.uniform(key, (D,), jnp.float32, 0.8, 1.25)
    return base * spread


def shard_levels(stream_key, extent, cuts, low, high):
    factor_of = 1.0
    for axis_at, parts in cuts:
        draws = jax.random.uniform(jax.random.fold_in(jax.random.fold_in(stream_key, 6), axis_at), (parts,), jnp.float32, low / len(cuts), high / len(cuts))
        factor_of = factor_of * jnp.repeat(jnp.exp(draws), extent[axis_at] // parts).reshape((-1,) + (1,) * (len(extent) - 1 - axis_at))
    return factor_of


def normal_values(own_key, shape, scale, reach, pieces=(), kind=jnp.bfloat16):
    drawn = scale * jax.random.normal(own_key, shape, jnp.float32)
    if pieces:
        drawn = drawn * shard_levels(own_key, shape, pieces, -0.22, 0.18)
    return jnp.clip(drawn, -reach, reach).astype(kind)


def setup_inputs(seed: int = 0) -> dict:
    splits = jax.random.split(jax.random.key(seed), 11)
    return {
        "inputs": normal_values(splits[0], (SEQS, TOKENS, D), 1.0, 6.0, ((0, 4), (1, 16), (2, 8))),
        "targets": normal_values(splits[1], (SEQS, TOKENS, D), 1.0, 6.0, ((0, 4), (1, 16), (2, 8))),
        "block_mix": normal_values(splits[2], (BLOCK, BLOCK), BLOCK ** -0.5, 0.375),
        "cross_mix": normal_values(splits[3], (NBLK, NBLK), NBLK ** -0.5, 1.5),
        "twiddle_in": jnp.clip(0.5 + 1.0 * jax.random.uniform(splits[4], (NBLK, BLOCK), jnp.float32) ** shard_levels(splits[4], (NBLK, BLOCK), ((0, 16),), -0.2, 0.2), 0.5, 1.5),
        "twiddle_out": jnp.clip(0.5 + 1.0 * jax.random.uniform(splits[5], (NBLK, BLOCK), jnp.float32) ** shard_levels(splits[5], (NBLK, BLOCK), ((1, 16),), -0.2, 0.2), 0.5, 1.5),
        "norm_gain": draw_norm_gain(jax.random.fold_in(splits[10], 71), 0),
        "w_gate": normal_values(splits[7], (D, FFN), D ** -0.5, 0.15625, ((1, 8),)),
        "w_up": normal_values(splits[8], (D, FFN), D ** -0.5, 0.15625, ((1, 8),)),
        "w_down": normal_values(splits[9], (D, FFN), FFN ** -0.5, 0.109375, ((1, 8),)),
    }


def reference(inputs, targets, block_mix, cross_mix, twiddle_in, twiddle_out, norm_gain, w_gate, w_up, w_down):
    highest = lax.Precision.HIGHEST
    group_width = FFN // N_TENSOR
    block_f = block_mix.astype(jnp.float32)
    cross_f = cross_mix.astype(jnp.float32)
    contract_last = (((1,), (1,)), ((), ()))
    contract_first = (((0,), (0,)), ((), ()))
    outputs = []
    d_inputs = []
    grad_down = jnp.zeros((D, FFN), jnp.float32)
    for seq_id in range(SEQS):
        source = inputs[seq_id]
        blocks = source.reshape(NBLK, BLOCK, D).astype(jnp.float32)
        section_mix = (jnp.einsum('pqc,qj->pjc', blocks, block_f, precision=highest) * twiddle_in[:, :, None]).astype(jnp.bfloat16)
        mixed = (jnp.einsum('pjc,pk->kjc', section_mix.astype(jnp.float32), cross_f, precision=highest) * twiddle_out[:, :, None]).astype(jnp.bfloat16)
        residual = (source.astype(jnp.float32) + mixed.reshape(TOKENS, D).astype(jnp.float32)).astype(jnp.bfloat16)
        res_f = residual.astype(jnp.float32)
        inv_rms = lax.rsqrt(lax.optimization_barrier(jnp.mean(res_f * res_f, axis=1, keepdims=True)) + 1e-05)
        normed = (res_f * inv_rms * norm_gain).astype(jnp.bfloat16)
        gate_pre = jnp.dot(normed, w_gate, preferred_element_type=jnp.float32)
        up_pre = jnp.dot(normed, w_up, preferred_element_type=jnp.float32)
        sigmoid_gate = jax.nn.sigmoid(gate_pre)
        hidden = (gate_pre * sigmoid_gate * up_pre).astype(jnp.bfloat16)
        projected = jnp.zeros((TOKENS, D), jnp.float32)
        for group in range(N_TENSOR):
            lower = group * group_width
            upper = lower + group_width
            partial_value = lax.dot_general(hidden[:, lower:upper], w_down[:, lower:upper], contract_last, preferred_element_type=jnp.float32)
            projected = projected + lax.optimization_barrier(partial_value.astype(jnp.bfloat16)).astype(jnp.float32)
        summed_out = res_f + projected
        outputs.append(summed_out.astype(jnp.bfloat16))
        cotangent = (summed_out - targets[seq_id].astype(jnp.float32)).astype(jnp.bfloat16)
        grad_down = grad_down + lax.dot_general(cotangent, hidden, contract_first, preferred_element_type=jnp.float32)
        d_hidden = jnp.dot(cotangent, w_down, preferred_element_type=jnp.float32)
        d_gate = (d_hidden * up_pre * sigmoid_gate * (1.0 + gate_pre * (1.0 - sigmoid_gate))).astype(jnp.bfloat16)
        d_up = (d_hidden * gate_pre * sigmoid_gate).astype(jnp.bfloat16)
        d_normed = jnp.zeros((TOKENS, D), jnp.float32)
        for group in range(N_TENSOR):
            lower = group * group_width
            upper = lower + group_width
            partial_value = lax.dot_general(d_gate[:, lower:upper], w_gate[:, lower:upper], contract_last, preferred_element_type=jnp.float32)
            partial_value = partial_value + lax.dot_general(d_up[:, lower:upper], w_up[:, lower:upper], contract_last, preferred_element_type=jnp.float32)
            d_normed = d_normed + lax.optimization_barrier(partial_value.astype(jnp.bfloat16)).astype(jnp.float32)
        unit = res_f * inv_rms
        scaled = norm_gain * d_normed
        correction = lax.optimization_barrier(jnp.mean(scaled * unit, axis=1, keepdims=True))
        d_resid = (cotangent.astype(jnp.float32) + inv_rms * (scaled - unit * correction)).astype(jnp.bfloat16)
        back_weighted = lax.optimization_barrier((d_resid.reshape(NBLK, BLOCK, D).astype(jnp.float32) * twiddle_out[:, :, None]).astype(jnp.bfloat16))
        back_section = lax.optimization_barrier(jnp.einsum('kjc,pk->pjc', back_weighted.astype(jnp.float32), cross_f, precision=highest).astype(jnp.bfloat16))
        back_scaled = lax.optimization_barrier((back_section.astype(jnp.float32) * twiddle_in[:, :, None]).astype(jnp.bfloat16))
        d_mix = jnp.einsum('pjc,qj->pqc', back_scaled.astype(jnp.float32), block_f, precision=highest).reshape(TOKENS, D)
        d_inputs.append((d_resid.astype(jnp.float32) + d_mix).astype(jnp.bfloat16))
    return (jnp.stack(outputs), jnp.stack(d_inputs), grad_down)
```

```python
import functools

import jax
import jax.numpy as jnp
from jax import lax
from jax.experimental import pallas as pl
from jax.experimental.pallas import tpu as pltpu
from jax.sharding import PartitionSpec as P

F32 = jnp.float32
BF16 = jnp.bfloat16
MESH = pl.DeviceIdType.MESH

TOK = 256
CH = 192
HID = 384
NSEQ = 16
NTEN = 8
POS = 16
D = 1536
GY = 256
GZ = HID - GY
ROWS = 24
EPS = 1e-05


def mm(a, b, ca=1, cb=0):
    return lax.dot_general(a, b, (((ca,), (cb,)), ((), ())), preferred_element_type=F32)


def eye(n, dtype=BF16):
    rows = lax.broadcasted_iota(jnp.int32, (n, n), 0)
    cols = lax.broadcasted_iota(jnp.int32, (n, n), 1)
    return jnp.where(rows == cols, 1.0, 0.0).astype(dtype)


def column_of(row):
    n = row.shape[1]
    return jnp.sum(eye(n, F32) * row, axis=1, keepdims=True)


def kernel(
    x_ref, tgt_ref, bm_ref, cm_ref, ti_ref, to_ref, gain_ref, wg_hbm, wu_hbm, wd_hbm,
    out_ref, din_ref, gd_ref,
    wg, wu, wd, wguT, wdT, kron, kronT,
    a1s, a1r, a2s, a2r, a3s, a3r, a4s, a4r,
    r1, r2, v1, v2,
    p1, p2, sb1, sb2, q1, q2, t1, t2, own, gate_s, up_s, hid_s, res_s,
    ya, yr, zb, zr, y2s, y2r, z2s, z2r,
    wsem, a_ss, a_rs, ag_ss, ag_rs, sib_ss, sib_rs, v_ss, v_rs,
    rsib_ss, rsib_rs, rs_ss, rs_rs, g_ss, g_rs,
):
    dp = lax.axis_index("dp")
    sq = lax.axis_index("seq")
    tn = lax.axis_index("tensor")
    x, c = tn // 2, tn % 2
    y, zh = sq // 2, sq % 2
    z = zh * 4 + dp

    def seq_dev(s):
        return (dp, s, tn)

    def ten_dev(t):
        return (dp, sq, t)

    def y_dev(yy):
        return (dp, yy * 2 + zh, tn)

    def z_dev(zz):
        return (lax.rem(zz, 4), y * 2 + zz // 4, tn)

    sent = []

    def send(src, dst, ss, rs, dev):
        cp = pltpu.make_async_remote_copy(
            src_ref=src, dst_ref=dst, send_sem=ss, recv_sem=rs, device_id=dev, device_id_type=MESH
        )
        cp.start()
        sent.append(cp)

    def wait_recv(buf, ss, rs):
        pltpu.make_async_remote_copy(
            src_ref=buf, dst_ref=buf, send_sem=ss, recv_sem=rs,
            device_id=(dp, sq, tn), device_id_type=MESH,
        ).wait_recv()

    barrier = pltpu.get_barrier_semaphore()

    def greet(dev):
        pl.semaphore_signal(barrier, inc=1, device_id=dev, device_id_type=MESH)

    def greet_seq(i, carry):
        greet(seq_dev(lax.rem(sq + i, NSEQ)))
        return carry

    def greet_ten(i, carry):
        greet(ten_dev(lax.rem(tn + i, NTEN)))
        return carry

    lax.fori_loop(1, NSEQ, greet_seq, 0)
    lax.fori_loop(1, NTEN, greet_ten, 0)
    for i in (1, 2, 3, 5, 6, 7):
        greet(z_dev(lax.rem(z + i, 8)))

    loads = []
    for n, (src, dst) in enumerate(((wg_hbm, wg), (wu_hbm, wu), (wd_hbm, wd))):
        cp = pltpu.make_async_copy(src, dst, wsem.at[n])
        cp.start()
        loads.append(cp)

    def all_to_all_send(n, src, dst):
        def one(i, carry):
            peer = lax.rem(sq + i, NSEQ)
            pltpu.make_async_remote_copy(
                src_ref=src.at[peer], dst_ref=dst.at[sq],
                send_sem=a_ss.at[n, peer], recv_sem=a_rs.at[n, sq],
                device_id=seq_dev(peer), device_id_type=MESH,
            ).start()
            return carry

        lax.fori_loop(1, NSEQ, one, 0)
        dst[sq] = src[sq]

    def all_to_all_wait(n, src, dst):
        def one(i, carry):
            peer = lax.rem(sq + i, NSEQ)
            wait_recv(dst.at[peer], a_ss.at[n, peer], a_rs.at[n, peer])
            return carry

        lax.fori_loop(1, NSEQ, one, 0)

    def all_to_all_done(n, src):
        def one(i, carry):
            peer = lax.rem(sq + i, NSEQ)
            pltpu.make_async_remote_copy(
                src_ref=src.at[peer], dst_ref=src.at[peer],
                send_sem=a_ss.at[n, peer], recv_sem=a_rs.at[n, peer],
                device_id=seq_dev(peer), device_id_type=MESH,
            ).wait_send()
            return carry

        lax.fori_loop(1, NSEQ, one, 0)

    tin = column_of(ti_ref[...])
    section = mm(bm_ref[...], x_ref[...], 0, 0) * tin
    a1s[...] = section.astype(BF16).reshape(NSEQ, POS, CH)

    pl.semaphore_wait(barrier, (NSEQ - 1) + (NTEN - 1) + 6)
    all_to_all_send(0, a1s, a1r)

    rows = lax.broadcasted_iota(jnp.int32, (TOK, NSEQ), 0)
    cols = lax.broadcasted_iota(jnp.int32, (TOK, NSEQ), 1)
    pick_block = jnp.where(rows // POS == cols, 1.0, 0.0)
    pick_pos = jnp.where(rows % POS == cols, 1.0, 0.0)
    cross = cm_ref[...]
    wide = mm(pick_block.astype(BF16), cross, 1, 1).astype(BF16)
    wide = mm(wide, pick_block.astype(BF16), 1, 1)
    wideT = mm(pick_block.astype(BF16), cross, 1, 0).astype(BF16)
    wideT = mm(wideT, pick_block.astype(BF16), 1, 1)
    big_r = lax.broadcasted_iota(jnp.int32, (TOK, TOK), 0)
    big_c = lax.broadcasted_iota(jnp.int32, (TOK, TOK), 1)
    same_pos = (big_r % POS) == (big_c % POS)
    kron[...] = jnp.where(same_pos, wide, 0.0).astype(BF16)
    kronT[...] = jnp.where(same_pos, wideT, 0.0).astype(BF16)
    tout_all = jnp.broadcast_to(to_ref[...][:, None, :], (NSEQ, POS, POS)).reshape(TOK, POS)
    tout = jnp.sum(tout_all * pick_pos, axis=1, keepdims=True)
    gains = gain_ref[...]
    gain_row = jnp.zeros((1, CH), F32)
    for r in range(NTEN):
        gain_row = gain_row + jnp.where(tn == r, gains[:, r * CH : (r + 1) * CH], 0.0)
    gain = column_of(gain_row)
    for cp in loads:
        cp.wait()
    eye_h = eye(HID)
    for k in range(4):
        block = slice(k * HID, (k + 1) * HID)
        wguT[k, 0:HID, :] = mm(eye_h, wg[block, :], 1, 1).astype(BF16)
        wguT[k, HID : 2 * HID, :] = mm(eye_h, wu[block, :], 1, 1).astype(BF16)
        wdT[k] = mm(eye_h, wd[block, :], 1, 1).astype(BF16)
    eye_c = eye(CH)
    eye_t = eye(TOK)
    tgtT = mm(eye_c, tgt_ref[...], 1, 1)

    all_to_all_wait(0, a1s, a1r)

    mixed = mm(kron[...], a1r[...].reshape(TOK, CH)) * tout
    a2s[...] = mixed.astype(BF16).reshape(NSEQ, POS, CH)
    all_to_all_send(1, a2s, a2r)
    all_to_all_wait(1, a2s, a2r)

    residual = (x_ref[...].astype(F32) + a2r[...].reshape(TOK, CH).astype(F32)).astype(BF16)
    res = mm(eye_c, residual, 1, 1)
    res_s[...] = res

    def share_row(n, buf, row):
        buf[tn] = jnp.broadcast_to(row, (8, TOK))

        def one(i, carry):
            peer = lax.rem(tn + i, NTEN)
            pltpu.make_async_remote_copy(
                src_ref=buf.at[tn], dst_ref=buf.at[tn],
                send_sem=v_ss.at[n, peer], recv_sem=v_rs.at[n, tn],
                device_id=ten_dev(peer), device_id_type=MESH,
            ).start()
            return carry

        lax.fori_loop(1, NTEN, one, 0)

    def sum_rows(n, buf):
        def one(i, carry):
            peer = lax.rem(tn + i, NTEN)
            wait_recv(buf.at[peer], v_ss.at[n, peer], v_rs.at[n, peer])
            return carry

        lax.fori_loop(1, NTEN, one, 0)
        return jnp.sum(buf[:, 0:1, :], axis=0)

    def rows_done(n, buf):
        def one(i, carry):
            peer = lax.rem(tn + i, NTEN)
            pltpu.make_async_remote_copy(
                src_ref=buf.at[tn], dst_ref=buf.at[tn],
                send_sem=v_ss.at[n, peer], recv_sem=v_rs.at[n, peer],
                device_id=ten_dev(peer), device_id_type=MESH,
            ).wait_send()
            return carry

        lax.fori_loop(1, NTEN, one, 0)

    chips = [lax.rem(x + d, 4) for d in range(4)]
    other = 1 - c
    HALF = CH // 2

    def gather_start(n, buf):
        for h in range(2):
            part = buf.at[tn, pl.ds(h * HALF, HALF)]
            for d in (2, 1, 3):
                send(part, part, ag_ss.at[n, d, h], ag_rs.at[n, d, h], ten_dev(chips[d] * 2 + c))
            send(part, part, sib_ss.at[n, 0, h], sib_rs.at[n, 0, h], ten_dev(x * 2 + other))

    def gather_forward(n, buf):
        for d in (1, 3, 2):
            src = lax.rem(x + 4 - d, 4) * 2 + c
            for h in range(2):
                part = buf.at[src, pl.ds(h * HALF, HALF)]
                wait_recv(part, ag_ss.at[n, d, h], ag_rs.at[n, d, h])
                send(part, part, sib_ss.at[n, d, h], sib_rs.at[n, d, h], ten_dev(x * 2 + other))

    def gather_chip(n, buf, d):
        chip = lax.rem(x + 4 - d, 4)
        for h in range(2):
            part = buf.at[chip * 2 + other, pl.ds(h * HALF, HALF)]
            wait_recv(part, sib_ss.at[n, d, h], sib_rs.at[n, d, h])
        return chip, buf[pl.ds(chip * 2, 2)].reshape(2 * CH, TOK)

    def gather_matmul(n, buf, weights):
        acc = None
        for d in (0, 1, 3, 2):
            chip, block = gather_chip(n, buf, d)
            term = mm(weights[chip], block)
            acc = term if acc is None else acc + term
        return acc

    def scatter_start(n, part_of, p, sb, q, t):
        for d in (2, 1, 3, 0):
            p[d] = part_of(chips[d] * 2 + other).astype(BF16)
            send(p.at[d], sb.at[d], rsib_ss.at[n, d], rsib_rs.at[n, d], ten_dev(x * 2 + other))
        for d in (2, 1, 3, 0):
            own[d] = part_of(chips[d] * 2 + c)
        for d in (2, 1, 3):
            wait_recv(sb.at[d], rsib_ss.at[n, d], rsib_rs.at[n, d])
            q[d] = (own[d] + sb[d].astype(F32)).astype(BF16)
            send(q.at[d], t.at[d], rs_ss.at[n, d], rs_rs.at[n, d], ten_dev(chips[d] * 2 + c))

    def scatter_end(n, sb, t):
        wait_recv(sb.at[0], rsib_ss.at[n, 0], rsib_rs.at[n, 0])
        total = own[0] + sb[0].astype(F32)
        for d in (1, 3, 2):
            wait_recv(t.at[d], rs_ss.at[n, d], rs_rs.at[n, d])
            total = total + t[d].astype(F32)
        return total

    r1[tn] = (res * gain).astype(BF16)
    gather_start(0, r1)
    share_row(0, v1, jnp.sum(res * res, axis=0, keepdims=True))
    gather_forward(0, r1)
    pre = gather_matmul(0, r1, wguT)
    inv = lax.rsqrt(sum_rows(0, v1) / D + EPS)
    gate_pre = pre[0:HID] * inv
    up_pre = pre[HID : 2 * HID] * inv
    sig = jax.nn.sigmoid(gate_pre)
    hidden = (gate_pre * sig * up_pre).astype(BF16)
    hid_s[...] = hidden
    gate_s[...] = gate_pre
    up_s[...] = up_pre

    scatter_start(0, lambda r: mm(wd[pl.ds(pl.multiple_of(r * CH, CH), CH), :], hid_s[...]), p1, sb1, q1, t1)
    projected = scatter_end(0, sb1, t1)
    summed = res_s[...] + projected
    cot = (summed - tgtT).astype(BF16)
    r2[tn] = cot
    gather_start(1, r2)
    out_ref[...] = mm(eye_t, summed.astype(BF16), 1, 1).astype(BF16)
    gather_forward(1, r2)
    d_hidden = gather_matmul(1, r2, wdT)

    gate_pre = gate_s[...]
    up_pre = up_s[...]
    sig = jax.nn.sigmoid(gate_pre)
    d_gate = (d_hidden * up_pre * sig * (1.0 + gate_pre * (1.0 - sig))).astype(BF16)
    d_up = (d_hidden * gate_pre * sig).astype(BF16)
    inner = d_gate.astype(F32) * gate_pre + d_up.astype(F32) * up_pre
    share_row(1, v2, jnp.sum(inner, axis=0, keepdims=True))

    def back_part(r):
        block = pl.ds(pl.multiple_of(r * CH, CH), CH)
        return mm(wg[block, :], d_gate) + mm(wu[block, :], d_up)

    scatter_start(1, back_part, p2, sb2, q2, t2)

    hid = hid_s[...]
    for r in range(NTEN):
        g = mm(r2[r], hid, 1, 1)
        zl, yhi = r // 2, r % 2
        for m in range(4):
            ya[yhi * 4 + m, zl * 48 : zl * 48 + 48, :] = g[m * 48 : m * 48 + 48, 0:GY].astype(BF16)
        for half in range(2):
            pieces = [g[m * 48 + half * 24 : m * 48 + half * 24 + 24, GY:HID] for m in range(4)]
            zb[half * 4 + zl, yhi * 96 : yhi * 96 + 96, :] = jnp.concatenate(pieces, axis=0).astype(BF16)

    def grad_send(n, src, dst, me, dev):
        def one(i, carry):
            peer = lax.rem(me + i, 8)
            pltpu.make_async_remote_copy(
                src_ref=src(peer), dst_ref=dst.at[me],
                send_sem=g_ss.at[n, peer], recv_sem=g_rs.at[n, me],
                device_id=dev(peer), device_id_type=MESH,
            ).start()
            return carry

        lax.fori_loop(1, 8, one, 0)

    def grad_sum(n, first, dst, me):
        def one(i, acc):
            peer = lax.rem(me + i, 8)
            wait_recv(dst.at[peer], g_ss.at[n, peer], g_rs.at[n, peer])
            return acc + dst[peer].astype(F32)

        return lax.fori_loop(1, 8, one, first)

    def grad_done(n, src, me, dev):
        def one(i, carry):
            peer = lax.rem(me + i, 8)
            pltpu.make_async_remote_copy(
                src_ref=src(peer), dst_ref=src(peer),
                send_sem=g_ss.at[n, peer], recv_sem=g_rs.at[n, peer],
                device_id=dev(peer), device_id_type=MESH,
            ).wait_send()
            return carry

        lax.fori_loop(1, 8, one, 0)

    def ya_of(yy):
        return ya.at[yy]

    def zb_of(zz):
        return zb.at[zz]

    def y2_of(zz):
        return y2s.at[pl.ds(pl.multiple_of(lax.rem(zz, 4) * 48 + (zz // 4) * 24, 8), ROWS)]

    def z2_of(yy):
        return z2s.at[pl.ds(pl.multiple_of(yy * ROWS, 8), ROWS)]

    grad_send(0, ya_of, yr, y, y_dev)
    grad_send(1, zb_of, zr, z, z_dev)

    d_normed = scatter_end(1, sb2, t2)
    corr = sum_rows(1, v2) / D
    res = res_s[...]
    d_res = (cot.astype(F32) + inv * (gain * d_normed - res * inv * corr)).astype(BF16)
    d_tok = mm(eye_t, d_res, 1, 1)
    a3s[...] = d_tok.astype(BF16).reshape(NSEQ, POS, CH)

    all_to_all_send(2, a3s, a3r)
    all_to_all_wait(2, a3s, a3r)
    weighted = (a3r[...].reshape(TOK, CH).astype(F32) * tout).astype(BF16)
    a4s[...] = mm(kronT[...], weighted).astype(BF16).reshape(NSEQ, POS, CH)
    all_to_all_send(3, a4s, a4r)

    y2s[...] = grad_sum(0, ya[y].astype(F32), yr, y)
    grad_send(2, y2_of, y2r, z, z_dev)
    z2s[...] = grad_sum(1, zb[z].astype(F32), zr, z)
    grad_send(3, z2_of, z2r, y, y_dev)

    all_to_all_wait(3, a4s, a4r)
    scaled = (a4r[...].reshape(TOK, CH).astype(F32) * tin).astype(BF16)
    d_mix = mm(bm_ref[...], scaled)
    din_ref[...] = (a3s[...].reshape(TOK, CH).astype(F32) + d_mix).astype(BF16)

    gd_ref[:, 0:GY] = grad_sum(2, y2s[pl.ds(pl.multiple_of(dp * 48 + zh * 24, 8), ROWS), :], y2r, z)
    gd_ref[:, GY:HID] = grad_sum(3, z2s[pl.ds(pl.multiple_of(y * ROWS, 8), ROWS), :], z2r, y)

    for cp in sent:
        cp.wait_send()
    for n, src in enumerate((a1s, a2s, a3s, a4s)):
        all_to_all_done(n, src)
    rows_done(0, v1)
    rows_done(1, v2)
    grad_done(0, ya_of, y, y_dev)
    grad_done(1, zb_of, z, z_dev)
    grad_done(2, y2_of, z, z_dev)
    grad_done(3, z2_of, y, y_dev)


def body(
    inputs, targets, block_mix, cross_mix, twiddle_in, twiddle_out, norm_gain, w_gate, w_up, w_down
):
    vmem = pl.BlockSpec(memory_space=pltpu.VMEM)
    hbm = pl.BlockSpec(memory_space=pl.ANY)
    dma = pltpu.SemaphoreType.DMA
    chunks = pltpu.VMEM((NSEQ, POS, CH), BF16)
    blocks4 = pltpu.VMEM((4, CH, TOK), BF16)
    output, d_input, grad_down = pl.pallas_call(
        kernel,
        out_shape=(
            jax.ShapeDtypeStruct((TOK, CH), BF16),
            jax.ShapeDtypeStruct((TOK, CH), BF16),
            jax.ShapeDtypeStruct((ROWS, HID), F32),
        ),
        in_specs=[vmem] * 7 + [hbm] * 3,
        out_specs=(vmem, vmem, vmem),
        scratch_shapes=[
            pltpu.VMEM((D, HID), BF16),
            pltpu.VMEM((D, HID), BF16),
            pltpu.VMEM((D, HID), BF16),
            pltpu.VMEM((4, 2 * HID, HID), BF16),
            pltpu.VMEM((4, HID, HID), BF16),
            pltpu.VMEM((TOK, TOK), BF16),
            pltpu.VMEM((TOK, TOK), BF16),
        ]
        + [chunks] * 8
        + [
            pltpu.VMEM((NTEN, CH, TOK), BF16),
            pltpu.VMEM((NTEN, CH, TOK), BF16),
            pltpu.VMEM((NTEN, 8, TOK), F32),
            pltpu.VMEM((NTEN, 8, TOK), F32),
        ]
        + [blocks4] * 8
        + [
            pltpu.VMEM((4, CH, TOK), F32),
            pltpu.VMEM((HID, TOK), F32),
            pltpu.VMEM((HID, TOK), F32),
            pltpu.VMEM((HID, TOK), BF16),
            pltpu.VMEM((CH, TOK), F32),
            pltpu.VMEM((8, CH, GY), BF16),
            pltpu.VMEM((8, CH, GY), BF16),
            pltpu.VMEM((8, CH, GZ), BF16),
            pltpu.VMEM((8, CH, GZ), BF16),
            pltpu.VMEM((CH, GY), F32),
            pltpu.VMEM((8, ROWS, GY), F32),
            pltpu.VMEM((CH, GZ), F32),
            pltpu.VMEM((8, ROWS, GZ), F32),
            dma((3,)),
            dma((4, NSEQ)),
            dma((4, NSEQ)),
            dma((2, 4, 2)),
            dma((2, 4, 2)),
            dma((2, 4, 2)),
            dma((2, 4, 2)),
            dma((2, NTEN)),
            dma((2, NTEN)),
            dma((2, 4)),
            dma((2, 4)),
            dma((2, 4)),
            dma((2, 4)),
            dma((4, 8)),
            dma((4, 8)),
        ],
        compiler_params=pltpu.CompilerParams(
            collective_id=0, has_side_effects=True, vmem_limit_bytes=48 * 1024 * 1024
        ),
        name="monarch_block",
    )(
        inputs[0],
        targets[0],
        block_mix,
        cross_mix,
        twiddle_in,
        twiddle_out,
        norm_gain.reshape(1, D),
        w_gate,
        w_up,
        w_down,
    )
    return output[None], d_input[None], grad_down


def solution(mesh):
    return jax.shard_map(
        body,
        mesh=mesh,
        in_specs=(
            P("dp", "seq", "tensor"),
            P("dp", "seq", "tensor"),
            P(),
            P(),
            P("seq", None),
            P(None, "seq"),
            P(),
            P(None, "tensor"),
            P(None, "tensor"),
            P(None, "tensor"),
        ),
        out_specs=(P("dp", "seq", "tensor"), P("dp", "seq", "tensor"), P(("dp", "seq"), "tensor")),
        check_vma=False,
    )
```

```python
import functools

import jax
import jax.numpy as jnp
from jax import lax
from jax.experimental import pallas as pl
from jax.experimental.pallas import tpu as pltpu
from jax.sharding import PartitionSpec as P

F32 = jnp.float32
BF16 = jnp.bfloat16
MESH = pl.DeviceIdType.MESH

TOK = 256
CH = 192
HID = 384
NSEQ = 16
NTEN = 8
POS = 16
D = 1536
LANES = 128
ROWS = 24
EPS = 1e-05


def mm(a, b, ca=1, cb=0):
    return lax.dot_general(a, b, (((ca,), (cb,)), ((), ())), preferred_element_type=F32)


def eye(n, dtype=BF16):
    rows = lax.broadcasted_iota(jnp.int32, (n, n), 0)
    cols = lax.broadcasted_iota(jnp.int32, (n, n), 1)
    return jnp.where(rows == cols, 1.0, 0.0).astype(dtype)


def column_of(row):
    n = row.shape[1]
    return jnp.sum(eye(n, F32) * row, axis=1, keepdims=True)


def kernel(
    x_hbm, tgt_hbm, bm_hbm, cm_hbm, ti_hbm, to_hbm, gain_hbm, wg_hbm, wu_hbm, wd_hbm,
    out_hbm, din_hbm, gd_hbm,
    out_ref, din_ref, gd_ref, x_ref, tgt_ref, bm_ref, cm_ref, ti_ref, to_ref, gain_ref,
    wg, wu, wd, wguT, wdT, kron, kronT,
    a1s, a1r, a2s, a2r, a3s, a3r, a4s, a4r,
    r1, r2, v1, v2,
    p1, p2, sb1, sb2, q1, q2, t1, t2, own, gate_s, up_s, hid_s, res_s,
    ya, yr, zb, zr, y2s, y2r, z2s, z2r,
    osem, wsem, a_ss, a_rs, ag_ss, ag_rs, sib_ss, sib_rs, v_ss, v_rs,
    rsib_ss, rsib_rs, rs_ss, rs_rs, gy_ss, gy_rs, gz_ss, gz_rs, g2_ss, g2_rs,
):
    dp = lax.axis_index("dp")
    sq = lax.axis_index("seq")
    tn = lax.axis_index("tensor")
    x, c = tn // 2, tn % 2
    y, zh = sq // 2, sq % 2
    z = zh * 4 + dp

    def seq_dev(s):
        return (dp, s, tn)

    def ten_dev(t):
        return (dp, sq, t)

    def y_dev(yy):
        return (dp, yy * 2 + zh, tn)

    def z_dev(zz):
        return (lax.rem(zz, 4), y * 2 + zz // 4, tn)

    pending = []

    def drain():
        while pending:
            pending.pop(0)()


    def send(src, dst, ss, rs, dev):
        cp = pltpu.make_async_remote_copy(
            src_ref=src, dst_ref=dst, send_sem=ss, recv_sem=rs, device_id=dev, device_id_type=MESH
        )
        cp.start()
        pending.append(cp.wait_send)

    def wait_recv(buf, ss, rs):
        pltpu.make_async_remote_copy(
            src_ref=buf, dst_ref=buf, send_sem=ss, recv_sem=rs,
            device_id=(dp, sq, tn), device_id_type=MESH,
        ).wait_recv()

    loads = []
    for n, (src, dst) in enumerate(
        (
            (x_hbm, x_ref), (bm_hbm, bm_ref), (ti_hbm, ti_ref), (cm_hbm, cm_ref), (to_hbm, to_ref),
            (gain_hbm, gain_ref), (wg_hbm, wg), (wu_hbm, wu), (wd_hbm, wd), (tgt_hbm, tgt_ref),
        )
    ):
        cp = pltpu.make_async_copy(src, dst, wsem.at[n])
        loads.append(cp)
    for cp in loads[0:3]:
        cp.start()

    barrier = pltpu.get_barrier_semaphore()

    def greet(dev):
        pl.semaphore_signal(barrier, inc=1, device_id=dev, device_id_type=MESH)

    def greet_seq(i, carry):
        greet(seq_dev(lax.rem(sq + i, NSEQ)))
        return carry

    def greet_ten(i, carry):
        greet(ten_dev(lax.rem(tn + i, NTEN)))
        return carry

    lax.fori_loop(1, NSEQ, greet_seq, 0)
    lax.fori_loop(1, NTEN, greet_ten, 0)
    for i in (1, 2, 3, 5, 6, 7):
        greet(z_dev(lax.rem(z + i, 8)))

    for cp in loads[3:]:
        cp.start()

    def store(n, src, dst):
        cp = pltpu.make_async_copy(src, dst, osem.at[n])
        cp.start()
        pending.append(cp.wait)

    def all_to_all_send(n, src, dst):
        def one(i, carry):
            peer = lax.rem(sq + i, NSEQ)
            pltpu.make_async_remote_copy(
                src_ref=src.at[peer], dst_ref=dst.at[sq],
                send_sem=a_ss.at[n, peer], recv_sem=a_rs.at[n, sq],
                device_id=seq_dev(peer), device_id_type=MESH,
            ).start()
            return carry

        lax.fori_loop(1, NSEQ, one, 0)
        dst[sq] = src[sq]
        pending.append(functools.partial(all_to_all_done, n, src))

    def all_to_all_wait(n, src, dst):
        def one(i, carry):
            peer = lax.rem(sq + i, NSEQ)
            wait_recv(dst.at[peer], a_ss.at[n, peer], a_rs.at[n, peer])
            return carry

        lax.fori_loop(1, NSEQ, one, 0)

    def all_to_all_done(n, src):
        def one(i, carry):
            peer = lax.rem(sq + i, NSEQ)
            pltpu.make_async_remote_copy(
                src_ref=src.at[peer], dst_ref=src.at[peer],
                send_sem=a_ss.at[n, peer], recv_sem=a_rs.at[n, peer],
                device_id=seq_dev(peer), device_id_type=MESH,
            ).wait_send()
            return carry

        lax.fori_loop(1, NSEQ, one, 0)

    for cp in loads[0:3]:
        cp.wait()
    tin = column_of(ti_ref[...])
    section = mm(bm_ref[...], x_ref[...], 0, 1) * tin
    a1s[...] = section.astype(BF16).reshape(NSEQ, POS, CH)

    pl.semaphore_wait(barrier, (NSEQ - 1) + (NTEN - 1) + 6)
    all_to_all_send(0, a1s, a1r)

    rows = lax.broadcasted_iota(jnp.int32, (TOK, NSEQ), 0)
    cols = lax.broadcasted_iota(jnp.int32, (TOK, NSEQ), 1)
    pick_block = jnp.where(rows // POS == cols, 1.0, 0.0)
    pick_pos = jnp.where(rows % POS == cols, 1.0, 0.0)
    for cp in loads[3:6]:
        cp.wait()
    cross = cm_ref[...]
    wide = mm(pick_block.astype(BF16), cross, 1, 1).astype(BF16)
    wide = mm(wide, pick_block.astype(BF16), 1, 1)
    wideT = mm(pick_block.astype(BF16), cross, 1, 0).astype(BF16)
    wideT = mm(wideT, pick_block.astype(BF16), 1, 1)
    big_r = lax.broadcasted_iota(jnp.int32, (TOK, TOK), 0)
    big_c = lax.broadcasted_iota(jnp.int32, (TOK, TOK), 1)
    same_pos = (big_r % POS) == (big_c % POS)
    kron[...] = jnp.where(same_pos, wide, 0.0).astype(BF16)
    kronT[...] = jnp.where(same_pos, wideT, 0.0).astype(BF16)
    tout_all = jnp.broadcast_to(to_ref[...][:, None, :], (NSEQ, POS, POS)).reshape(TOK, POS)
    tout = jnp.sum(tout_all * pick_pos, axis=1, keepdims=True)
    flat = tn * CH + lax.broadcasted_iota(jnp.int32, (CH, 128), 0)
    lane = lax.broadcasted_iota(jnp.int32, (CH, 128), 1)
    gain = jnp.zeros((CH, 128), F32)
    for k in range(D // 128):
        gain = gain + jnp.where(flat == k * 128 + lane, gain_ref[k : k + 1, :], 0.0)
    gain = jnp.sum(gain, axis=1, keepdims=True)
    for cp in loads[6:]:
        cp.wait()
    eye_h = eye(HID)
    for k in range(4):
        block = slice(k * HID, (k + 1) * HID)
        wguT[k, 0:HID, :] = mm(eye_h, wg[block, :], 1, 1).astype(BF16)
        wguT[k, HID : 2 * HID, :] = mm(eye_h, wu[block, :], 1, 1).astype(BF16)
        wdT[k] = mm(eye_h, wd[block, :], 1, 1).astype(BF16)
    eye_c = eye(CH)
    eye_t = eye(TOK)

    all_to_all_wait(0, a1s, a1r)

    mixed = mm(kron[...], a1r[...].reshape(TOK, CH)) * tout
    a2s[...] = mixed.astype(BF16).reshape(NSEQ, POS, CH)
    all_to_all_send(1, a2s, a2r)
    all_to_all_wait(1, a2s, a2r)

    mixed = mm(eye_c, a2r[...].reshape(TOK, CH), 1, 1)
    res = (x_ref[...].astype(F32) + mixed).astype(BF16).astype(F32)
    res_s[...] = res

    def share_row(n, buf, row):
        buf[tn] = jnp.broadcast_to(row, (8, TOK))

        def one(i, carry):
            peer = lax.rem(tn + i, NTEN)
            pltpu.make_async_remote_copy(
                src_ref=buf.at[tn], dst_ref=buf.at[tn],
                send_sem=v_ss.at[n, peer], recv_sem=v_rs.at[n, tn],
                device_id=ten_dev(peer), device_id_type=MESH,
            ).start()
            return carry

        lax.fori_loop(1, NTEN, one, 0)
        pending.append(functools.partial(rows_done, n, buf))

    def sum_rows(n, buf):
        def one(i, carry):
            peer = lax.rem(tn + i, NTEN)
            wait_recv(buf.at[peer], v_ss.at[n, peer], v_rs.at[n, peer])
            return carry

        lax.fori_loop(1, NTEN, one, 0)
        return jnp.sum(buf[:, 0:1, :], axis=0)

    def rows_done(n, buf):
        def one(i, carry):
            peer = lax.rem(tn + i, NTEN)
            pltpu.make_async_remote_copy(
                src_ref=buf.at[tn], dst_ref=buf.at[tn],
                send_sem=v_ss.at[n, peer], recv_sem=v_rs.at[n, peer],
                device_id=ten_dev(peer), device_id_type=MESH,
            ).wait_send()
            return carry

        lax.fori_loop(1, NTEN, one, 0)

    chips = [lax.rem(x + d, 4) for d in range(4)]
    other = 1 - c
    HALF = CH // 2

    def gather_start(n, buf):
        for h in range(2):
            part = buf.at[tn, pl.ds(h * HALF, HALF)]
            for d in (2, 1, 3):
                send(part, part, ag_ss.at[n, d, h], ag_rs.at[n, d, h], ten_dev(chips[d] * 2 + c))
            send(part, part, sib_ss.at[n, 0, h], sib_rs.at[n, 0, h], ten_dev(x * 2 + other))

    def gather_forward(n, buf, then=None):
        for d in (1, 3, 2):
            src = lax.rem(x + 4 - d, 4) * 2 + c
            for h in range(2):
                part = buf.at[src, pl.ds(h * HALF, HALF)]
                wait_recv(part, ag_ss.at[n, d, h], ag_rs.at[n, d, h])
                send(part, part, sib_ss.at[n, d, h], sib_rs.at[n, d, h], ten_dev(x * 2 + other))
            if then is not None:
                then(src // 2, c)

    def gather_chip(n, buf, d):
        chip = lax.rem(x + 4 - d, 4)
        for h in range(2):
            part = buf.at[chip * 2 + other, pl.ds(h * HALF, HALF)]
            wait_recv(part, sib_ss.at[n, d, h], sib_rs.at[n, d, h])
        return chip, buf[pl.ds(chip * 2, 2)].reshape(2 * CH, TOK)

    def gather_matmul(n, buf, weights, offsets, acc=None):
        for d in offsets:
            chip, block = gather_chip(n, buf, d)
            term = mm(weights[chip], block)
            acc = term if acc is None else acc + term
        return acc

    def scatter_start(n, part_of, p, sb, q, t, then=None):
        for d in (2, 1, 3, 0):
            p[d] = part_of(chips[d] * 2 + other).astype(BF16)
            send(p.at[d], sb.at[d], rsib_ss.at[n, d], rsib_rs.at[n, d], ten_dev(x * 2 + other))
        for d in (2, 1, 3, 0):
            own[d] = part_of(chips[d] * 2 + c)
        if then is not None:
            then()
        for d in (2, 1, 3):
            wait_recv(sb.at[d], rsib_ss.at[n, d], rsib_rs.at[n, d])
            q[d] = (own[d] + sb[d].astype(F32)).astype(BF16)
            send(q.at[d], t.at[d], rs_ss.at[n, d], rs_rs.at[n, d], ten_dev(chips[d] * 2 + c))

    def scatter_end(n, sb, t):
        wait_recv(sb.at[0], rsib_ss.at[n, 0], rsib_rs.at[n, 0])
        total = own[0] + sb[0].astype(F32)
        for d in (1, 3, 2):
            wait_recv(t.at[d], rs_ss.at[n, d], rs_rs.at[n, d])
            total = total + t[d].astype(F32)
        return total

    r1[tn] = (res * gain).astype(BF16)
    gather_start(0, r1)
    share_row(0, v1, jnp.sum(res * res, axis=0, keepdims=True))
    pre = gather_matmul(0, r1, wguT, (0,))
    gather_forward(0, r1)
    pre = gather_matmul(0, r1, wguT, (1, 3, 2), pre)
    inv = lax.rsqrt(sum_rows(0, v1) / D + EPS)
    gate_pre = pre[0:HID] * inv
    up_pre = pre[HID : 2 * HID] * inv
    sig = jax.nn.sigmoid(gate_pre)
    hidden = (gate_pre * sig * up_pre).astype(BF16)
    hid_s[...] = hidden
    gate_s[...] = gate_pre
    up_s[...] = up_pre

    def grad_rank(chip, yhi):
        g = mm(r2[chip * 2 + yhi], hid_s[...], 1, 1)
        first, second, third = (g[:, n * LANES : (n + 1) * LANES] for n in range(3))
        for m in range(4):
            ya[chip, yhi * 4 + m, 0:48, :] = first[m * 48 : m * 48 + 48].astype(BF16)
            ya[chip, yhi * 4 + m, 48:96, :] = third[m * 48 : m * 48 + 48].astype(BF16)
        for half in range(2):
            for at, part in ((0, second), (96, third)):
                pieces = [part[m * 48 + half * ROWS : m * 48 + half * ROWS + ROWS] for m in range(4)]
                zb[half * 4 + chip, yhi, at : at + 96, :] = jnp.concatenate(pieces, axis=0).astype(BF16)

        def send_all(y_rows, z_rows):
            for m in range(4):
                peer = yhi * 4 + m

                @pl.when(peer != y)
                def _():
                    pltpu.make_async_remote_copy(
                        src_ref=ya.at[chip, peer, pl.ds(0, y_rows)],
                        dst_ref=yr.at[chip, y, pl.ds(0, y_rows)],
                        send_sem=gy_ss.at[chip, peer], recv_sem=gy_rs.at[chip, y],
                        device_id=y_dev(peer), device_id_type=MESH,
                    ).start()

            for half in range(2):
                zpeer = half * 4 + chip

                @pl.when(zpeer != z)
                def _():
                    pltpu.make_async_remote_copy(
                        src_ref=zb.at[zpeer, yhi, pl.ds(0, z_rows)],
                        dst_ref=zr.at[z, yhi, pl.ds(0, z_rows)],
                        send_sem=gz_ss.at[zpeer, yhi], recv_sem=gz_rs.at[z, yhi],
                        device_id=z_dev(zpeer), device_id_type=MESH,
                    ).start()

        @pl.when(chip < 2)
        def _():
            send_all(96, 96)

        @pl.when(chip >= 2)
        def _():
            send_all(48, 2 * 96)

    def grad_first_done():
        def one(i, carry):
            peer = lax.rem(y + i, 8)
            for zl in range(4):
                buf = ya.at[zl, peer, pl.ds(0, 96 if zl < 2 else 48)]
                pltpu.make_async_remote_copy(
                    src_ref=buf, dst_ref=buf, send_sem=gy_ss.at[zl, peer], recv_sem=gy_rs.at[zl, peer],
                    device_id=y_dev(peer), device_id_type=MESH,
                ).wait_send()
            return carry

        lax.fori_loop(1, 8, one, 0)
        for zz in range(8):

            @pl.when(z != zz)
            def _():
                for yhi in range(2):
                    buf = zb.at[zz, yhi, pl.ds(0, 96 if zz % 4 < 2 else 2 * 96)]
                    pltpu.make_async_remote_copy(
                        src_ref=buf, dst_ref=buf, send_sem=gz_ss.at[zz, yhi],
                        recv_sem=gz_rs.at[zz, yhi], device_id=z_dev(zz), device_id_type=MESH,
                    ).wait_send()

    def grad_second():
        for zl in range(4):
            rows = 96 if zl < 2 else 48

            def add(i, acc):
                peer = lax.rem(y + i, 8)
                buf = yr.at[zl, peer, pl.ds(0, rows)]
                wait_recv(buf, gy_ss.at[zl, peer], gy_rs.at[zl, peer])
                return acc + buf[...].astype(F32)

            total = lax.fori_loop(1, 8, add, ya[zl, y, 0:rows, :].astype(F32))
            for half in range(2):
                pieces = [total[half * ROWS : half * ROWS + ROWS]]
                if zl < 2:
                    pieces.append(total[48 + half * ROWS : 48 + half * ROWS + ROWS])
                else:
                    pieces.append(jnp.zeros((ROWS, LANES), F32))
                y2s[half * 4 + zl] = jnp.concatenate(pieces, axis=0).astype(BF16)
        second_send(0, y2s, y2r, z, z_dev)

        def sum_z(rows):
            for yhi in range(2):

                def add(i, acc):
                    peer = lax.rem(z + i, 8)
                    buf = zr.at[peer, yhi, pl.ds(0, rows)]
                    wait_recv(buf, gz_ss.at[peer, yhi], gz_rs.at[peer, yhi])
                    return acc + buf[...].astype(F32)

                total = lax.fori_loop(1, 8, add, zb[z, yhi, 0:rows, :].astype(F32))
                for m in range(4):
                    pieces = [total[m * ROWS : m * ROWS + ROWS]]
                    if rows > 96:
                        pieces.append(total[96 + m * ROWS : 96 + m * ROWS + ROWS])
                    else:
                        pieces.append(jnp.zeros((ROWS, LANES), F32))
                    z2s[yhi * 4 + m] = jnp.concatenate(pieces, axis=0).astype(BF16)

        @pl.when(dp < 2)
        def _():
            sum_z(96)

        @pl.when(dp >= 2)
        def _():
            sum_z(2 * 96)

        second_send(1, z2s, z2r, y, y_dev)

    def second_send(n, src, dst, me, dev):
        def one(i, carry):
            peer = lax.rem(me + i, 8)
            pltpu.make_async_remote_copy(
                src_ref=src.at[peer], dst_ref=dst.at[me],
                send_sem=g2_ss.at[n, peer], recv_sem=g2_rs.at[n, me],
                device_id=dev(peer), device_id_type=MESH,
            ).start()
            return carry

        lax.fori_loop(1, 8, one, 0)
        pending.append(functools.partial(second_done, n, src, me, dev))

    def second_done(n, src, me, dev):
        def one(i, carry):
            peer = lax.rem(me + i, 8)
            pltpu.make_async_remote_copy(
                src_ref=src.at[peer], dst_ref=src.at[peer],
                send_sem=g2_ss.at[n, peer], recv_sem=g2_rs.at[n, peer],
                device_id=dev(peer), device_id_type=MESH,
            ).wait_send()
            return carry

        lax.fori_loop(1, 8, one, 0)

    def second_sum(n, src, dst, me):
        def add(i, acc):
            peer = lax.rem(me + i, 8)
            wait_recv(dst.at[peer], g2_ss.at[n, peer], g2_rs.at[n, peer])
            return acc + dst[peer].astype(F32)

        return lax.fori_loop(1, 8, add, src[me].astype(F32))

    scatter_start(0, lambda r: mm(wd[pl.ds(pl.multiple_of(r * CH, CH), CH), :], hid_s[...]), p1, sb1, q1, t1)
    projected = scatter_end(0, sb1, t1)
    summed = res_s[...] + projected
    cot = (summed - tgt_ref[...].astype(F32)).astype(BF16)
    r2[tn] = cot
    gather_start(1, r2)
    out_ref[...] = summed.astype(BF16)
    store(0, out_ref, out_hbm)
    grad_rank(x, c)
    d_hidden = gather_matmul(1, r2, wdT, (0,))
    grad_rank(x, other)
    gather_forward(1, r2, grad_rank)
    d_hidden = gather_matmul(1, r2, wdT, (1, 3, 2), d_hidden)

    gate_pre = gate_s[...]
    up_pre = up_s[...]
    sig = jax.nn.sigmoid(gate_pre)
    d_gate = (d_hidden * up_pre * sig * (1.0 + gate_pre * (1.0 - sig))).astype(BF16)
    d_up = (d_hidden * gate_pre * sig).astype(BF16)
    inner = d_gate.astype(F32) * gate_pre + d_up.astype(F32) * up_pre
    share_row(1, v2, jnp.sum(inner, axis=0, keepdims=True))

    def back_part(r):
        block = pl.ds(pl.multiple_of(r * CH, CH), CH)
        return mm(wg[block, :], d_gate) + mm(wu[block, :], d_up)

    def grad_rest():
        for d in (1, 3, 2):
            grad_rank(chips[d], other)
        pending.append(grad_first_done)

    scatter_start(1, back_part, p2, sb2, q2, t2, grad_rest)

    d_normed = scatter_end(1, sb2, t2)
    corr = sum_rows(1, v2) / D
    res = res_s[...]
    d_res = (cot.astype(F32) + inv * (gain * d_normed - res * inv * corr)).astype(BF16)
    d_tok = mm(eye_t, d_res, 1, 1)
    a3s[...] = d_tok.astype(BF16).reshape(NSEQ, POS, CH)

    all_to_all_send(2, a3s, a3r)
    grad_second()
    all_to_all_wait(2, a3s, a3r)
    weighted = (a3r[...].reshape(TOK, CH).astype(F32) * tout).astype(BF16)
    a4s[...] = mm(kronT[...], weighted).astype(BF16).reshape(NSEQ, POS, CH)
    all_to_all_send(3, a4s, a4r)

    rows_y = second_sum(0, y2s, y2r, z)
    rows_z = second_sum(1, z2s, z2r, y)
    gd_ref[:, 0:LANES] = rows_y[0:ROWS]
    gd_ref[:, LANES : 2 * LANES] = rows_z[0:ROWS]
    gd_ref[:, 2 * LANES : HID] = rows_y[ROWS:48] + rows_z[ROWS:48]
    store(2, gd_ref, gd_hbm)

    drain()
    all_to_all_wait(3, a4s, a4r)
    scaled = (a4r[...].reshape(TOK, CH).astype(F32) * tin).astype(BF16)
    d_mix = mm(scaled, bm_ref[...], 0, 1)
    din_ref[...] = (d_res.astype(F32) + d_mix).astype(BF16)

    store(1, din_ref, din_hbm)

    drain()


def finish(out_in, din_in, gd_in, out_ref, din_ref, gd_ref):
    out_ref[...] = out_in[...]
    din_ref[...] = din_in[...]
    gd_ref[...] = gd_in[...]


def body(
    inputs, targets, block_mix, cross_mix, twiddle_in, twiddle_out, norm_gain, w_gate, w_up, w_down
):
    hbm = pl.BlockSpec(memory_space=pltpu.HBM)
    vmem = pl.BlockSpec(memory_space=pltpu.VMEM)
    dma = pltpu.SemaphoreType.DMA
    chunks = pltpu.VMEM((NSEQ, POS, CH), BF16)
    blocks4 = pltpu.VMEM((4, CH, TOK), BF16)
    results = (
        jax.ShapeDtypeStruct((CH, TOK), BF16),
        jax.ShapeDtypeStruct((CH, TOK), BF16),
        jax.ShapeDtypeStruct((ROWS, HID), F32),
    )
    made = pl.pallas_call(
        kernel,
        out_shape=results,
        in_specs=[hbm] * 10,
        out_specs=(hbm, hbm, hbm),
        scratch_shapes=[
            pltpu.VMEM((CH, TOK), BF16),
            pltpu.VMEM((CH, TOK), BF16),
            pltpu.VMEM((ROWS, HID), F32),
            pltpu.VMEM((CH, TOK), BF16),
            pltpu.VMEM((CH, TOK), BF16),
            pltpu.VMEM((TOK, TOK), BF16),
            pltpu.VMEM((NSEQ, NSEQ), BF16),
            pltpu.VMEM((1, TOK), F32),
            pltpu.VMEM((NSEQ, POS), F32),
            pltpu.VMEM((D // 128, 128), F32),
            pltpu.VMEM((D, HID), BF16),
            pltpu.VMEM((D, HID), BF16),
            pltpu.VMEM((D, HID), BF16),
            pltpu.VMEM((4, 2 * HID, HID), BF16),
            pltpu.VMEM((4, HID, HID), BF16),
            pltpu.VMEM((TOK, TOK), BF16),
            pltpu.VMEM((TOK, TOK), BF16),
        ]
        + [chunks] * 8
        + [
            pltpu.VMEM((NTEN, CH, TOK), BF16),
            pltpu.VMEM((NTEN, CH, TOK), BF16),
            pltpu.VMEM((NTEN, 8, TOK), F32),
            pltpu.VMEM((NTEN, 8, TOK), F32),
        ]
        + [blocks4] * 8
        + [
            pltpu.VMEM((4, CH, TOK), F32),
            pltpu.VMEM((HID, TOK), F32),
            pltpu.VMEM((HID, TOK), F32),
            pltpu.VMEM((HID, TOK), BF16),
            pltpu.VMEM((CH, TOK), F32),
            pltpu.VMEM((4, 8, 96, LANES), BF16),
            pltpu.VMEM((4, 8, 96, LANES), BF16),
            pltpu.VMEM((8, 2, 2 * 96, LANES), BF16),
            pltpu.VMEM((8, 2, 2 * 96, LANES), BF16),
            pltpu.VMEM((8, 48, LANES), BF16),
            pltpu.VMEM((8, 48, LANES), BF16),
            pltpu.VMEM((8, 48, LANES), BF16),
            pltpu.VMEM((8, 48, LANES), BF16),
            dma((3,)),
            dma((10,)),
            dma((4, NSEQ)),
            dma((4, NSEQ)),
            dma((2, 4, 2)),
            dma((2, 4, 2)),
            dma((2, 4, 2)),
            dma((2, 4, 2)),
            dma((2, NTEN)),
            dma((2, NTEN)),
            dma((2, 4)),
            dma((2, 4)),
            dma((2, 4)),
            dma((2, 4)),
            dma((4, 8)),
            dma((4, 8)),
            dma((8, 2)),
            dma((8, 2)),
            dma((2, 8)),
            dma((2, 8)),
        ],
        compiler_params=pltpu.CompilerParams(
            collective_id=0, has_side_effects=True, vmem_limit_bytes=64 * 1024 * 1024
        ),
        name="monarch_block",
    )(
        inputs[0].T,
        targets[0].T,
        block_mix,
        cross_mix,
        twiddle_in,
        twiddle_out,
        norm_gain.reshape(D // 128, 128),
        w_gate,
        w_up,
        w_down,
    )
    output, d_input, grad_down = pl.pallas_call(
        finish,
        out_shape=results,
        in_specs=[vmem] * 3,
        out_specs=(vmem, vmem, vmem),
        compiler_params=pltpu.CompilerParams(vmem_limit_bytes=64 * 1024 * 1024),
        name="hand_over",
    )(*made)
    return output.T[None], d_input.T[None], grad_down


def solution(mesh):
    return jax.shard_map(
        body,
        mesh=mesh,
        in_specs=(
            P("dp", "seq", "tensor"),
            P("dp", "seq", "tensor"),
            P(),
            P(),
            P("seq", None),
            P(None, "seq"),
            P(),
            P(None, "tensor"),
            P(None, "tensor"),
            P(None, "tensor"),
        ),
        out_specs=(P("dp", "seq", "tensor"), P("dp", "seq", "tensor"), P(("dp", "seq"), "tensor")),
        check_vma=False,
    )
```

```python
import functools

import jax
import jax.numpy as jnp
from jax import lax
from jax.experimental import pallas as pl
from jax.experimental.pallas import tpu as pltpu
from jax.sharding import PartitionSpec as P

F32 = jnp.float32
BF16 = jnp.bfloat16
MESH = pl.DeviceIdType.MESH

TOK = 256
HT = TOK // 2
CH = 192
HID = 384
NSEQ = 16
NTEN = 8
POS = 16
D = 1536
LANES = 128
ROWS = 24
EPS = 1e-05


def mm(a, b, ca=1, cb=0):
    return lax.dot_general(a, b, (((ca,), (cb,)), ((), ())), preferred_element_type=F32)


def eye(n, dtype=BF16):
    rows = lax.broadcasted_iota(jnp.int32, (n, n), 0)
    cols = lax.broadcasted_iota(jnp.int32, (n, n), 1)
    return jnp.where(rows == cols, 1.0, 0.0).astype(dtype)


def column_of(row):
    n = row.shape[1]
    return jnp.sum(eye(n, F32) * row, axis=1, keepdims=True)


def kernel(
    x_hbm, tgt_hbm, bm_hbm, cm_hbm, ti_hbm, to_hbm, gain_hbm, wg_hbm, wu_hbm, wd_hbm,
    out_hbm, din_hbm, gd_hbm,
    out_ref, din_ref, gd_ref, x_ref, tgt_ref, bm_ref, cm_ref, ti_ref, to_ref, gain_ref,
    wg, wu, wd, wguT, wdT, kron, kronT,
    a1s, a1r, a2s, a2r, a3s, a3r, a4s, a4r,
    r1, r2, v1, v2,
    p1, p2, sb1, sb2, q1, q2, t1, t2, own, gate_s, up_s, hid_s, res_s, dres_s,
    ya, yr, zb, zr, y2s, y2r, z2s, z2r,
    osem, wsem, a_ss, a_rs, ag_ss, ag_rs, sib_ss, sib_rs, v_ss, v_rs,
    rsib_ss, rsib_rs, rs_ss, rs_rs, g_ss, g_rs, g2_ss, g2_rs,
):
    dp = lax.axis_index("dp")
    sq = lax.axis_index("seq")
    tn = lax.axis_index("tensor")
    x, c = tn // 2, tn % 2
    y, zh = sq // 2, sq % 2
    z = zh * 4 + dp

    def seq_dev(s):
        return (dp, s, tn)

    def ten_dev(t):
        return (dp, sq, t)

    def y_dev(yy):
        return (dp, yy * 2 + zh, tn)

    def z_dev(zz):
        return (lax.rem(zz, 4), y * 2 + zz // 4, tn)

    pending = []

    def drain():
        while pending:
            pending.pop(0)()


    def send(src, dst, ss, rs, dev):
        cp = pltpu.make_async_remote_copy(
            src_ref=src, dst_ref=dst, send_sem=ss, recv_sem=rs, device_id=dev, device_id_type=MESH
        )
        cp.start()
        pending.append(cp.wait_send)

    def wait_recv(buf, ss, rs):
        pltpu.make_async_remote_copy(
            src_ref=buf, dst_ref=buf, send_sem=ss, recv_sem=rs,
            device_id=(dp, sq, tn), device_id_type=MESH,
        ).wait_recv()

    loads = []
    for n, (src, dst) in enumerate(
        (
            (x_hbm, x_ref), (bm_hbm, bm_ref), (ti_hbm, ti_ref), (cm_hbm, cm_ref), (to_hbm, to_ref),
            (gain_hbm, gain_ref), (wg_hbm, wg), (wu_hbm, wu), (wd_hbm, wd), (tgt_hbm, tgt_ref),
        )
    ):
        cp = pltpu.make_async_copy(src, dst, wsem.at[n])
        loads.append(cp)
    for cp in loads[0:3]:
        cp.start()

    barrier = pltpu.get_barrier_semaphore()

    def greet(dev):
        pl.semaphore_signal(barrier, inc=1, device_id=dev, device_id_type=MESH)

    def greet_seq(i, carry):
        greet(seq_dev(lax.rem(sq + i, NSEQ)))
        return carry

    def greet_ten(i, carry):
        greet(ten_dev(lax.rem(tn + i, NTEN)))
        return carry

    lax.fori_loop(1, NSEQ, greet_seq, 0)
    lax.fori_loop(1, NTEN, greet_ten, 0)
    for i in (1, 2, 3, 5, 6, 7):
        greet(z_dev(lax.rem(z + i, 8)))

    for cp in loads[3:]:
        cp.start()

    def store(n, src, dst):
        cp = pltpu.make_async_copy(src, dst, osem.at[n])
        cp.start()
        pending.append(cp.wait)

    def all_to_all_send(n, src, dst, halves=(0, 1)):
        for h in halves:

            def one(i, carry):
                peer = h * 8 + lax.rem(sq + i, 8)

                @pl.when(peer != sq)
                def _():
                    pltpu.make_async_remote_copy(
                        src_ref=src.at[peer], dst_ref=dst.at[sq],
                        send_sem=a_ss.at[n, peer], recv_sem=a_rs.at[n, sq],
                        device_id=seq_dev(peer), device_id_type=MESH,
                    ).start()

                return carry

            lax.fori_loop(0, 8, one, 0)
        if 1 in halves:
            dst[sq] = src[sq]
            pending.append(functools.partial(all_to_all_done, n, src))

    def all_to_all_wait(n, src, dst, halves=(0, 1)):
        for h in halves:

            def one(i, carry):
                peer = h * 8 + lax.rem(sq + i, 8)

                @pl.when(peer != sq)
                def _():
                    wait_recv(dst.at[peer], a_ss.at[n, peer], a_rs.at[n, peer])

                return carry

            lax.fori_loop(0, 8, one, 0)

    def all_to_all_done(n, src):
        def one(i, carry):
            peer = lax.rem(sq + i, NSEQ)
            pltpu.make_async_remote_copy(
                src_ref=src.at[peer], dst_ref=src.at[peer],
                send_sem=a_ss.at[n, peer], recv_sem=a_rs.at[n, peer],
                device_id=seq_dev(peer), device_id_type=MESH,
            ).wait_send()
            return carry

        lax.fori_loop(1, NSEQ, one, 0)

    for cp in loads[0:3]:
        cp.wait()
    tin = column_of(ti_ref[...])
    section = mm(bm_ref[...], x_ref[...], 0, 1) * tin
    a1s[...] = section.astype(BF16).reshape(NSEQ, POS, CH)

    pl.semaphore_wait(barrier, (NSEQ - 1) + (NTEN - 1) + 6)
    all_to_all_send(0, a1s, a1r)

    rows = lax.broadcasted_iota(jnp.int32, (TOK, NSEQ), 0)
    cols = lax.broadcasted_iota(jnp.int32, (TOK, NSEQ), 1)
    pick_block = jnp.where(rows // POS == cols, 1.0, 0.0)
    pick_pos = jnp.where(rows % POS == cols, 1.0, 0.0)
    for cp in loads[3:6]:
        cp.wait()
    cross = cm_ref[...]
    wide = mm(pick_block.astype(BF16), cross, 1, 1).astype(BF16)
    wide = mm(wide, pick_block.astype(BF16), 1, 1)
    wideT = mm(pick_block.astype(BF16), cross, 1, 0).astype(BF16)
    wideT = mm(wideT, pick_block.astype(BF16), 1, 1)
    big_r = lax.broadcasted_iota(jnp.int32, (TOK, TOK), 0)
    big_c = lax.broadcasted_iota(jnp.int32, (TOK, TOK), 1)
    same_pos = (big_r % POS) == (big_c % POS)
    kron[...] = jnp.where(same_pos, wide, 0.0).astype(BF16)
    kronT[...] = jnp.where(same_pos, wideT, 0.0).astype(BF16)
    tout_all = jnp.broadcast_to(to_ref[...][:, None, :], (NSEQ, POS, POS)).reshape(TOK, POS)
    tout = jnp.sum(tout_all * pick_pos, axis=1, keepdims=True)
    flat = tn * CH + lax.broadcasted_iota(jnp.int32, (CH, 128), 0)
    lane = lax.broadcasted_iota(jnp.int32, (CH, 128), 1)
    gain = jnp.zeros((CH, 128), F32)
    for k in range(D // 128):
        gain = gain + jnp.where(flat == k * 128 + lane, gain_ref[k : k + 1, :], 0.0)
    gain = jnp.sum(gain, axis=1, keepdims=True)
    for cp in loads[6:]:
        cp.wait()
    eye_h = eye(HID)
    for k in range(4):
        block = slice(k * HID, (k + 1) * HID)
        wguT[k, 0:HID, :] = mm(eye_h, wg[block, :], 1, 1).astype(BF16)
        wguT[k, HID : 2 * HID, :] = mm(eye_h, wu[block, :], 1, 1).astype(BF16)
        wdT[k] = mm(eye_h, wd[block, :], 1, 1).astype(BF16)
    eye_c = eye(CH)

    all_to_all_wait(0, a1s, a1r)

    mixed = mm(kron[...], a1r[...].reshape(TOK, CH)) * tout
    a2s[...] = mixed.astype(BF16).reshape(NSEQ, POS, CH)
    all_to_all_send(1, a2s, a2r)
    halves = [slice(0, HT), slice(HT, TOK)]

    def residual(h):
        all_to_all_wait(1, a2s, a2r, (h,))
        mixed = mm(eye_c, a2r[h * 8 : h * 8 + 8].reshape(HT, CH), 1, 1)
        res = (x_ref[:, halves[h]].astype(F32) + mixed).astype(BF16).astype(F32)
        res_s[h] = res
        r1[h, tn] = (res * gain).astype(BF16)
        gather_start(0, h, r1)
        share_row(0, h, v1, jnp.sum(res * res, axis=0, keepdims=True))

    def share_row(n, h, buf, row):
        buf[h, tn] = jnp.broadcast_to(row, (8, HT))

        def one(i, carry):
            peer = lax.rem(tn + i, NTEN)
            pltpu.make_async_remote_copy(
                src_ref=buf.at[h, tn], dst_ref=buf.at[h, tn],
                send_sem=v_ss.at[n, h, peer], recv_sem=v_rs.at[n, h, tn],
                device_id=ten_dev(peer), device_id_type=MESH,
            ).start()
            return carry

        lax.fori_loop(1, NTEN, one, 0)
        pending.append(functools.partial(rows_done, n, h, buf))

    def sum_rows(n, h, buf):
        def one(i, carry):
            peer = lax.rem(tn + i, NTEN)
            wait_recv(buf.at[h, peer], v_ss.at[n, h, peer], v_rs.at[n, h, peer])
            return carry

        lax.fori_loop(1, NTEN, one, 0)
        return jnp.sum(buf[h, :, 0:1, :], axis=0)

    def rows_done(n, h, buf):
        def one(i, carry):
            peer = lax.rem(tn + i, NTEN)
            pltpu.make_async_remote_copy(
                src_ref=buf.at[h, tn], dst_ref=buf.at[h, tn],
                send_sem=v_ss.at[n, h, peer], recv_sem=v_rs.at[n, h, peer],
                device_id=ten_dev(peer), device_id_type=MESH,
            ).wait_send()
            return carry

        lax.fori_loop(1, NTEN, one, 0)

    chips = [lax.rem(x + d, 4) for d in range(4)]
    other = 1 - c

    def gather_start(n, h, buf):
        part = buf.at[h, tn]
        for d in (2, 1, 3):
            send(part, part, ag_ss.at[n, d, h], ag_rs.at[n, d, h], ten_dev(chips[d] * 2 + c))
        send(part, part, sib_ss.at[n, 0, h], sib_rs.at[n, 0, h], ten_dev(x * 2 + other))

    def gather_forward(n, h, buf, then=None):
        for d in (1, 3, 2):
            src = lax.rem(x + 4 - d, 4) * 2 + c
            part = buf.at[h, src]
            wait_recv(part, ag_ss.at[n, d, h], ag_rs.at[n, d, h])
            send(part, part, sib_ss.at[n, d, h], sib_rs.at[n, d, h], ten_dev(x * 2 + other))
            if then is not None:
                then(src // 2, c)

    def gather_matmul(n, h, buf, weights):
        acc = None
        for d in (0, 1, 3, 2):
            chip = lax.rem(x + 4 - d, 4)
            wait_recv(buf.at[h, chip * 2 + other], sib_ss.at[n, d, h], sib_rs.at[n, d, h])
            term = mm(weights[chip], buf[h, pl.ds(chip * 2, 2)].reshape(2 * CH, HT))
            acc = term if acc is None else acc + term
        return acc

    def scatter_start(n, h, part_of, p, sb):
        for d in (2, 1, 3, 0):
            p[h, d] = part_of(chips[d] * 2 + other).astype(BF16)
            send(p.at[h, d], sb.at[h, d], rsib_ss.at[n, h, d], rsib_rs.at[n, h, d], ten_dev(x * 2 + other))
        for d in (2, 1, 3, 0):
            own[h, d] = part_of(chips[d] * 2 + c)

    def scatter_mid(n, h, sb, q, t):
        for d in (2, 1, 3):
            wait_recv(sb.at[h, d], rsib_ss.at[n, h, d], rsib_rs.at[n, h, d])
            q[h, d] = (own[h, d] + sb[h, d].astype(F32)).astype(BF16)
            send(q.at[h, d], t.at[h, d], rs_ss.at[n, h, d], rs_rs.at[n, h, d], ten_dev(chips[d] * 2 + c))

    def scatter_end(n, h, sb, t):
        wait_recv(sb.at[h, 0], rsib_ss.at[n, h, 0], rsib_rs.at[n, h, 0])
        total = own[h, 0] + sb[h, 0].astype(F32)
        for d in (1, 3, 2):
            wait_recv(t.at[h, d], rs_ss.at[n, h, d], rs_rs.at[n, h, d])
            total = total + t[h, d].astype(F32)
        return total

    def rows_of(ref, r):
        return ref[pl.ds(pl.multiple_of(r * CH, CH), CH), :]

    inv = [None, None]

    def forward(h):
        pre = gather_matmul(0, h, r1, wguT)
        inv[h] = lax.rsqrt(sum_rows(0, h, v1) / D + EPS)
        gate_pre = pre[0:HID] * inv[h]
        up_pre = pre[HID : 2 * HID] * inv[h]
        sig = jax.nn.sigmoid(gate_pre)
        hid_s[h] = (gate_pre * sig * up_pre).astype(BF16)
        gate_s[h] = gate_pre
        up_s[h] = up_pre
        scatter_start(0, h, lambda r: mm(rows_of(wd, r), hid_s[h]), p1, sb1)

    def cotangent(h):
        summed = res_s[h] + scatter_end(0, h, sb1, t1)
        r2[h, tn] = (summed - tgt_ref[:, halves[h]].astype(F32)).astype(BF16)
        gather_start(1, h, r2)
        out_ref[:, halves[h]] = summed.astype(BF16)

    def backward(h):
        d_hidden = gather_matmul(1, h, r2, wdT)
        gate_pre = gate_s[h]
        up_pre = up_s[h]
        sig = jax.nn.sigmoid(gate_pre)
        d_gate = (d_hidden * up_pre * sig * (1.0 + gate_pre * (1.0 - sig))).astype(BF16)
        d_up = (d_hidden * gate_pre * sig).astype(BF16)
        inner = d_gate.astype(F32) * gate_pre + d_up.astype(F32) * up_pre
        share_row(1, h, v2, jnp.sum(inner, axis=0, keepdims=True))
        scatter_start(1, h, lambda r: mm(rows_of(wg, r), d_gate) + mm(rows_of(wu, r), d_up), p2, sb2)

    def d_residual(h):
        d_normed = scatter_end(1, h, sb2, t2)
        corr = sum_rows(1, h, v2) / D
        d_res = r2[h, tn].astype(F32) + inv[h] * (gain * d_normed - res_s[h] * inv[h] * corr)
        dres_s[:, halves[h]] = d_res.astype(BF16)
        d_tok = mm(eye_h[0:HT, 0:HT], d_res.astype(BF16), 1, 1)
        a3s[h * 8 : h * 8 + 8] = d_tok.astype(BF16).reshape(8, POS, CH)
        all_to_all_send(2, a3s, a3r, (h,))

    sign = 1 - 2 * c

    def grad_rank(chip, yhi):
        cots = jnp.concatenate([r2[h, chip * 2 + yhi] for h in range(2)], axis=1)
        hids = jnp.concatenate([hid_s[h] for h in range(2)], axis=1)
        g = mm(cots, hids, 1, 1)
        first, second, third = (g[:, n * LANES : (n + 1) * LANES] for n in range(3))
        at = pl.multiple_of(chip * 48, 16)
        for m in range(4):
            ya[yhi * 4 + m, pl.ds(at, 48), :] = first[m * 48 : m * 48 + 48].astype(BF16)
        zat = pl.multiple_of(yhi * 96, 16)
        for half in range(2):
            pieces = [second[m * 48 + half * ROWS : m * 48 + half * ROWS + ROWS] for m in range(4)]
            zb[half * 4 + chip, pl.ds(zat, 96), :] = jnp.concatenate(pieces, axis=0).astype(BF16)

        @pl.when(chip < 2)
        def _():
            for m in range(4):
                ya[yhi * 4 + m, pl.ds(CH + at, 48), :] = third[m * 48 : m * 48 + 48].astype(BF16)

        @pl.when(chip >= 2)
        def _():
            for half in range(2):
                pieces = [third[m * 48 + half * ROWS : m * 48 + half * ROWS + ROWS] for m in range(4)]
                zb[half * 4 + chip, pl.ds(CH + zat, 96), :] = jnp.concatenate(pieces, axis=0).astype(BF16)

    def away(me, k):
        return lax.rem(me + sign * k + 8, 8)

    def sized(axis, target, work):
        if axis == 0:
            work(CH + 96)
            return

        @pl.when(lax.rem(target, 4) < 2)
        def _():
            work(CH)

        @pl.when(lax.rem(target, 4) >= 2)
        def _():
            work(2 * CH)

    AXES = ((ya, yr, y, y_dev), (zb, zr, z, z_dev))

    def grad_copy(axis, slot, to, target, rows):
        src, dst, me, dev = AXES[axis]
        return pltpu.make_async_remote_copy(
            src_ref=src.at[target, pl.ds(0, rows)], dst_ref=dst.at[slot, pl.ds(0, rows)],
            send_sem=g_ss.at[axis, slot], recv_sem=g_rs.at[axis, slot],
            device_id=dev(away(me, to)), device_id_type=MESH,
        )

    STEP1 = ((0, 2, 4), (1, 1, 3), (2, -1, -3), (3, 1, 1), (4, -1, -1))
    STEP2 = ((5, 2, 2), (6, -2, -2))

    def grad_step(axis, sends):
        me = AXES[axis][2]
        for slot, to, place in sends:
            target = away(me, place)
            sized(axis, target, lambda rows: grad_copy(axis, slot, to, target, rows).start())

            def done(slot=slot, to=to, target=target):
                sized(axis, target, lambda rows: grad_copy(axis, slot, to, target, rows).wait_send())

            pending.append(done)

    def grad_add(axis, target, slots):
        buf, got, me, dev = AXES[axis]

        def work(rows):
            total = buf[target, 0:rows, :].astype(F32)
            for slot in slots:
                part = got.at[slot, pl.ds(0, rows)]
                wait_recv(part, g_ss.at[axis, slot], g_rs.at[axis, slot])
                total = total + part[...].astype(F32)
            buf[target, 0:rows, :] = total.astype(BF16)

        sized(axis, target, work)

    def grad_first():
        for axis in range(2):
            grad_step(axis, STEP1)

    def grad_middle():
        for axis in range(2):
            me = AXES[axis][2]
            grad_add(axis, away(me, 2), (0, 1))
            grad_add(axis, away(me, -2), (2,))
            grad_step(axis, STEP2)

    def grad_second():
        total = ya[y].astype(F32)
        for slot in (3, 4, 6, 5):
            wait_recv(yr.at[slot], g_ss.at[0, slot], g_rs.at[0, slot])
            total = total + yr[slot].astype(F32)
        for zl in range(4):
            for half in range(2):
                at = zl * 48 + half * ROWS
                pieces = [total[at : at + ROWS]]
                if zl < 2:
                    pieces.append(total[CH + at : CH + at + ROWS])
                else:
                    pieces.append(jnp.zeros((ROWS, LANES), F32))
                y2s[half * 4 + zl] = jnp.concatenate(pieces, axis=0).astype(BF16)
        second_send(0, y2s, y2r, z, z_dev)

        def sum_z(rows):
            total = zb[z, 0:rows, :].astype(F32)
            for slot in (3, 4, 6, 5):
                part = zr.at[slot, pl.ds(0, rows)]
                wait_recv(part, g_ss.at[1, slot], g_rs.at[1, slot])
                total = total + part[...].astype(F32)
            for yy in range(8):
                pieces = [total[yy * ROWS : yy * ROWS + ROWS]]
                if rows > CH:
                    pieces.append(total[CH + yy * ROWS : CH + yy * ROWS + ROWS])
                else:
                    pieces.append(jnp.zeros((ROWS, LANES), F32))
                z2s[yy] = jnp.concatenate(pieces, axis=0).astype(BF16)

        sized(1, z, sum_z)
        second_send(1, z2s, z2r, y, y_dev)

    def second_send(n, src, dst, me, dev):
        def one(i, carry):
            peer = lax.rem(me + i, 8)
            pltpu.make_async_remote_copy(
                src_ref=src.at[peer], dst_ref=dst.at[me],
                send_sem=g2_ss.at[n, peer], recv_sem=g2_rs.at[n, me],
                device_id=dev(peer), device_id_type=MESH,
            ).start()
            return carry

        lax.fori_loop(1, 8, one, 0)
        pending.append(functools.partial(second_done, n, src, me, dev))

    def second_done(n, src, me, dev):
        def one(i, carry):
            peer = lax.rem(me + i, 8)
            pltpu.make_async_remote_copy(
                src_ref=src.at[peer], dst_ref=src.at[peer],
                send_sem=g2_ss.at[n, peer], recv_sem=g2_rs.at[n, peer],
                device_id=dev(peer), device_id_type=MESH,
            ).wait_send()
            return carry

        lax.fori_loop(1, 8, one, 0)

    def second_sum(n, src, dst, me):
        def add(i, acc):
            peer = lax.rem(me + i, 8)
            wait_recv(dst.at[peer], g2_ss.at[n, peer], g2_rs.at[n, peer])
            return acc + dst[peer].astype(F32)

        return lax.fori_loop(1, 8, add, src[me].astype(F32))

    residual(0)
    residual(1)
    gather_forward(0, 0, r1)
    forward(0)
    gather_forward(0, 1, r1)
    scatter_mid(0, 0, sb1, q1, t1)
    forward(1)
    scatter_mid(0, 1, sb1, q1, t1)
    cotangent(0)
    cotangent(1)
    store(0, out_ref, out_hbm)
    grad_rank(x, c)
    gather_forward(1, 0, r2)
    backward(0)
    gather_forward(1, 1, r2)
    scatter_mid(1, 0, sb2, q2, t2)
    backward(1)
    for d in (1, 3, 2):
        grad_rank(chips[d], c)
    scatter_mid(1, 1, sb2, q2, t2)
    for d in (0, 1, 3, 2):
        grad_rank(chips[d], other)
    grad_first()
    d_residual(0)
    d_residual(1)
    grad_middle()

    all_to_all_wait(2, a3s, a3r)
    weighted = (a3r[...].reshape(TOK, CH).astype(F32) * tout).astype(BF16)
    a4s[...] = mm(kronT[...], weighted).astype(BF16).reshape(NSEQ, POS, CH)
    all_to_all_send(3, a4s, a4r)
    grad_second()
    drain()

    rows_y = second_sum(0, y2s, y2r, z)
    rows_z = second_sum(1, z2s, z2r, y)
    gd_ref[:, 0:LANES] = rows_y[0:ROWS]
    gd_ref[:, LANES : 2 * LANES] = rows_z[0:ROWS]
    gd_ref[:, 2 * LANES : HID] = rows_y[ROWS:48] + rows_z[ROWS:48]
    store(2, gd_ref, gd_hbm)

    all_to_all_wait(3, a4s, a4r)
    scaled = (a4r[...].reshape(TOK, CH).astype(F32) * tin).astype(BF16)
    d_mix = mm(scaled, bm_ref[...], 0, 1)
    din_ref[...] = (dres_s[...].astype(F32) + d_mix).astype(BF16)

    store(1, din_ref, din_hbm)

    drain()


def finish(out_in, din_in, gd_in, out_ref, din_ref, gd_ref):
    out_ref[...] = out_in[...]
    din_ref[...] = din_in[...]
    gd_ref[...] = gd_in[...]


def body(
    inputs, targets, block_mix, cross_mix, twiddle_in, twiddle_out, norm_gain, w_gate, w_up, w_down
):
    hbm = pl.BlockSpec(memory_space=pltpu.HBM)
    vmem = pl.BlockSpec(memory_space=pltpu.VMEM)
    dma = pltpu.SemaphoreType.DMA
    chunks = pltpu.VMEM((NSEQ, POS, CH), BF16)
    blocks4 = pltpu.VMEM((2, 4, CH, HT), BF16)
    results = (
        jax.ShapeDtypeStruct((CH, TOK), BF16),
        jax.ShapeDtypeStruct((CH, TOK), BF16),
        jax.ShapeDtypeStruct((ROWS, HID), F32),
    )
    made = pl.pallas_call(
        kernel,
        out_shape=results,
        in_specs=[hbm] * 10,
        out_specs=(hbm, hbm, hbm),
        scratch_shapes=[
            pltpu.VMEM((CH, TOK), BF16),
            pltpu.VMEM((CH, TOK), BF16),
            pltpu.VMEM((ROWS, HID), F32),
            pltpu.VMEM((CH, TOK), BF16),
            pltpu.VMEM((CH, TOK), BF16),
            pltpu.VMEM((TOK, TOK), BF16),
            pltpu.VMEM((NSEQ, NSEQ), BF16),
            pltpu.VMEM((1, TOK), F32),
            pltpu.VMEM((NSEQ, POS), F32),
            pltpu.VMEM((D // 128, 128), F32),
            pltpu.VMEM((D, HID), BF16),
            pltpu.VMEM((D, HID), BF16),
            pltpu.VMEM((D, HID), BF16),
            pltpu.VMEM((4, 2 * HID, HID), BF16),
            pltpu.VMEM((4, HID, HID), BF16),
            pltpu.VMEM((TOK, TOK), BF16),
            pltpu.VMEM((TOK, TOK), BF16),
        ]
        + [chunks] * 8
        + [
            pltpu.VMEM((2, NTEN, CH, HT), BF16),
            pltpu.VMEM((2, NTEN, CH, HT), BF16),
            pltpu.VMEM((2, NTEN, 8, HT), F32),
            pltpu.VMEM((2, NTEN, 8, HT), F32),
        ]
        + [blocks4] * 8
        + [
            pltpu.VMEM((2, 4, CH, HT), F32),
            pltpu.VMEM((2, HID, HT), F32),
            pltpu.VMEM((2, HID, HT), F32),
            pltpu.VMEM((2, HID, HT), BF16),
            pltpu.VMEM((2, CH, HT), F32),
            pltpu.VMEM((CH, TOK), BF16),
            pltpu.VMEM((8, CH + 96, LANES), BF16),
            pltpu.VMEM((7, CH + 96, LANES), BF16),
            pltpu.VMEM((8, 2 * CH, LANES), BF16),
            pltpu.VMEM((7, 2 * CH, LANES), BF16),
            pltpu.VMEM((8, 48, LANES), BF16),
            pltpu.VMEM((8, 48, LANES), BF16),
            pltpu.VMEM((8, 48, LANES), BF16),
            pltpu.VMEM((8, 48, LANES), BF16),
            dma((3,)),
            dma((10,)),
            dma((4, NSEQ)),
            dma((4, NSEQ)),
            dma((2, 4, 2)),
            dma((2, 4, 2)),
            dma((2, 4, 2)),
            dma((2, 4, 2)),
            dma((2, 2, NTEN)),
            dma((2, 2, NTEN)),
            dma((2, 2, 4)),
            dma((2, 2, 4)),
            dma((2, 2, 4)),
            dma((2, 2, 4)),
            dma((2, 7)),
            dma((2, 7)),
            dma((2, 8)),
            dma((2, 8)),
        ],
        compiler_params=pltpu.CompilerParams(
            collective_id=0, has_side_effects=True, vmem_limit_bytes=64 * 1024 * 1024
        ),
        name="monarch_block",
    )(
        inputs[0].T,
        targets[0].T,
        block_mix,
        cross_mix,
        twiddle_in,
        twiddle_out,
        norm_gain.reshape(D // 128, 128),
        w_gate,
        w_up,
        w_down,
    )
    output, d_input, grad_down = pl.pallas_call(
        finish,
        out_shape=results,
        in_specs=[vmem] * 3,
        out_specs=(vmem, vmem, vmem),
        compiler_params=pltpu.CompilerParams(vmem_limit_bytes=64 * 1024 * 1024),
        name="hand_over",
    )(*made)
    return output.T[None], d_input.T[None], grad_down


def solution(mesh):
    return jax.shard_map(
        body,
        mesh=mesh,
        in_specs=(
            P("dp", "seq", "tensor"),
            P("dp", "seq", "tensor"),
            P(),
            P(),
            P("seq", None),
            P(None, "seq"),
            P(),
            P(None, "tensor"),
            P(None, "tensor"),
            P(None, "tensor"),
        ),
        out_specs=(P("dp", "seq", "tensor"), P("dp", "seq", "tensor"), P(("dp", "seq"), "tensor")),
        check_vma=False,
    )
```

```python
import functools

import jax
import jax.numpy as jnp
from jax import lax
from jax.experimental import pallas as pl
from jax.experimental.pallas import tpu as pltpu
from jax.sharding import PartitionSpec as P

F32 = jnp.float32
BF16 = jnp.bfloat16
MESH = pl.DeviceIdType.MESH

TOK = 256
HT = TOK // 2
CH = 192
HID = 384
NSEQ = 16
NTEN = 8
POS = 16
LINE = 32
FAR_FIRST = (4, 3, 5, 2, 6, 1, 7)
D = 1536
LANES = 128
ROWS = 24
EPS = 1e-05


def mm(a, b, ca=1, cb=0):
    return lax.dot_general(a, b, (((ca,), (cb,)), ((), ())), preferred_element_type=F32)


def eye(n, dtype=BF16):
    rows = lax.broadcasted_iota(jnp.int32, (n, n), 0)
    cols = lax.broadcasted_iota(jnp.int32, (n, n), 1)
    return jnp.where(rows == cols, 1.0, 0.0).astype(dtype)


def column_of(row):
    n = row.shape[1]
    return jnp.sum(eye(n, F32) * row, axis=1, keepdims=True)


def kernel(
    x_hbm, tgt_hbm, bm_hbm, cm_hbm, ti_hbm, to_hbm, gain_hbm, wg_hbm, wu_hbm, wd_hbm,
    out_hbm, din_hbm, gd_hbm,
    out_ref, din_ref, gd_ref, x_ref, tgt_ref, bm_ref, cm_ref, ti_ref, to_ref, gain_ref,
    wg, wu, wd, wguT, wdT, kron, kronT,
    a1s, a1r, a2s, a2r, a3s, a3r, a4s, a4r,
    r1, r2, v1, v2,
    p1, p2, sb1, sb2, q1, q2, t1, t2, own, gate_s, up_s, hid_s, res_s, dres_s,
    ya, yr, zb, zr, y2s, y2r, z2s, z2r,
    to_pair, cross_sem, tw_sem, osem, wsem, a_ss, a_rs, ag_ss, ag_rs, sib_ss, sib_rs, v_ss, v_rs,
    rsib_ss, rsib_rs, rs_ss, rs_rs, g_ss, g_rs, g2_ss, g2_rs,
):
    dp = lax.axis_index("dp")
    sq = lax.axis_index("seq")
    tn = lax.axis_index("tensor")
    x, c = tn // 2, tn % 2
    y, zh = sq // 2, sq % 2
    z = zh * 4 + dp

    def seq_dev(s):
        return (dp, s, tn)

    def ten_dev(t):
        return (dp, sq, t)

    def y_dev(yy):
        return (dp, yy * 2 + zh, tn)

    def z_dev(zz):
        return (lax.rem(zz, 4), y * 2 + zz // 4, tn)

    pending = []

    def drain():
        while pending:
            pending.pop(0)()


    def send(src, dst, ss, rs, dev):
        cp = pltpu.make_async_remote_copy(
            src_ref=src, dst_ref=dst, send_sem=ss, recv_sem=rs, device_id=dev, device_id_type=MESH
        )
        cp.start()
        pending.append(cp.wait_send)

    def wait_recv(buf, ss, rs):
        pltpu.make_async_remote_copy(
            src_ref=buf, dst_ref=buf, send_sem=ss, recv_sem=rs,
            device_id=(dp, sq, tn), device_id_type=MESH,
        ).wait_recv()

    loads = []
    for n, (src, dst) in enumerate(
        (
            (x_hbm, x_ref), (bm_hbm, bm_ref), (ti_hbm, ti_ref), (cm_hbm, cm_ref), (to_hbm, to_ref),
            (gain_hbm, gain_ref), (wg_hbm, wg), (wu_hbm, wu), (wd_hbm, wd), (tgt_hbm, tgt_ref),
        )
    ):
        cp = pltpu.make_async_copy(src, dst, wsem.at[n])
        loads.append(cp)
    for cp in loads[0:3]:
        cp.start()

    barrier = pltpu.get_barrier_semaphore()

    def greet(dev):
        pl.semaphore_signal(barrier, inc=1, device_id=dev, device_id_type=MESH)

    for i in FAR_FIRST:
        greet(y_dev(lax.rem(y + i, 8)))
        greet(z_dev(lax.rem(z + i, 8)))
    for i in (4, 5, 3, 6, 2, 7, 1):
        greet(ten_dev(lax.rem(tn + i, NTEN)))
    for cp in loads[3:]:
        cp.start()

    def store(n, src, dst):
        cp = pltpu.make_async_copy(src, dst, osem.at[n])
        cp.start()
        pending.append(cp.wait)

    def a2a_copy(n, src, dst, peer):
        return pltpu.make_async_remote_copy(
            src_ref=src.at[peer], dst_ref=dst.at[sq],
            send_sem=a_ss.at[n, peer], recv_sem=a_rs.at[n, sq],
            device_id=seq_dev(peer), device_id_type=MESH,
        )

    def all_to_all_send(n, src, dst):
        for i in FAR_FIRST + (0,):
            yy = lax.rem(y + i, 8)
            a2a_copy(n, src, dst, yy * 2 + 1 - zh).start()
            if i:
                a2a_copy(n, src, dst, yy * 2 + zh).start()
        dst[sq] = src[sq]
        pending.append(functools.partial(all_to_all_done, n, src, dst))

    def all_to_all_send_half(n, src, dst, h):
        for i in (2, 1, 3, 0):
            yy = h * 4 + lax.rem(y + i, 4)
            a2a_copy(n, src, dst, yy * 2 + 1 - zh).start()

            @pl.when(yy != y)
            def _():
                a2a_copy(n, src, dst, yy * 2 + zh).start()

        if h:
            dst[sq] = src[sq]
            pending.append(functools.partial(all_to_all_done, n, src, dst))

    def all_to_all_wait(n, src, dst, halves=(0, 1)):
        for h in halves:

            def one(i, carry):
                peer = h * 8 + lax.rem(sq + i, 8)

                @pl.when(peer != sq)
                def _():
                    wait_recv(dst.at[peer], a_ss.at[n, peer], a_rs.at[n, peer])

                return carry

            lax.fori_loop(0, 8, one, 0)

    def all_to_all_done(n, src, dst):
        def one(i, carry):
            a2a_copy(n, src, dst, lax.rem(sq + i, NSEQ)).wait_send()
            return carry

        lax.fori_loop(1, NSEQ, one, 0)

    def line_copy(peer):
        return pltpu.make_async_remote_copy(
            src_ref=a1s.at[peer], dst_ref=a1r.at[y],
            send_sem=a_ss.at[0, peer], recv_sem=a_rs.at[0, y],
            device_id=y_dev(peer), device_id_type=MESH,
        )

    def line_done():
        for i in FAR_FIRST:
            line_copy(lax.rem(y + i, 8)).wait_send()

    for cp in loads[0:3]:
        cp.wait()
    tin = column_of(ti_ref[...])
    section = mm(bm_ref[...], x_ref[...], 0, 1) * tin
    a1s[...] = section.astype(BF16).reshape(8, LINE, CH)

    pl.semaphore_wait(barrier, 7 + 7 + (NTEN - 1))
    partner = (dp, y * 2 + 1 - zh, tn)
    for i in FAR_FIRST:
        line_copy(lax.rem(y + i, 8)).start()
    pending.append(line_done)
    a1r[y] = a1s[y]
    pl.semaphore_signal(cross_sem, inc=1, device_id=partner, device_id_type=MESH)
    loads[4].wait()
    to_pair[zh] = to_ref[...]
    send(to_pair.at[zh], to_pair.at[zh], tw_sem.at[0], tw_sem.at[1], partner)

    rows = lax.broadcasted_iota(jnp.int32, (TOK, NSEQ), 0)
    cols = lax.broadcasted_iota(jnp.int32, (TOK, NSEQ), 1)
    loads[3].wait()
    loads[5].wait()
    cross = cm_ref[...]

    def iota(shape, dim):
        return lax.broadcasted_iota(jnp.int32, shape, dim)

    def flags(hit):
        return jnp.where(hit, 1.0, 0.0).astype(BF16)

    rows_here = flags(iota((8, NSEQ), 1) == 2 * iota((8, NSEQ), 0) + zh)
    cross_here = mm(rows_here, cross).astype(BF16)
    wide = mm(flags(iota((NSEQ * LINE, NSEQ), 0) // LINE == iota((NSEQ * LINE, NSEQ), 1)), cross_here, 1, 1)
    wide = mm(wide.astype(BF16), flags(iota((8, TOK), 1) // LINE == iota((8, TOK), 0)))
    same_pos = iota((NSEQ * LINE, TOK), 0) % LINE == iota((NSEQ * LINE, TOK), 1) % LINE
    kron[...] = jnp.where(same_pos, wide, 0.0).astype(BF16)
    pick_block = flags(rows // POS == cols)
    pick_pos = jnp.where(rows % POS == cols, 1.0, 0.0)
    wide = mm(mm(pick_block, cross).astype(BF16), pick_block, 1, 1)
    same_pos = iota((TOK, TOK), 0) % POS == iota((TOK, TOK), 1) % POS
    kronT[...] = jnp.where(same_pos, wide, 0.0).astype(BF16)
    tout_all = jnp.broadcast_to(to_ref[...][:, None, :], (NSEQ, POS, POS)).reshape(TOK, POS)
    tout = jnp.sum(tout_all * pick_pos, axis=1, keepdims=True)
    flat = tn * CH + lax.broadcasted_iota(jnp.int32, (CH, 128), 0)
    lane = lax.broadcasted_iota(jnp.int32, (CH, 128), 1)
    gain = jnp.zeros((CH, 128), F32)
    for k in range(D // 128):
        gain = gain + jnp.where(flat == k * 128 + lane, gain_ref[k : k + 1, :], 0.0)
    gain = jnp.sum(gain, axis=1, keepdims=True)
    for cp in loads[6:]:
        cp.wait()
    eye_h = eye(HID)
    for k in range(4):
        block = slice(k * HID, (k + 1) * HID)
        wguT[k, 0:HID, :] = mm(eye_h, wg[block, :], 1, 1).astype(BF16)
        wguT[k, HID : 2 * HID, :] = mm(eye_h, wu[block, :], 1, 1).astype(BF16)
        wdT[k] = mm(eye_h, wd[block, :], 1, 1).astype(BF16)
    eye_c = eye(CH)

    wait_recv(to_pair.at[1 - zh], tw_sem.at[0], tw_sem.at[1])
    tline = jnp.zeros((NSEQ * LINE, 1), F32)
    for half in range(2):
        spread = jnp.broadcast_to(to_pair[half][:, None, :], (NSEQ, LINE, POS)).reshape(NSEQ * LINE, POS)
        here = iota((NSEQ * LINE, POS), 0) % LINE == half * POS + iota((NSEQ * LINE, POS), 1)
        tline = tline + jnp.sum(jnp.where(here, spread, 0.0), axis=1, keepdims=True)
    pl.semaphore_wait(cross_sem, 1)
    for i in FAR_FIRST:
        peer = lax.rem(y + i, 8)
        wait_recv(a1r.at[peer], a_ss.at[0, peer], a_rs.at[0, peer])

    mixed = mm(kron[...], a1r[...].reshape(TOK, CH)) * tline
    a2s[...] = mixed.astype(BF16).reshape(NSEQ, LINE, CH)
    all_to_all_send(1, a2s, a2r)

    halves = [slice(0, HT), slice(HT, TOK)]

    def residual(h):
        all_to_all_wait(1, a2s, a2r, (h,))
        terms = a2r[h * 8 : h * 8 + 8].astype(F32).reshape(4, 2, LINE, CH)
        mixed = (terms[:, 0] + terms[:, 1]).astype(BF16).reshape(HT, CH)
        mixed = mm(eye_c, mixed, 1, 1)
        res = (x_ref[:, halves[h]].astype(F32) + mixed).astype(BF16).astype(F32)
        res_s[h] = res
        r1[h, tn] = (res * gain).astype(BF16)
        gather_start(0, h, r1)
        share_row(0, h, v1, jnp.sum(res * res, axis=0, keepdims=True))

    def share_row(n, h, buf, row):
        buf[h, tn] = jnp.broadcast_to(row, (8, HT))

        def one(i, carry):
            peer = lax.rem(tn + i, NTEN)
            pltpu.make_async_remote_copy(
                src_ref=buf.at[h, tn], dst_ref=buf.at[h, tn],
                send_sem=v_ss.at[n, h, peer], recv_sem=v_rs.at[n, h, tn],
                device_id=ten_dev(peer), device_id_type=MESH,
            ).start()
            return carry

        lax.fori_loop(1, NTEN, one, 0)
        pending.append(functools.partial(rows_done, n, h, buf))

    def sum_rows(n, h, buf):
        def one(i, carry):
            peer = lax.rem(tn + i, NTEN)
            wait_recv(buf.at[h, peer], v_ss.at[n, h, peer], v_rs.at[n, h, peer])
            return carry

        lax.fori_loop(1, NTEN, one, 0)
        return jnp.sum(buf[h, :, 0:1, :], axis=0)

    def rows_done(n, h, buf):
        def one(i, carry):
            peer = lax.rem(tn + i, NTEN)
            pltpu.make_async_remote_copy(
                src_ref=buf.at[h, tn], dst_ref=buf.at[h, tn],
                send_sem=v_ss.at[n, h, peer], recv_sem=v_rs.at[n, h, peer],
                device_id=ten_dev(peer), device_id_type=MESH,
            ).wait_send()
            return carry

        lax.fori_loop(1, NTEN, one, 0)

    chips = [lax.rem(x + d, 4) for d in range(4)]
    other = 1 - c

    def gather_start(n, h, buf):
        part = buf.at[h, tn]
        for d in (2, 1, 3):
            send(part, part, ag_ss.at[n, d, h], ag_rs.at[n, d, h], ten_dev(chips[d] * 2 + c))
        send(part, part, sib_ss.at[n, 0, h], sib_rs.at[n, 0, h], ten_dev(x * 2 + other))

    def gather_forward(n, h, buf, then=None):
        for d in (1, 3, 2):
            src = lax.rem(x + 4 - d, 4) * 2 + c
            part = buf.at[h, src]
            wait_recv(part, ag_ss.at[n, d, h], ag_rs.at[n, d, h])
            send(part, part, sib_ss.at[n, d, h], sib_rs.at[n, d, h], ten_dev(x * 2 + other))
            if then is not None:
                then(src // 2, c)

    def gather_matmul(n, h, buf, weights):
        acc = None
        for d in (0, 1, 3, 2):
            chip = lax.rem(x + 4 - d, 4)
            wait_recv(buf.at[h, chip * 2 + other], sib_ss.at[n, d, h], sib_rs.at[n, d, h])
            term = mm(weights[chip], buf[h, pl.ds(chip * 2, 2)].reshape(2 * CH, HT))
            acc = term if acc is None else acc + term
        return acc

    def scatter_start(n, h, part_of, p, sb):
        for d in (2, 1, 3, 0):
            p[h, d] = part_of(chips[d] * 2 + other).astype(BF16)
            send(p.at[h, d], sb.at[h, d], rsib_ss.at[n, h, d], rsib_rs.at[n, h, d], ten_dev(x * 2 + other))
        for d in (2, 1, 3, 0):
            own[h, d] = part_of(chips[d] * 2 + c)

    def scatter_mid(n, h, sb, q, t):
        for d in (2, 1, 3):
            wait_recv(sb.at[h, d], rsib_ss.at[n, h, d], rsib_rs.at[n, h, d])
            q[h, d] = (own[h, d] + sb[h, d].astype(F32)).astype(BF16)
            send(q.at[h, d], t.at[h, d], rs_ss.at[n, h, d], rs_rs.at[n, h, d], ten_dev(chips[d] * 2 + c))

    def scatter_end(n, h, sb, t):
        wait_recv(sb.at[h, 0], rsib_ss.at[n, h, 0], rsib_rs.at[n, h, 0])
        total = own[h, 0] + sb[h, 0].astype(F32)
        for d in (1, 3, 2):
            wait_recv(t.at[h, d], rs_ss.at[n, h, d], rs_rs.at[n, h, d])
            total = total + t[h, d].astype(F32)
        return total

    def rows_of(ref, r):
        return ref[pl.ds(pl.multiple_of(r * CH, CH), CH), :]

    inv = [None, None]

    def forward(h):
        pre = gather_matmul(0, h, r1, wguT)
        inv[h] = lax.rsqrt(sum_rows(0, h, v1) / D + EPS)
        gate_pre = pre[0:HID] * inv[h]
        up_pre = pre[HID : 2 * HID] * inv[h]
        sig = jax.nn.sigmoid(gate_pre)
        hid_s[h] = (gate_pre * sig * up_pre).astype(BF16)
        gate_s[h] = gate_pre
        up_s[h] = up_pre
        scatter_start(0, h, lambda r: mm(rows_of(wd, r), hid_s[h]), p1, sb1)

    def cotangent(h):
        summed = res_s[h] + scatter_end(0, h, sb1, t1)
        r2[h, tn] = (summed - tgt_ref[:, halves[h]].astype(F32)).astype(BF16)
        gather_start(1, h, r2)
        out_ref[:, halves[h]] = summed.astype(BF16)

    def backward(h):
        d_hidden = gather_matmul(1, h, r2, wdT)
        gate_pre = gate_s[h]
        up_pre = up_s[h]
        sig = jax.nn.sigmoid(gate_pre)
        d_gate = (d_hidden * up_pre * sig * (1.0 + gate_pre * (1.0 - sig))).astype(BF16)
        d_up = (d_hidden * gate_pre * sig).astype(BF16)
        inner = d_gate.astype(F32) * gate_pre + d_up.astype(F32) * up_pre
        share_row(1, h, v2, jnp.sum(inner, axis=0, keepdims=True))
        scatter_start(1, h, lambda r: mm(rows_of(wg, r), d_gate) + mm(rows_of(wu, r), d_up), p2, sb2)

    def d_residual(h):
        d_normed = scatter_end(1, h, sb2, t2)
        corr = sum_rows(1, h, v2) / D
        d_res = r2[h, tn].astype(F32) + inv[h] * (gain * d_normed - res_s[h] * inv[h] * corr)
        dres_s[:, halves[h]] = d_res.astype(BF16)
        d_tok = mm(eye_h[0:HT, 0:HT], d_res.astype(BF16), 1, 1)
        a3s[h * 8 : h * 8 + 8] = d_tok.astype(BF16).reshape(8, POS, CH)
        all_to_all_send_half(2, a3s, a3r, h)

    sign = 1 - 2 * c

    def grad_rank(chip, yhi):
        cots = jnp.concatenate([r2[h, chip * 2 + yhi] for h in range(2)], axis=1)
        hids = jnp.concatenate([hid_s[h] for h in range(2)], axis=1)
        g = mm(cots, hids, 1, 1)
        first, second, third = (g[:, n * LANES : (n + 1) * LANES] for n in range(3))
        at = pl.multiple_of(chip * 48, 16)
        for m in range(4):
            ya[yhi * 4 + m, pl.ds(at, 48), :] = first[m * 48 : m * 48 + 48].astype(BF16)
        zat = pl.multiple_of(yhi * 96, 16)
        for half in range(2):
            pieces = [second[m * 48 + half * ROWS : m * 48 + half * ROWS + ROWS] for m in range(4)]
            zb[half * 4 + chip, pl.ds(zat, 96), :] = jnp.concatenate(pieces, axis=0).astype(BF16)

        @pl.when(chip < 2)
        def _():
            for m in range(4):
                ya[yhi * 4 + m, pl.ds(CH + at, 48), :] = third[m * 48 : m * 48 + 48].astype(BF16)

        @pl.when(chip >= 2)
        def _():
            for half in range(2):
                pieces = [third[m * 48 + half * ROWS : m * 48 + half * ROWS + ROWS] for m in range(4)]
                zb[half * 4 + chip, pl.ds(CH + zat, 96), :] = jnp.concatenate(pieces, axis=0).astype(BF16)

    def away(me, k):
        return lax.rem(me + sign * k + 8, 8)

    def sized(axis, target, work):
        if axis == 0:
            work(CH + 96)
            return

        @pl.when(lax.rem(target, 4) < 2)
        def _():
            work(CH)

        @pl.when(lax.rem(target, 4) >= 2)
        def _():
            work(2 * CH)

    AXES = ((ya, yr, y, y_dev), (zb, zr, z, z_dev))

    def grad_copy(axis, slot, to, target, rows):
        src, dst, me, dev = AXES[axis]
        return pltpu.make_async_remote_copy(
            src_ref=src.at[target, pl.ds(0, rows)], dst_ref=dst.at[slot, pl.ds(0, rows)],
            send_sem=g_ss.at[axis, slot], recv_sem=g_rs.at[axis, slot],
            device_id=dev(away(me, to)), device_id_type=MESH,
        )

    STEP1 = ((0, 2, 4), (1, 1, 3), (2, -1, -3), (3, 1, 1), (4, -1, -1))
    STEP2 = ((5, 2, 2), (6, -2, -2))

    def grad_step(axis, sends):
        me = AXES[axis][2]
        for slot, to, place in sends:
            target = away(me, place)
            sized(axis, target, lambda rows: grad_copy(axis, slot, to, target, rows).start())

            def done(slot=slot, to=to, target=target):
                sized(axis, target, lambda rows: grad_copy(axis, slot, to, target, rows).wait_send())

            pending.append(done)

    def grad_add(axis, target, slots):
        buf, got, me, dev = AXES[axis]

        def work(rows):
            total = buf[target, 0:rows, :].astype(F32)
            for slot in slots:
                part = got.at[slot, pl.ds(0, rows)]
                wait_recv(part, g_ss.at[axis, slot], g_rs.at[axis, slot])
                total = total + part[...].astype(F32)
            buf[target, 0:rows, :] = total.astype(BF16)

        sized(axis, target, work)

    def grad_first():
        for axis in range(2):
            grad_step(axis, STEP1)

    def grad_middle():
        for axis in range(2):
            me = AXES[axis][2]
            grad_add(axis, away(me, 2), (0, 1))
            grad_add(axis, away(me, -2), (2,))
            grad_step(axis, STEP2)

    def grad_second():
        total = ya[y].astype(F32)
        for slot in (3, 4, 6, 5):
            wait_recv(yr.at[slot], g_ss.at[0, slot], g_rs.at[0, slot])
            total = total + yr[slot].astype(F32)
        for zl in range(4):
            for half in range(2):
                at = zl * 48 + half * ROWS
                pieces = [total[at : at + ROWS]]
                if zl < 2:
                    pieces.append(total[CH + at : CH + at + ROWS])
                else:
                    pieces.append(jnp.zeros((ROWS, LANES), F32))
                y2s[half * 4 + zl] = jnp.concatenate(pieces, axis=0).astype(BF16)
        second_send(0, y2s, y2r, z, z_dev)

        def sum_z(rows):
            total = zb[z, 0:rows, :].astype(F32)
            for slot in (3, 4, 6, 5):
                part = zr.at[slot, pl.ds(0, rows)]
                wait_recv(part, g_ss.at[1, slot], g_rs.at[1, slot])
                total = total + part[...].astype(F32)
            for yy in range(8):
                pieces = [total[yy * ROWS : yy * ROWS + ROWS]]
                if rows > CH:
                    pieces.append(total[CH + yy * ROWS : CH + yy * ROWS + ROWS])
                else:
                    pieces.append(jnp.zeros((ROWS, LANES), F32))
                z2s[yy] = jnp.concatenate(pieces, axis=0).astype(BF16)

        sized(1, z, sum_z)
        second_send(1, z2s, z2r, y, y_dev)

    def second_send(n, src, dst, me, dev):
        def one(i, carry):
            peer = lax.rem(me + i, 8)
            pltpu.make_async_remote_copy(
                src_ref=src.at[peer], dst_ref=dst.at[me],
                send_sem=g2_ss.at[n, peer], recv_sem=g2_rs.at[n, me],
                device_id=dev(peer), device_id_type=MESH,
            ).start()
            return carry

        lax.fori_loop(1, 8, one, 0)
        pending.append(functools.partial(second_done, n, src, me, dev))

    def second_done(n, src, me, dev):
        def one(i, carry):
            peer = lax.rem(me + i, 8)
            pltpu.make_async_remote_copy(
                src_ref=src.at[peer], dst_ref=src.at[peer],
                send_sem=g2_ss.at[n, peer], recv_sem=g2_rs.at[n, peer],
                device_id=dev(peer), device_id_type=MESH,
            ).wait_send()
            return carry

        lax.fori_loop(1, 8, one, 0)

    def second_sum(n, src, dst, me):
        def add(i, acc):
            peer = lax.rem(me + i, 8)
            wait_recv(dst.at[peer], g2_ss.at[n, peer], g2_rs.at[n, peer])
            return acc + dst[peer].astype(F32)

        return lax.fori_loop(1, 8, add, src[me].astype(F32))

    residual(0)
    residual(1)
    gather_forward(0, 0, r1)
    forward(0)
    gather_forward(0, 1, r1)
    scatter_mid(0, 0, sb1, q1, t1)
    forward(1)
    scatter_mid(0, 1, sb1, q1, t1)
    cotangent(0)
    cotangent(1)
    store(0, out_ref, out_hbm)
    grad_rank(x, c)
    gather_forward(1, 0, r2)
    backward(0)
    gather_forward(1, 1, r2)
    scatter_mid(1, 0, sb2, q2, t2)
    backward(1)
    for d in (1, 3, 2):
        grad_rank(chips[d], c)
    scatter_mid(1, 1, sb2, q2, t2)
    for d in (0, 1, 3, 2):
        grad_rank(chips[d], other)
    grad_first()
    d_residual(0)
    d_residual(1)
    grad_middle()

    all_to_all_wait(2, a3s, a3r)
    weighted = (a3r[...].reshape(TOK, CH).astype(F32) * tout).astype(BF16)
    a4s[...] = mm(kronT[...], weighted).astype(BF16).reshape(NSEQ, POS, CH)
    all_to_all_send(3, a4s, a4r)
    grad_second()
    drain()

    rows_y = second_sum(0, y2s, y2r, z)
    rows_z = second_sum(1, z2s, z2r, y)
    gd_ref[:, 0:LANES] = rows_y[0:ROWS]
    gd_ref[:, LANES : 2 * LANES] = rows_z[0:ROWS]
    gd_ref[:, 2 * LANES : HID] = rows_y[ROWS:48] + rows_z[ROWS:48]
    store(2, gd_ref, gd_hbm)

    all_to_all_wait(3, a4s, a4r)
    scaled = (a4r[...].reshape(TOK, CH).astype(F32) * tin).astype(BF16)
    d_mix = mm(scaled, bm_ref[...], 0, 1)
    din_ref[...] = (dres_s[...].astype(F32) + d_mix).astype(BF16)

    store(1, din_ref, din_hbm)

    drain()


def finish(out_in, din_in, gd_in, out_ref, din_ref, gd_ref):
    out_ref[...] = out_in[...]
    din_ref[...] = din_in[...]
    gd_ref[...] = gd_in[...]


def body(
    inputs, targets, block_mix, cross_mix, twiddle_in, twiddle_out, norm_gain, w_gate, w_up, w_down
):
    hbm = pl.BlockSpec(memory_space=pltpu.HBM)
    vmem = pl.BlockSpec(memory_space=pltpu.VMEM)
    dma = pltpu.SemaphoreType.DMA
    chunks = pltpu.VMEM((NSEQ, POS, CH), BF16)
    blocks4 = pltpu.VMEM((2, 4, CH, HT), BF16)
    results = (
        jax.ShapeDtypeStruct((CH, TOK), BF16),
        jax.ShapeDtypeStruct((CH, TOK), BF16),
        jax.ShapeDtypeStruct((ROWS, HID), F32),
    )
    made = pl.pallas_call(
        kernel,
        out_shape=results,
        in_specs=[hbm] * 10,
        out_specs=(hbm, hbm, hbm),
        scratch_shapes=[
            pltpu.VMEM((CH, TOK), BF16),
            pltpu.VMEM((CH, TOK), BF16),
            pltpu.VMEM((ROWS, HID), F32),
            pltpu.VMEM((CH, TOK), BF16),
            pltpu.VMEM((CH, TOK), BF16),
            pltpu.VMEM((TOK, TOK), BF16),
            pltpu.VMEM((NSEQ, NSEQ), BF16),
            pltpu.VMEM((1, TOK), F32),
            pltpu.VMEM((NSEQ, POS), F32),
            pltpu.VMEM((D // 128, 128), F32),
            pltpu.VMEM((D, HID), BF16),
            pltpu.VMEM((D, HID), BF16),
            pltpu.VMEM((D, HID), BF16),
            pltpu.VMEM((4, 2 * HID, HID), BF16),
            pltpu.VMEM((4, HID, HID), BF16),
            pltpu.VMEM((NSEQ * LINE, TOK), BF16),
            pltpu.VMEM((TOK, TOK), BF16),
        ]
        + [pltpu.VMEM((8, LINE, CH), BF16)] * 2
        + [pltpu.VMEM((NSEQ, LINE, CH), BF16)] * 2
        + [chunks] * 4
        + [
            pltpu.VMEM((2, NTEN, CH, HT), BF16),
            pltpu.VMEM((2, NTEN, CH, HT), BF16),
            pltpu.VMEM((2, NTEN, 8, HT), F32),
            pltpu.VMEM((2, NTEN, 8, HT), F32),
        ]
        + [blocks4] * 8
        + [
            pltpu.VMEM((2, 4, CH, HT), F32),
            pltpu.VMEM((2, HID, HT), F32),
            pltpu.VMEM((2, HID, HT), F32),
            pltpu.VMEM((2, HID, HT), BF16),
            pltpu.VMEM((2, CH, HT), F32),
            pltpu.VMEM((CH, TOK), BF16),
            pltpu.VMEM((8, CH + 96, LANES), BF16),
            pltpu.VMEM((7, CH + 96, LANES), BF16),
            pltpu.VMEM((8, 2 * CH, LANES), BF16),
            pltpu.VMEM((7, 2 * CH, LANES), BF16),
            pltpu.VMEM((8, 48, LANES), BF16),
            pltpu.VMEM((8, 48, LANES), BF16),
            pltpu.VMEM((8, 48, LANES), BF16),
            pltpu.VMEM((8, 48, LANES), BF16),
            pltpu.VMEM((2, NSEQ, POS), F32),
            pltpu.SemaphoreType.REGULAR,
            dma((2,)),
            dma((3,)),
            dma((10,)),
            dma((4, NSEQ)),
            dma((4, NSEQ)),
            dma((2, 4, 2)),
            dma((2, 4, 2)),
            dma((2, 4, 2)),
            dma((2, 4, 2)),
            dma((2, 2, NTEN)),
            dma((2, 2, NTEN)),
            dma((2, 2, 4)),
            dma((2, 2, 4)),
            dma((2, 2, 4)),
            dma((2, 2, 4)),
            dma((2, 7)),
            dma((2, 7)),
            dma((2, 8)),
            dma((2, 8)),
        ],
        compiler_params=pltpu.CompilerParams(
            collective_id=0, has_side_effects=True, vmem_limit_bytes=64 * 1024 * 1024
        ),
        name="monarch_block",
    )(
        inputs[0].T,
        targets[0].T,
        block_mix,
        cross_mix,
        twiddle_in,
        twiddle_out,
        norm_gain.reshape(D // 128, 128),
        w_gate,
        w_up,
        w_down,
    )
    output, d_input, grad_down = pl.pallas_call(
        finish,
        out_shape=results,
        in_specs=[vmem] * 3,
        out_specs=(vmem, vmem, vmem),
        compiler_params=pltpu.CompilerParams(vmem_limit_bytes=64 * 1024 * 1024),
        name="hand_over",
    )(*made)
    return output.T[None], d_input.T[None], grad_down


def solution(mesh):
    return jax.shard_map(
        body,
        mesh=mesh,
        in_specs=(
            P("dp", "seq", "tensor"),
            P("dp", "seq", "tensor"),
            P(),
            P(),
            P("seq", None),
            P(None, "seq"),
            P(),
            P(None, "tensor"),
            P(None, "tensor"),
            P(None, "tensor"),
        ),
        out_specs=(P("dp", "seq", "tensor"), P("dp", "seq", "tensor"), P(("dp", "seq"), "tensor")),
        check_vma=False,
    )
```

```python
import functools

import jax
import jax.numpy as jnp
from jax import lax
from jax.experimental import pallas as pl
from jax.experimental.pallas import tpu as pltpu
from jax.sharding import PartitionSpec as P

F32 = jnp.float32
BF16 = jnp.bfloat16
MESH = pl.DeviceIdType.MESH

TOK = 256
HT = TOK // 2
CH = 192
HID = 384
NSEQ = 16
NTEN = 8
POS = 16
PACKED = 48
LINE = 32
FAR_FIRST = (4, 3, 5, 2, 6, 1, 7)
D = 1536
LANES = 128
ROWS = 24
EPS = 1e-05


def mm(a, b, ca=1, cb=0):
    return lax.dot_general(a, b, (((ca,), (cb,)), ((), ())), preferred_element_type=F32)


def eye(n, dtype=BF16):
    rows = lax.broadcasted_iota(jnp.int32, (n, n), 0)
    cols = lax.broadcasted_iota(jnp.int32, (n, n), 1)
    return jnp.where(rows == cols, 1.0, 0.0).astype(dtype)


def column_of(row):
    n = row.shape[1]
    return jnp.sum(eye(n, F32) * row, axis=1, keepdims=True)


def kernel(
    x_hbm, tgt_hbm, bm_hbm, cm_hbm, ti_hbm, to_hbm, gain_hbm, wg_hbm, wu_hbm, wd_hbm,
    out_hbm, din_hbm, gd_hbm,
    out_ref, din_ref, gd_ref, x_ref, tgt_ref, bm_ref, cm_ref, ti_ref, to_ref, gain_ref,
    wg, wu, wd, wguT, wdT, kron, kronT,
    a1s, a1r, a2s, a2r, a3s, a3r, a4s, a4r,
    r1, r2, v1, v2,
    p1, p2, sb1, sb2, q1, q2, t1, t2, own, gate_s, up_s, hid_s, res_s, dres_s,
    ya, yr, zb, zr, y2s, y2r, z2s, z2r,
    to_pair, cross_sem, tw_sem, osem, wsem, a_ss, a_rs, ag_ss, ag_rs, sib_ss, sib_rs, v_ss, v_rs,
    rsib_ss, rsib_rs, rs_ss, rs_rs, g_ss, g_rs, g2_ss, g2_rs,
):
    dp = lax.axis_index("dp")
    sq = lax.axis_index("seq")
    tn = lax.axis_index("tensor")
    x, c = tn // 2, tn % 2
    y, zh = sq // 2, sq % 2
    z = zh * 4 + dp

    def seq_dev(s):
        return (dp, s, tn)

    def ten_dev(t):
        return (dp, sq, t)

    def y_dev(yy):
        return (dp, yy * 2 + zh, tn)

    def z_dev(zz):
        return (lax.rem(zz, 4), y * 2 + zz // 4, tn)

    pending = []

    def drain():
        while pending:
            pending.pop(0)()


    def send(src, dst, ss, rs, dev):
        cp = pltpu.make_async_remote_copy(
            src_ref=src, dst_ref=dst, send_sem=ss, recv_sem=rs, device_id=dev, device_id_type=MESH
        )
        cp.start()
        pending.append(cp.wait_send)

    def wait_recv(buf, ss, rs):
        pltpu.make_async_remote_copy(
            src_ref=buf, dst_ref=buf, send_sem=ss, recv_sem=rs,
            device_id=(dp, sq, tn), device_id_type=MESH,
        ).wait_recv()

    loads = []
    for n, (src, dst) in enumerate(
        (
            (x_hbm, x_ref), (bm_hbm, bm_ref), (ti_hbm, ti_ref), (cm_hbm, cm_ref), (to_hbm, to_ref),
            (gain_hbm, gain_ref), (wg_hbm, wg), (wu_hbm, wu), (wd_hbm, wd), (tgt_hbm, tgt_ref),
        )
    ):
        cp = pltpu.make_async_copy(src, dst, wsem.at[n])
        loads.append(cp)
    for cp in loads[0:3]:
        cp.start()

    barrier = pltpu.get_barrier_semaphore()

    def greet(dev):
        pl.semaphore_signal(barrier, inc=1, device_id=dev, device_id_type=MESH)

    for i in FAR_FIRST:
        greet(y_dev(lax.rem(y + i, 8)))
        greet(z_dev(lax.rem(z + i, 8)))
    for i in (4, 5, 3, 6, 2, 7, 1):
        greet(ten_dev(lax.rem(tn + i, NTEN)))
    for cp in loads[3:]:
        cp.start()

    def store(n, src, dst):
        cp = pltpu.make_async_copy(src, dst, osem.at[n])
        cp.start()
        pending.append(cp.wait)

    def a2a_copy(n, src, dst, peer):
        return pltpu.make_async_remote_copy(
            src_ref=src.at[peer], dst_ref=dst.at[sq],
            send_sem=a_ss.at[n, peer], recv_sem=a_rs.at[n, sq],
            device_id=seq_dev(peer), device_id_type=MESH,
        )

    def all_to_all_send(n, src, dst):
        for i in FAR_FIRST + (0,):
            yy = lax.rem(y + i, 8)
            a2a_copy(n, src, dst, yy * 2 + 1 - zh).start()
            if i:
                a2a_copy(n, src, dst, yy * 2 + zh).start()
        dst[sq] = src[sq]
        pending.append(functools.partial(all_to_all_done, n, src, dst))

    def all_to_all_send_half(n, src, dst, h):
        for i in (2, 1, 3, 0):
            yy = h * 4 + lax.rem(y + i, 4)
            a2a_copy(n, src, dst, yy * 2 + 1 - zh).start()

            @pl.when(yy != y)
            def _():
                a2a_copy(n, src, dst, yy * 2 + zh).start()

        if h:
            dst[sq] = src[sq]
            pending.append(functools.partial(all_to_all_done, n, src, dst))

    def all_to_all_wait(n, src, dst):
        for i in (0, 7, 1, 6, 2, 5, 3, 4):
            for other_line in range(2):
                if i or other_line:
                    peer = lax.rem(y + i, 8) * 2 + (1 - zh if other_line else zh)
                    wait_recv(dst.at[peer], a_ss.at[n, peer], a_rs.at[n, peer])

    def all_to_all_wait_half(n, src, dst, h):
        for i in (0, 3, 1, 2):
            yy = h * 4 + lax.rem(y + i, 4)

            @pl.when(yy != y)
            def _():
                peer = yy * 2 + zh
                wait_recv(dst.at[peer], a_ss.at[n, peer], a_rs.at[n, peer])

            peer = yy * 2 + 1 - zh
            wait_recv(dst.at[peer], a_ss.at[n, peer], a_rs.at[n, peer])

    def all_to_all_done(n, src, dst):
        def one(i, carry):
            a2a_copy(n, src, dst, lax.rem(sq + i, NSEQ)).wait_send()
            return carry

        lax.fori_loop(1, NSEQ, one, 0)

    def line_copy(peer):
        return pltpu.make_async_remote_copy(
            src_ref=a1s.at[peer], dst_ref=a1r.at[y],
            send_sem=a_ss.at[0, peer], recv_sem=a_rs.at[0, y],
            device_id=y_dev(peer), device_id_type=MESH,
        )

    def line_done():
        for i in FAR_FIRST:
            line_copy(lax.rem(y + i, 8)).wait_send()

    for cp in loads[0:3]:
        cp.wait()
    tin = column_of(ti_ref[...])
    section = mm(bm_ref[...], x_ref[...], 0, 1) * tin
    a1s[...] = section.astype(BF16).reshape(8, LINE, CH)

    rows = lax.broadcasted_iota(jnp.int32, (TOK, NSEQ), 0)
    cols = lax.broadcasted_iota(jnp.int32, (TOK, NSEQ), 1)
    for cp in loads[3:6]:
        cp.wait()
    cross = cm_ref[...]

    def iota(shape, dim):
        return lax.broadcasted_iota(jnp.int32, shape, dim)

    def flags(hit):
        return jnp.where(hit, 1.0, 0.0).astype(BF16)

    rows_here = flags(iota((8, NSEQ), 1) == 2 * iota((8, NSEQ), 0) + zh)
    cross_here = mm(rows_here, cross).astype(BF16)
    wide = mm(flags(iota((NSEQ * LINE, NSEQ), 0) // LINE == iota((NSEQ * LINE, NSEQ), 1)), cross_here, 1, 1)
    wide = mm(wide.astype(BF16), flags(iota((8, TOK), 1) // LINE == iota((8, TOK), 0)))
    same_pos = iota((NSEQ * LINE, TOK), 0) % LINE == iota((NSEQ * LINE, TOK), 1) % LINE
    kron[...] = jnp.where(same_pos, wide, 0.0).astype(BF16)
    pick_block = flags(rows // POS == cols)
    pick_pos = jnp.where(rows % POS == cols, 1.0, 0.0)
    wide = mm(mm(pick_block, cross).astype(BF16), pick_block, 1, 1)
    same_pos = iota((TOK, TOK), 0) % POS == iota((TOK, TOK), 1) % POS
    kronT[...] = jnp.where(same_pos, wide, 0.0).astype(BF16)
    tout_all = jnp.broadcast_to(to_ref[...][:, None, :], (NSEQ, POS, POS)).reshape(TOK, POS)
    tout = jnp.sum(tout_all * pick_pos, axis=1, keepdims=True)
    flat = tn * CH + lax.broadcasted_iota(jnp.int32, (CH, 128), 0)
    lane = lax.broadcasted_iota(jnp.int32, (CH, 128), 1)
    gain = jnp.zeros((CH, 128), F32)
    for k in range(D // 128):
        gain = gain + jnp.where(flat == k * 128 + lane, gain_ref[k : k + 1, :], 0.0)
    gain = jnp.sum(gain, axis=1, keepdims=True)

    pl.semaphore_wait(barrier, 7 + 7 + (NTEN - 1))
    partner = (dp, y * 2 + 1 - zh, tn)
    for i in FAR_FIRST:
        line_copy(lax.rem(y + i, 8)).start()
    pending.append(line_done)
    a1r[y] = a1s[y]
    pl.semaphore_signal(cross_sem, inc=1, device_id=partner, device_id_type=MESH)
    to_pair[zh] = to_ref[...]
    send(to_pair.at[zh], to_pair.at[zh], tw_sem.at[0], tw_sem.at[1], partner)

    for cp in loads[6:]:
        cp.wait()
    eye_h = eye(HID)
    for r in range(NTEN):
        block = slice(r * CH, (r + 1) * CH)
        wguT[r, 0:HID, :] = mm(eye_h, wg[block, :], 1, 1).astype(BF16)
        wguT[r, HID : 2 * HID, :] = mm(eye_h, wu[block, :], 1, 1).astype(BF16)
        wdT[r] = mm(eye_h, wd[block, :], 1, 1).astype(BF16)
    eye_c = eye(CH)

    wait_recv(to_pair.at[1 - zh], tw_sem.at[0], tw_sem.at[1])
    tline = jnp.zeros((NSEQ * LINE, 1), F32)
    for half in range(2):
        spread = jnp.broadcast_to(to_pair[half][:, None, :], (NSEQ, LINE, POS)).reshape(NSEQ * LINE, POS)
        here = iota((NSEQ * LINE, POS), 0) % LINE == half * POS + iota((NSEQ * LINE, POS), 1)
        tline = tline + jnp.sum(jnp.where(here, spread, 0.0), axis=1, keepdims=True)
    pl.semaphore_wait(cross_sem, 1)
    for i in FAR_FIRST:
        peer = lax.rem(y + i, 8)
        wait_recv(a1r.at[peer], a_ss.at[0, peer], a_rs.at[0, peer])

    mixed = mm(kron[...], a1r[...].reshape(TOK, CH)) * tline
    mixed = mixed.reshape(NSEQ, LINE, CH)
    a2s[:, 0:LINE, :] = mixed[:, :, 0:LANES].astype(BF16)
    rest = mixed[:, :, LANES:CH]
    rest = jnp.concatenate([rest[:, 0:POS], rest[:, POS:LINE]], axis=2)
    a2s[:, LINE:PACKED, :] = rest.astype(BF16)
    all_to_all_send(1, a2s, a2r)

    halves = [slice(0, HT), slice(HT, TOK)]

    def residual(h):
        all_to_all_wait_half(1, a2s, a2r, h)
        terms = a2r[h * 8 : h * 8 + 8].astype(F32).reshape(4, 2, PACKED, LANES)
        terms = terms[:, 0] + terms[:, 1]
        rest = terms[:, LINE:PACKED]
        rest = jnp.concatenate([rest[:, :, 0 : CH - LANES], rest[:, :, CH - LANES : LANES]], axis=1)
        mixed = jnp.concatenate([terms[:, 0:LINE], rest], axis=2).astype(BF16).reshape(HT, CH)
        mixed = mm(eye_c, mixed, 1, 1)
        res = (x_ref[:, halves[h]].astype(F32) + mixed).astype(BF16).astype(F32)
        res_s[h] = res
        r1[h, tn] = (res * gain).astype(BF16)
        gather_start(0, h, r1)
        share_row(0, h, v1, jnp.sum(res * res, axis=0, keepdims=True))

    def share_row(n, h, buf, row):
        buf[h, tn] = jnp.broadcast_to(row, (8, HT))

        for i in (4, 5, 3, 6, 2, 7, 1):
            peer = lax.rem(tn + i, NTEN)
            pltpu.make_async_remote_copy(
                src_ref=buf.at[h, tn], dst_ref=buf.at[h, tn],
                send_sem=v_ss.at[n, h, peer], recv_sem=v_rs.at[n, h, tn],
                device_id=ten_dev(peer), device_id_type=MESH,
            ).start()
        pending.append(functools.partial(rows_done, n, h, buf))

    def sum_rows(n, h, buf):
        for i in range(1, NTEN):
            peer = lax.rem(tn + i, NTEN)
            wait_recv(buf.at[h, peer], v_ss.at[n, h, peer], v_rs.at[n, h, peer])
        return jnp.sum(buf[h, :, 0:1, :], axis=0)

    def rows_done(n, h, buf):
        def one(i, carry):
            peer = lax.rem(tn + i, NTEN)
            pltpu.make_async_remote_copy(
                src_ref=buf.at[h, tn], dst_ref=buf.at[h, tn],
                send_sem=v_ss.at[n, h, peer], recv_sem=v_rs.at[n, h, peer],
                device_id=ten_dev(peer), device_id_type=MESH,
            ).wait_send()
            return carry

        lax.fori_loop(1, NTEN, one, 0)

    chips = [lax.rem(x + d, 4) for d in range(4)]
    other = 1 - c

    def gather_start(n, h, buf):
        part = buf.at[h, tn]
        for d in (2, 1, 3):
            send(part, part, ag_ss.at[n, d, h], ag_rs.at[n, d, h], ten_dev(chips[d] * 2 + c))
        send(part, part, sib_ss.at[n, 0, h], sib_rs.at[n, 0, h], ten_dev(x * 2 + other))

    def gather_forward(n, h, buf, then=None):
        for d in (1, 3, 2):
            src = lax.rem(x + 4 - d, 4) * 2 + c
            part = buf.at[h, src]
            wait_recv(part, ag_ss.at[n, d, h], ag_rs.at[n, d, h])
            send(part, part, sib_ss.at[n, d, h], sib_rs.at[n, d, h], ten_dev(x * 2 + other))
            if then is not None:
                then(src // 2, c)

    def gather_matmul(n, h, buf, weights):
        acc = None
        for d in (0, 1, 3, 2):
            rank = lax.rem(x + 4 - d, 4) * 2 + c
            term = mm(weights[rank], buf[h, rank])
            acc = term if acc is None else acc + term
        for d in (0, 1, 3, 2):
            rank = lax.rem(x + 4 - d, 4) * 2 + other
            wait_recv(buf.at[h, rank], sib_ss.at[n, d, h], sib_rs.at[n, d, h])
            acc = acc + mm(weights[rank], buf[h, rank])
        return acc

    def scatter_start(n, h, part_of, p, sb):
        for d in (2, 1, 3, 0):
            p[h, d] = part_of(chips[d] * 2 + other).astype(BF16)
            send(p.at[h, d], sb.at[h, d], rsib_ss.at[n, h, d], rsib_rs.at[n, h, d], ten_dev(x * 2 + other))
        for d in (2, 1, 3, 0):
            own[h, d] = part_of(chips[d] * 2 + c)

    def scatter_mid(n, h, sb, q, t):
        for d in (2, 1, 3):
            wait_recv(sb.at[h, d], rsib_ss.at[n, h, d], rsib_rs.at[n, h, d])
            q[h, d] = (own[h, d] + sb[h, d].astype(F32)).astype(BF16)
            send(q.at[h, d], t.at[h, d], rs_ss.at[n, h, d], rs_rs.at[n, h, d], ten_dev(chips[d] * 2 + c))

    def scatter_end(n, h, sb, t):
        wait_recv(sb.at[h, 0], rsib_ss.at[n, h, 0], rsib_rs.at[n, h, 0])
        total = own[h, 0] + sb[h, 0].astype(F32)
        for d in (1, 3, 2):
            wait_recv(t.at[h, d], rs_ss.at[n, h, d], rs_rs.at[n, h, d])
            total = total + t[h, d].astype(F32)
        return total

    def rows_of(ref, r):
        return ref[pl.ds(pl.multiple_of(r * CH, CH), CH), :]

    inv = [None, None]

    def forward(h):
        pre = gather_matmul(0, h, r1, wguT)
        inv[h] = lax.rsqrt(sum_rows(0, h, v1) / D + EPS)
        gate_pre = pre[0:HID] * inv[h]
        up_pre = pre[HID : 2 * HID] * inv[h]
        sig = jax.nn.sigmoid(gate_pre)
        hid_s[h] = (gate_pre * sig * up_pre).astype(BF16)
        gate_s[h] = gate_pre
        up_s[h] = up_pre
        scatter_start(0, h, lambda r: mm(rows_of(wd, r), hid_s[h]), p1, sb1)

    def cotangent(h):
        summed = res_s[h] + scatter_end(0, h, sb1, t1)
        r2[h, tn] = (summed - tgt_ref[:, halves[h]].astype(F32)).astype(BF16)
        gather_start(1, h, r2)
        out_ref[:, halves[h]] = summed.astype(BF16)

    def backward(h):
        d_hidden = gather_matmul(1, h, r2, wdT)
        gate_pre = gate_s[h]
        up_pre = up_s[h]
        sig = jax.nn.sigmoid(gate_pre)
        d_gate = (d_hidden * up_pre * sig * (1.0 + gate_pre * (1.0 - sig))).astype(BF16)
        d_up = (d_hidden * gate_pre * sig).astype(BF16)
        inner = d_gate.astype(F32) * gate_pre + d_up.astype(F32) * up_pre
        share_row(1, h, v2, jnp.sum(inner, axis=0, keepdims=True))
        scatter_start(1, h, lambda r: mm(rows_of(wg, r), d_gate) + mm(rows_of(wu, r), d_up), p2, sb2)

    def d_residual(h):
        d_normed = scatter_end(1, h, sb2, t2)
        corr = sum_rows(1, h, v2) / D
        d_res = r2[h, tn].astype(F32) + inv[h] * (gain * d_normed - res_s[h] * inv[h] * corr)
        dres_s[:, halves[h]] = d_res.astype(BF16)
        d_tok = mm(eye_h[0:HT, 0:HT], d_res.astype(BF16), 1, 1)
        a3s[h * 8 : h * 8 + 8] = d_tok.astype(BF16).reshape(8, POS, CH)
        all_to_all_send_half(2, a3s, a3r, h)

    sign = 1 - 2 * c

    def grad_rank(chip, yhi):
        cots = jnp.concatenate([r2[h, chip * 2 + yhi] for h in range(2)], axis=1)
        hids = jnp.concatenate([hid_s[h] for h in range(2)], axis=1)
        g = mm(cots, hids, 1, 1)
        first, second, third = (g[:, n * LANES : (n + 1) * LANES] for n in range(3))
        at = pl.multiple_of(chip * 48, 16)
        for m in range(4):
            ya[yhi * 4 + m, pl.ds(at, 48), :] = first[m * 48 : m * 48 + 48].astype(BF16)
        zat = pl.multiple_of(yhi * 96, 16)
        for half in range(2):
            pieces = [second[m * 48 + half * ROWS : m * 48 + half * ROWS + ROWS] for m in range(4)]
            zb[half * 4 + chip, pl.ds(zat, 96), :] = jnp.concatenate(pieces, axis=0).astype(BF16)

        @pl.when(chip < 2)
        def _():
            for m in range(4):
                ya[yhi * 4 + m, pl.ds(CH + at, 48), :] = third[m * 48 : m * 48 + 48].astype(BF16)

        @pl.when(chip >= 2)
        def _():
            for half in range(2):
                pieces = [third[m * 48 + half * ROWS : m * 48 + half * ROWS + ROWS] for m in range(4)]
                zb[half * 4 + chip, pl.ds(CH + zat, 96), :] = jnp.concatenate(pieces, axis=0).astype(BF16)

    def away(me, k):
        return lax.rem(me + sign * k + 8, 8)

    def sized(axis, target, work):
        if axis == 0:
            work(CH + 96)
            return

        @pl.when(lax.rem(target, 4) < 2)
        def _():
            work(CH)

        @pl.when(lax.rem(target, 4) >= 2)
        def _():
            work(2 * CH)

    AXES = ((ya, yr, y, y_dev), (zb, zr, z, z_dev))

    def grad_copy(axis, slot, to, target, rows):
        src, dst, me, dev = AXES[axis]
        return pltpu.make_async_remote_copy(
            src_ref=src.at[target, pl.ds(0, rows)], dst_ref=dst.at[slot, pl.ds(0, rows)],
            send_sem=g_ss.at[axis, slot], recv_sem=g_rs.at[axis, slot],
            device_id=dev(away(me, to)), device_id_type=MESH,
        )

    STEP1 = ((0, 2, 4), (1, 1, 3), (2, -1, -3))
    STEP2 = ((3, 1, 1), (4, -1, -1))
    STEP3 = ((5, 2, 2), (6, -2, -2))

    def grad_step(axis, sends):
        me = AXES[axis][2]
        for slot, to, place in sends:
            target = away(me, place)
            sized(axis, target, lambda rows: grad_copy(axis, slot, to, target, rows).start())

            def done(slot=slot, to=to, target=target):
                sized(axis, target, lambda rows: grad_copy(axis, slot, to, target, rows).wait_send())

            pending.append(done)

    def grad_add(axis, target, slots):
        buf, got, me, dev = AXES[axis]

        def work(rows):
            total = buf[target, 0:rows, :].astype(F32)
            for slot in slots:
                part = got.at[slot, pl.ds(0, rows)]
                wait_recv(part, g_ss.at[axis, slot], g_rs.at[axis, slot])
                total = total + part[...].astype(F32)
            buf[target, 0:rows, :] = total.astype(BF16)

        sized(axis, target, work)

    def grad_first():
        for axis in range(2):
            grad_step(axis, STEP1)

    def grad_middle():
        for axis in range(2):
            grad_step(axis, STEP2)
        for axis in range(2):
            me = AXES[axis][2]
            grad_add(axis, away(me, 2), (0, 1))
            grad_add(axis, away(me, -2), (2,))
            grad_step(axis, STEP3)

    def grad_second():
        total = ya[y].astype(F32)
        for slot in (3, 4, 6, 5):
            wait_recv(yr.at[slot], g_ss.at[0, slot], g_rs.at[0, slot])
            total = total + yr[slot].astype(F32)
        for zl in range(4):
            for half in range(2):
                at = zl * 48 + half * ROWS
                pieces = [total[at : at + ROWS]]
                if zl < 2:
                    pieces.append(total[CH + at : CH + at + ROWS])
                else:
                    pieces.append(jnp.zeros((ROWS, LANES), F32))
                y2s[half * 4 + zl] = jnp.concatenate(pieces, axis=0).astype(BF16)
        second_send(0, y2s, y2r, z, z_dev)

        def sum_z(rows):
            total = zb[z, 0:rows, :].astype(F32)
            for slot in (3, 4, 6, 5):
                part = zr.at[slot, pl.ds(0, rows)]
                wait_recv(part, g_ss.at[1, slot], g_rs.at[1, slot])
                total = total + part[...].astype(F32)
            for yy in range(8):
                pieces = [total[yy * ROWS : yy * ROWS + ROWS]]
                if rows > CH:
                    pieces.append(total[CH + yy * ROWS : CH + yy * ROWS + ROWS])
                else:
                    pieces.append(jnp.zeros((ROWS, LANES), F32))
                z2s[yy] = jnp.concatenate(pieces, axis=0).astype(BF16)

        sized(1, z, sum_z)
        second_send(1, z2s, z2r, y, y_dev)

    def second_send(n, src, dst, me, dev):
        for i in FAR_FIRST:
            peer = lax.rem(me + i, 8)
            pltpu.make_async_remote_copy(
                src_ref=src.at[peer], dst_ref=dst.at[me],
                send_sem=g2_ss.at[n, peer], recv_sem=g2_rs.at[n, me],
                device_id=dev(peer), device_id_type=MESH,
            ).start()
        pending.append(functools.partial(second_done, n, src, me, dev))

    def second_done(n, src, me, dev):
        def one(i, carry):
            peer = lax.rem(me + i, 8)
            pltpu.make_async_remote_copy(
                src_ref=src.at[peer], dst_ref=src.at[peer],
                send_sem=g2_ss.at[n, peer], recv_sem=g2_rs.at[n, peer],
                device_id=dev(peer), device_id_type=MESH,
            ).wait_send()
            return carry

        lax.fori_loop(1, 8, one, 0)

    def second_sum(n, src, dst, me):
        total = src[me].astype(F32)
        for i in (7, 1, 6, 2, 5, 3, 4):
            peer = lax.rem(me + i, 8)
            wait_recv(dst.at[peer], g2_ss.at[n, peer], g2_rs.at[n, peer])
            total = total + dst[peer].astype(F32)
        return total

    residual(0)
    residual(1)
    gather_forward(0, 0, r1)
    forward(0)
    gather_forward(0, 1, r1)
    scatter_mid(0, 0, sb1, q1, t1)
    forward(1)
    scatter_mid(0, 1, sb1, q1, t1)
    cotangent(0)
    cotangent(1)
    store(0, out_ref, out_hbm)
    grad_rank(x, c)
    gather_forward(1, 0, r2)
    backward(0)
    gather_forward(1, 1, r2)
    scatter_mid(1, 0, sb2, q2, t2)
    backward(1)
    for d in (1, 3, 2):
        grad_rank(chips[d], c)
    scatter_mid(1, 1, sb2, q2, t2)
    for d in (0, 1, 3, 2):
        grad_rank(chips[d], other)
    earlier = list(pending)
    pending.clear()
    grad_first()
    d_residual(0)
    d_residual(1)
    grad_middle()
    for wait in earlier:
        wait()

    all_to_all_wait(2, a3s, a3r)
    weighted = (a3r[...].reshape(TOK, CH).astype(F32) * tout).astype(BF16)
    a4s[...] = mm(kronT[...], weighted).astype(BF16).reshape(NSEQ, POS, CH)
    all_to_all_send(3, a4s, a4r)
    grad_second()
    drain()

    all_to_all_wait(3, a4s, a4r)
    scaled = (a4r[...].reshape(TOK, CH).astype(F32) * tin).astype(BF16)
    d_mix = mm(scaled, bm_ref[...], 0, 1)
    din_ref[...] = (dres_s[...].astype(F32) + d_mix).astype(BF16)

    store(1, din_ref, din_hbm)

    rows_y = second_sum(0, y2s, y2r, z)
    rows_z = second_sum(1, z2s, z2r, y)
    gd_ref[:, 0:LANES] = rows_y[0:ROWS]
    gd_ref[:, LANES : 2 * LANES] = rows_z[0:ROWS]
    gd_ref[:, 2 * LANES : HID] = rows_y[ROWS:48] + rows_z[ROWS:48]
    store(2, gd_ref, gd_hbm)

    drain()


def finish(out_in, din_in, gd_in, out_ref, din_ref, gd_ref):
    out_ref[...] = out_in[...]
    din_ref[...] = din_in[...]
    gd_ref[...] = gd_in[...]


def body(
    inputs, targets, block_mix, cross_mix, twiddle_in, twiddle_out, norm_gain, w_gate, w_up, w_down
):
    hbm = pl.BlockSpec(memory_space=pltpu.HBM)
    vmem = pl.BlockSpec(memory_space=pltpu.VMEM)
    dma = pltpu.SemaphoreType.DMA
    chunks = pltpu.VMEM((NSEQ, POS, CH), BF16)
    blocks4 = pltpu.VMEM((2, 4, CH, HT), BF16)
    results = (
        jax.ShapeDtypeStruct((CH, TOK), BF16),
        jax.ShapeDtypeStruct((CH, TOK), BF16),
        jax.ShapeDtypeStruct((ROWS, HID), F32),
    )
    made = pl.pallas_call(
        kernel,
        out_shape=results,
        in_specs=[hbm] * 10,
        out_specs=(hbm, hbm, hbm),
        scratch_shapes=[
            pltpu.VMEM((CH, TOK), BF16),
            pltpu.VMEM((CH, TOK), BF16),
            pltpu.VMEM((ROWS, HID), F32),
            pltpu.VMEM((CH, TOK), BF16),
            pltpu.VMEM((CH, TOK), BF16),
            pltpu.VMEM((TOK, TOK), BF16),
            pltpu.VMEM((NSEQ, NSEQ), BF16),
            pltpu.VMEM((1, TOK), F32),
            pltpu.VMEM((NSEQ, POS), F32),
            pltpu.VMEM((D // 128, 128), F32),
            pltpu.VMEM((D, HID), BF16),
            pltpu.VMEM((D, HID), BF16),
            pltpu.VMEM((D, HID), BF16),
            pltpu.VMEM((NTEN, 2 * HID, CH), BF16),
            pltpu.VMEM((NTEN, HID, CH), BF16),
            pltpu.VMEM((NSEQ * LINE, TOK), BF16),
            pltpu.VMEM((TOK, TOK), BF16),
        ]
        + [pltpu.VMEM((8, LINE, CH), BF16)] * 2
        + [pltpu.VMEM((NSEQ, PACKED, LANES), BF16)] * 2
        + [chunks] * 4
        + [
            pltpu.VMEM((2, NTEN, CH, HT), BF16),
            pltpu.VMEM((2, NTEN, CH, HT), BF16),
            pltpu.VMEM((2, NTEN, 8, HT), F32),
            pltpu.VMEM((2, NTEN, 8, HT), F32),
        ]
        + [blocks4] * 8
        + [
            pltpu.VMEM((2, 4, CH, HT), F32),
            pltpu.VMEM((2, HID, HT), F32),
            pltpu.VMEM((2, HID, HT), F32),
            pltpu.VMEM((2, HID, HT), BF16),
            pltpu.VMEM((2, CH, HT), F32),
            pltpu.VMEM((CH, TOK), BF16),
            pltpu.VMEM((8, CH + 96, LANES), BF16),
            pltpu.VMEM((7, CH + 96, LANES), BF16),
            pltpu.VMEM((8, 2 * CH, LANES), BF16),
            pltpu.VMEM((7, 2 * CH, LANES), BF16),
            pltpu.VMEM((8, 48, LANES), BF16),
            pltpu.VMEM((8, 48, LANES), BF16),
            pltpu.VMEM((8, 48, LANES), BF16),
            pltpu.VMEM((8, 48, LANES), BF16),
            pltpu.VMEM((2, NSEQ, POS), F32),
            pltpu.SemaphoreType.REGULAR,
            dma((2,)),
            dma((3,)),
            dma((10,)),
            dma((4, NSEQ)),
            dma((4, NSEQ)),
            dma((2, 4, 2)),
            dma((2, 4, 2)),
            dma((2, 4, 2)),
            dma((2, 4, 2)),
            dma((2, 2, NTEN)),
            dma((2, 2, NTEN)),
            dma((2, 2, 4)),
            dma((2, 2, 4)),
            dma((2, 2, 4)),
            dma((2, 2, 4)),
            dma((2, 7)),
            dma((2, 7)),
            dma((2, 8)),
            dma((2, 8)),
        ],
        compiler_params=pltpu.CompilerParams(
            collective_id=0, has_side_effects=True, vmem_limit_bytes=64 * 1024 * 1024
        ),
        name="monarch_block",
    )(
        inputs[0].T,
        targets[0].T,
        block_mix,
        cross_mix,
        twiddle_in,
        twiddle_out,
        norm_gain.reshape(D // 128, 128),
        w_gate,
        w_up,
        w_down,
    )
    output, d_input, grad_down = pl.pallas_call(
        finish,
        out_shape=results,
        in_specs=[vmem] * 3,
        out_specs=(vmem, vmem, vmem),
        compiler_params=pltpu.CompilerParams(vmem_limit_bytes=64 * 1024 * 1024),
        name="hand_over",
    )(*made)
    return output.T[None], d_input.T[None], grad_down


def solution(mesh):
    return jax.shard_map(
        body,
        mesh=mesh,
        in_specs=(
            P("dp", "seq", "tensor"),
            P("dp", "seq", "tensor"),
            P(),
            P(),
            P("seq", None),
            P(None, "seq"),
            P(),
            P(None, "tensor"),
            P(None, "tensor"),
            P(None, "tensor"),
        ),
        out_specs=(P("dp", "seq", "tensor"), P("dp", "seq", "tensor"), P(("dp", "seq"), "tensor")),
        check_vma=False,
    )
```

```python
import functools

import jax
import jax.numpy as jnp
from jax import lax
from jax.experimental import pallas as pl
from jax.experimental.pallas import tpu as pltpu
from jax.sharding import PartitionSpec as P

F32 = jnp.float32
BF16 = jnp.bfloat16
MESH = pl.DeviceIdType.MESH

TOK = 256
HT = TOK // 2
CH = 192
HID = 384
NSEQ = 16
NTEN = 8
POS = 16
PACKED = 48
LINE = 32
FAR_FIRST = (4, 3, 5, 2, 6, 1, 7)
D = 1536
LANES = 128
ROWS = 24
EPS = 1e-05


def mm(a, b, ca=1, cb=0):
    return lax.dot_general(a, b, (((ca,), (cb,)), ((), ())), preferred_element_type=F32)


def eye(n, dtype=BF16):
    rows = lax.broadcasted_iota(jnp.int32, (n, n), 0)
    cols = lax.broadcasted_iota(jnp.int32, (n, n), 1)
    return jnp.where(rows == cols, 1.0, 0.0).astype(dtype)


def column_of(row):
    n = row.shape[1]
    return jnp.sum(eye(n, F32) * row, axis=1, keepdims=True)


def kernel(
    x_hbm, tgt_hbm, bm_hbm, cm_hbm, ti_hbm, to_hbm, gain_hbm, wg_hbm, wu_hbm, wd_hbm,
    out_hbm, din_hbm, gd_hbm,
    out_ref, din_ref, gd_ref, x_ref, tgt_ref, bm_ref, cm_ref, ti_ref, to_ref, gain_ref,
    wg, wu, wd, wguT, wdT, kron, kronT,
    a1s, a1r, a2s, a2r, a3s, a3r, a4s, a4r,
    r1, r2, v1, v2,
    p1, p2, sb1, sb2, q1, q2, t1, t2, own, gate_s, up_s, hid_s, res_s, dres_s,
    ya, yr, zb, zr, y2s, y2r, z2s, z2r,
    to_pair, cross_sem, tw_sem, osem, wsem, a_ss, a_rs, ag_ss, ag_rs, sib_ss, sib_rs, v_ss, v_rs,
    rsib_ss, rsib_rs, rs_ss, rs_rs, g_ss, g_rs, g2_ss, g2_rs,
):
    dp = lax.axis_index("dp")
    sq = lax.axis_index("seq")
    tn = lax.axis_index("tensor")
    x, c = tn // 2, tn % 2
    y, zh = sq // 2, sq % 2
    z = zh * 4 + dp

    def seq_dev(s):
        return (dp, s, tn)

    def ten_dev(t):
        return (dp, sq, t)

    def y_dev(yy):
        return (dp, yy * 2 + zh, tn)

    def z_dev(zz):
        return (lax.rem(zz, 4), y * 2 + zz // 4, tn)

    pending = []

    def drain():
        while pending:
            pending.pop(0)()


    def send(src, dst, ss, rs, dev):
        cp = pltpu.make_async_remote_copy(
            src_ref=src, dst_ref=dst, send_sem=ss, recv_sem=rs, device_id=dev, device_id_type=MESH
        )
        cp.start()
        pending.append(cp.wait_send)

    def wait_recv(buf, ss, rs):
        pltpu.make_async_remote_copy(
            src_ref=buf, dst_ref=buf, send_sem=ss, recv_sem=rs,
            device_id=(dp, sq, tn), device_id_type=MESH,
        ).wait_recv()

    loads = []
    for n, (src, dst) in enumerate(
        (
            (x_hbm, x_ref), (bm_hbm, bm_ref), (ti_hbm, ti_ref), (cm_hbm, cm_ref), (to_hbm, to_ref),
            (gain_hbm, gain_ref), (wg_hbm, wg), (wu_hbm, wu), (wd_hbm, wd), (tgt_hbm, tgt_ref),
        )
    ):
        cp = pltpu.make_async_copy(src, dst, wsem.at[n])
        loads.append(cp)
    for cp in loads[0:3]:
        cp.start()

    barrier = pltpu.get_barrier_semaphore()

    def greet(dev):
        pl.semaphore_signal(barrier, inc=1, device_id=dev, device_id_type=MESH)

    for i in FAR_FIRST:
        greet(y_dev(lax.rem(y + i, 8)))
        greet(z_dev(lax.rem(z + i, 8)))
    for i in (4, 5, 3, 6, 2, 7, 1):
        greet(ten_dev(lax.rem(tn + i, NTEN)))
    for cp in loads[3:]:
        cp.start()

    def store(n, src, dst):
        cp = pltpu.make_async_copy(src, dst, osem.at[n])
        cp.start()
        pending.append(cp.wait)

    def a2a_copy(n, src, dst, peer):
        return pltpu.make_async_remote_copy(
            src_ref=src.at[peer], dst_ref=dst.at[sq],
            send_sem=a_ss.at[n, peer], recv_sem=a_rs.at[n, sq],
            device_id=seq_dev(peer), device_id_type=MESH,
        )

    def all_to_all_send(n, src, dst):
        for i in FAR_FIRST + (0,):
            yy = lax.rem(y + i, 8)
            a2a_copy(n, src, dst, yy * 2 + 1 - zh).start()
            if i:
                a2a_copy(n, src, dst, yy * 2 + zh).start()
        dst[sq] = src[sq]
        pending.append(functools.partial(all_to_all_done, n, src, dst))

    def all_to_all_send_half(n, src, dst, h):
        for i in (2, 1, 3, 0):
            yy = h * 4 + lax.rem(y + i, 4)
            a2a_copy(n, src, dst, yy * 2 + 1 - zh).start()

            @pl.when(yy != y)
            def _():
                a2a_copy(n, src, dst, yy * 2 + zh).start()

        if h:
            dst[sq] = src[sq]
            pending.append(functools.partial(all_to_all_done, n, src, dst))

    def all_to_all_wait(n, src, dst):
        for i in (0, 7, 1, 6, 2, 5, 3, 4):
            for other_line in range(2):
                if i or other_line:
                    peer = lax.rem(y + i, 8) * 2 + (1 - zh if other_line else zh)
                    wait_recv(dst.at[peer], a_ss.at[n, peer], a_rs.at[n, peer])

    def all_to_all_wait_half(n, src, dst, h):
        for i in (0, 3, 1, 2):
            yy = h * 4 + lax.rem(y + i, 4)

            @pl.when(yy != y)
            def _():
                peer = yy * 2 + zh
                wait_recv(dst.at[peer], a_ss.at[n, peer], a_rs.at[n, peer])

            peer = yy * 2 + 1 - zh
            wait_recv(dst.at[peer], a_ss.at[n, peer], a_rs.at[n, peer])

    def all_to_all_done(n, src, dst):
        def one(i, carry):
            a2a_copy(n, src, dst, lax.rem(sq + i, NSEQ)).wait_send()
            return carry

        lax.fori_loop(1, NSEQ, one, 0)

    def line_copy(peer):
        return pltpu.make_async_remote_copy(
            src_ref=a1s.at[peer], dst_ref=a1r.at[y],
            send_sem=a_ss.at[0, peer], recv_sem=a_rs.at[0, y],
            device_id=y_dev(peer), device_id_type=MESH,
        )

    def line_done():
        for i in FAR_FIRST:
            line_copy(lax.rem(y + i, 8)).wait_send()

    for cp in loads[0:3]:
        cp.wait()
    tin = column_of(ti_ref[...])
    section = mm(bm_ref[...], x_ref[...], 0, 1) * tin
    a1s[...] = section.astype(BF16).reshape(8, LINE, CH)

    rows = lax.broadcasted_iota(jnp.int32, (TOK, NSEQ), 0)
    cols = lax.broadcasted_iota(jnp.int32, (TOK, NSEQ), 1)
    for cp in loads[3:6]:
        cp.wait()
    cross = cm_ref[...]

    def iota(shape, dim):
        return lax.broadcasted_iota(jnp.int32, shape, dim)

    def flags(hit):
        return jnp.where(hit, 1.0, 0.0).astype(BF16)

    rows_here = flags(iota((8, NSEQ), 1) == 2 * iota((8, NSEQ), 0) + zh)
    cross_here = mm(rows_here, cross).astype(BF16)
    wide = mm(flags(iota((NSEQ * LINE, NSEQ), 0) // LINE == iota((NSEQ * LINE, NSEQ), 1)), cross_here, 1, 1)
    wide = mm(wide.astype(BF16), flags(iota((8, TOK), 1) // LINE == iota((8, TOK), 0)))
    same_pos = iota((NSEQ * LINE, TOK), 0) % LINE == iota((NSEQ * LINE, TOK), 1) % LINE
    kron[...] = jnp.where(same_pos, wide, 0.0).astype(BF16)
    pick_block = flags(rows // POS == cols)
    pick_pos = jnp.where(rows % POS == cols, 1.0, 0.0)
    wide = mm(mm(pick_block, cross).astype(BF16), pick_block, 1, 1)
    same_pos = iota((TOK, TOK), 0) % POS == iota((TOK, TOK), 1) % POS
    kronT[...] = jnp.where(same_pos, wide, 0.0).astype(BF16)
    tout_all = jnp.broadcast_to(to_ref[...][:, None, :], (NSEQ, POS, POS)).reshape(TOK, POS)
    tout = jnp.sum(tout_all * pick_pos, axis=1, keepdims=True)
    flat = tn * CH + lax.broadcasted_iota(jnp.int32, (CH, 128), 0)
    lane = lax.broadcasted_iota(jnp.int32, (CH, 128), 1)
    gain = jnp.zeros((CH, 128), F32)
    for k in range(D // 128):
        gain = gain + jnp.where(flat == k * 128 + lane, gain_ref[k : k + 1, :], 0.0)
    gain = jnp.sum(gain, axis=1, keepdims=True)

    pl.semaphore_wait(barrier, 7 + 7 + (NTEN - 1))
    partner = (dp, y * 2 + 1 - zh, tn)
    for i in FAR_FIRST:
        line_copy(lax.rem(y + i, 8)).start()
    pending.append(line_done)
    a1r[y] = a1s[y]
    pl.semaphore_signal(cross_sem, inc=1, device_id=partner, device_id_type=MESH)
    to_pair[zh] = to_ref[...]
    send(to_pair.at[zh], to_pair.at[zh], tw_sem.at[0], tw_sem.at[1], partner)

    for cp in loads[6:]:
        cp.wait()
    eye_h = eye(HID)
    for r in range(NTEN):
        block = slice(r * CH, (r + 1) * CH)
        wguT[r, 0:HID, :] = mm(eye_h, wg[block, :], 1, 1).astype(BF16)
        wguT[r, HID : 2 * HID, :] = mm(eye_h, wu[block, :], 1, 1).astype(BF16)
        wdT[r] = mm(eye_h, wd[block, :], 1, 1).astype(BF16)
    eye_c = eye(CH)

    wait_recv(to_pair.at[1 - zh], tw_sem.at[0], tw_sem.at[1])
    tline = jnp.zeros((NSEQ * LINE, 1), F32)
    for half in range(2):
        spread = jnp.broadcast_to(to_pair[half][:, None, :], (NSEQ, LINE, POS)).reshape(NSEQ * LINE, POS)
        here = iota((NSEQ * LINE, POS), 0) % LINE == half * POS + iota((NSEQ * LINE, POS), 1)
        tline = tline + jnp.sum(jnp.where(here, spread, 0.0), axis=1, keepdims=True)
    pl.semaphore_wait(cross_sem, 1)
    for i in FAR_FIRST:
        peer = lax.rem(y + i, 8)
        wait_recv(a1r.at[peer], a_ss.at[0, peer], a_rs.at[0, peer])

    mixed = mm(kron[...], a1r[...].reshape(TOK, CH)) * tline
    mixed = mixed.reshape(NSEQ, LINE, CH)
    a2s[:, 0:LINE, :] = mixed[:, :, 0:LANES].astype(BF16)
    rest = mixed[:, :, LANES:CH]
    rest = jnp.concatenate([rest[:, 0:POS], rest[:, POS:LINE]], axis=2)
    a2s[:, LINE:PACKED, :] = rest.astype(BF16)
    all_to_all_send(1, a2s, a2r)

    halves = [slice(0, HT), slice(HT, TOK)]

    def residual(h):
        all_to_all_wait_half(1, a2s, a2r, h)
        terms = a2r[h * 8 : h * 8 + 8].astype(F32).reshape(4, 2, PACKED, LANES)
        terms = terms[:, 0] + terms[:, 1]
        rest = terms[:, LINE:PACKED]
        rest = jnp.concatenate([rest[:, :, 0 : CH - LANES], rest[:, :, CH - LANES : LANES]], axis=1)
        mixed = jnp.concatenate([terms[:, 0:LINE], rest], axis=2).astype(BF16).reshape(HT, CH)
        mixed = mm(eye_c, mixed, 1, 1)
        res = (x_ref[:, halves[h]].astype(F32) + mixed).astype(BF16).astype(F32)
        res_s[h] = res
        r1[h, tn] = (res * gain).astype(BF16)
        gather_start(0, h, r1)
        share_row(0, h, v1, jnp.sum(res * res, axis=0, keepdims=True))

    def share_row(n, h, buf, row):
        buf[h, tn] = jnp.broadcast_to(row, (8, HT))

        for i in (4, 5, 3, 6, 2, 7, 1):
            peer = lax.rem(tn + i, NTEN)
            pltpu.make_async_remote_copy(
                src_ref=buf.at[h, tn], dst_ref=buf.at[h, tn],
                send_sem=v_ss.at[n, h, peer], recv_sem=v_rs.at[n, h, tn],
                device_id=ten_dev(peer), device_id_type=MESH,
            ).start()
        pending.append(functools.partial(rows_done, n, h, buf))

    def sum_rows(n, h, buf):
        for i in range(1, NTEN):
            peer = lax.rem(tn + i, NTEN)
            wait_recv(buf.at[h, peer], v_ss.at[n, h, peer], v_rs.at[n, h, peer])
        return jnp.sum(buf[h, :, 0:1, :], axis=0)

    def rows_done(n, h, buf):
        def one(i, carry):
            peer = lax.rem(tn + i, NTEN)
            pltpu.make_async_remote_copy(
                src_ref=buf.at[h, tn], dst_ref=buf.at[h, tn],
                send_sem=v_ss.at[n, h, peer], recv_sem=v_rs.at[n, h, peer],
                device_id=ten_dev(peer), device_id_type=MESH,
            ).wait_send()
            return carry

        lax.fori_loop(1, NTEN, one, 0)

    chips = [lax.rem(x + d, 4) for d in range(4)]
    other = 1 - c

    def gather_start(n, h, buf):
        part = buf.at[h, tn]
        for d in (2, 1, 3):
            send(part, part, ag_ss.at[n, d, h], ag_rs.at[n, d, h], ten_dev(chips[d] * 2 + c))
        send(part, part, sib_ss.at[n, 0, h], sib_rs.at[n, 0, h], ten_dev(x * 2 + other))

    def gather_forward(n, h, buf, then=None):
        for d in (1, 3, 2):
            src = lax.rem(x + 4 - d, 4) * 2 + c
            part = buf.at[h, src]
            wait_recv(part, ag_ss.at[n, d, h], ag_rs.at[n, d, h])
            send(part, part, sib_ss.at[n, d, h], sib_rs.at[n, d, h], ten_dev(x * 2 + other))
            if then is not None:
                then(src // 2, c)

    def gather_matmul(n, h, buf, weights, own_seen=False):
        acc = None
        for d in (0, 1, 3, 2):
            rank = lax.rem(x + 4 - d, 4) * 2 + c
            term = mm(weights[rank], buf[h, rank])
            acc = term if acc is None else acc + term
        for d in (0, 1, 3, 2):
            rank = lax.rem(x + 4 - d, 4) * 2 + other
            if d or not own_seen:
                wait_recv(buf.at[h, rank], sib_ss.at[n, d, h], sib_rs.at[n, d, h])
            acc = acc + mm(weights[rank], buf[h, rank])
        return acc

    def scatter_start(n, h, part_of, p, sb):
        for d in (2, 1, 3, 0):
            p[h, d] = part_of(chips[d] * 2 + other).astype(BF16)
            send(p.at[h, d], sb.at[h, d], rsib_ss.at[n, h, d], rsib_rs.at[n, h, d], ten_dev(x * 2 + other))
        for d in (2, 1, 3, 0):
            own[h, d] = part_of(chips[d] * 2 + c)

    def scatter_mid(n, h, sb, q, t):
        for d in (2, 1, 3):
            wait_recv(sb.at[h, d], rsib_ss.at[n, h, d], rsib_rs.at[n, h, d])
            q[h, d] = (own[h, d] + sb[h, d].astype(F32)).astype(BF16)
            send(q.at[h, d], t.at[h, d], rs_ss.at[n, h, d], rs_rs.at[n, h, d], ten_dev(chips[d] * 2 + c))

    def scatter_end(n, h, sb, t):
        wait_recv(sb.at[h, 0], rsib_ss.at[n, h, 0], rsib_rs.at[n, h, 0])
        total = own[h, 0] + sb[h, 0].astype(F32)
        for d in (1, 3, 2):
            wait_recv(t.at[h, d], rs_ss.at[n, h, d], rs_rs.at[n, h, d])
            total = total + t[h, d].astype(F32)
        return total

    def rows_of(ref, r):
        return ref[pl.ds(pl.multiple_of(r * CH, CH), CH), :]

    inv = [None, None]

    def forward(h):
        pre = gather_matmul(0, h, r1, wguT)
        inv[h] = lax.rsqrt(sum_rows(0, h, v1) / D + EPS)
        gate_pre = pre[0:HID] * inv[h]
        up_pre = pre[HID : 2 * HID] * inv[h]
        sig = jax.nn.sigmoid(gate_pre)
        hid_s[h] = (gate_pre * sig * up_pre).astype(BF16)
        gate_s[h] = gate_pre
        up_s[h] = up_pre
        scatter_start(0, h, lambda r: mm(rows_of(wd, r), hid_s[h]), p1, sb1)

    def cotangent(h):
        summed = res_s[h] + scatter_end(0, h, sb1, t1)
        r2[h, tn] = (summed - tgt_ref[:, halves[h]].astype(F32)).astype(BF16)
        gather_start(1, h, r2)
        out_ref[:, halves[h]] = summed.astype(BF16)

    def backward(h):
        d_hidden = gather_matmul(1, h, r2, wdT, own_seen=True)
        gate_pre = gate_s[h]
        up_pre = up_s[h]
        sig = jax.nn.sigmoid(gate_pre)
        d_gate = (d_hidden * up_pre * sig * (1.0 + gate_pre * (1.0 - sig))).astype(BF16)
        d_up = (d_hidden * gate_pre * sig).astype(BF16)
        inner = d_gate.astype(F32) * gate_pre + d_up.astype(F32) * up_pre
        share_row(1, h, v2, jnp.sum(inner, axis=0, keepdims=True))
        scatter_start(1, h, lambda r: mm(rows_of(wg, r), d_gate) + mm(rows_of(wu, r), d_up), p2, sb2)

    def d_residual(h):
        d_normed = scatter_end(1, h, sb2, t2)
        corr = sum_rows(1, h, v2) / D
        d_res = r2[h, tn].astype(F32) + inv[h] * (gain * d_normed - res_s[h] * inv[h] * corr)
        dres_s[:, halves[h]] = d_res.astype(BF16)
        d_tok = mm(eye_h[0:HT, 0:HT], d_res.astype(BF16), 1, 1)
        a3s[h * 8 : h * 8 + 8] = d_tok.astype(BF16).reshape(8, POS, CH)
        all_to_all_send_half(2, a3s, a3r, h)

    sign = 1 - 2 * c

    def grad_rank(chip, yhi):
        cots = jnp.concatenate([r2[h, chip * 2 + yhi] for h in range(2)], axis=1)
        hids = jnp.concatenate([hid_s[h] for h in range(2)], axis=1)
        g = mm(cots, hids, 1, 1)
        first, second, third = (g[:, n * LANES : (n + 1) * LANES] for n in range(3))
        at = pl.multiple_of(chip * 48, 16)
        for m in range(4):
            ya[yhi * 4 + m, pl.ds(at, 48), :] = first[m * 48 : m * 48 + 48].astype(BF16)
        zat = pl.multiple_of(yhi * 96, 16)
        for half in range(2):
            pieces = [second[m * 48 + half * ROWS : m * 48 + half * ROWS + ROWS] for m in range(4)]
            zb[half * 4 + chip, pl.ds(zat, 96), :] = jnp.concatenate(pieces, axis=0).astype(BF16)

        @pl.when(chip < 2)
        def _():
            for m in range(4):
                ya[yhi * 4 + m, pl.ds(CH + at, 48), :] = third[m * 48 : m * 48 + 48].astype(BF16)

        @pl.when(chip >= 2)
        def _():
            for half in range(2):
                pieces = [third[m * 48 + half * ROWS : m * 48 + half * ROWS + ROWS] for m in range(4)]
                zb[half * 4 + chip, pl.ds(CH + zat, 96), :] = jnp.concatenate(pieces, axis=0).astype(BF16)

    def away(me, k):
        return lax.rem(me + sign * k + 8, 8)

    def sized(axis, target, work):
        if axis == 0:
            work(CH + 96)
            return

        @pl.when(lax.rem(target, 4) < 2)
        def _():
            work(CH)

        @pl.when(lax.rem(target, 4) >= 2)
        def _():
            work(2 * CH)

    AXES = ((ya, yr, y, y_dev), (zb, zr, z, z_dev))

    def grad_copy(axis, slot, to, target, rows):
        src, dst, me, dev = AXES[axis]
        return pltpu.make_async_remote_copy(
            src_ref=src.at[target, pl.ds(0, rows)], dst_ref=dst.at[slot, pl.ds(0, rows)],
            send_sem=g_ss.at[axis, slot], recv_sem=g_rs.at[axis, slot],
            device_id=dev(away(me, to)), device_id_type=MESH,
        )

    STEP1 = ((0, 2, 4), (1, 1, 3), (2, -1, -3))
    STEP2 = ((3, 1, 1), (4, -1, -1))
    STEP3 = ((5, 2, 2), (6, -2, -2))

    def grad_step(axis, sends):
        me = AXES[axis][2]
        for slot, to, place in sends:
            target = away(me, place)
            sized(axis, target, lambda rows: grad_copy(axis, slot, to, target, rows).start())

            def done(slot=slot, to=to, target=target):
                sized(axis, target, lambda rows: grad_copy(axis, slot, to, target, rows).wait_send())

            pending.append(done)

    def grad_add(axis, target, slots):
        buf, got, me, dev = AXES[axis]

        def work(rows):
            total = buf[target, 0:rows, :].astype(F32)
            for slot in slots:
                part = got.at[slot, pl.ds(0, rows)]
                wait_recv(part, g_ss.at[axis, slot], g_rs.at[axis, slot])
                total = total + part[...].astype(F32)
            buf[target, 0:rows, :] = total.astype(BF16)

        sized(axis, target, work)

    def grad_first():
        for axis in range(2):
            grad_step(axis, STEP1)

    def grad_middle():
        for axis in range(2):
            grad_step(axis, STEP2)
        for axis in range(2):
            me = AXES[axis][2]
            grad_add(axis, away(me, 2), (0, 1))
            grad_add(axis, away(me, -2), (2,))
            grad_step(axis, STEP3)

    def grad_second():
        total = ya[y].astype(F32)
        for slot in (3, 4, 6, 5):
            wait_recv(yr.at[slot], g_ss.at[0, slot], g_rs.at[0, slot])
            total = total + yr[slot].astype(F32)
        for zl in range(4):
            for half in range(2):
                at = zl * 48 + half * ROWS
                pieces = [total[at : at + ROWS]]
                if zl < 2:
                    pieces.append(total[CH + at : CH + at + ROWS])
                else:
                    pieces.append(jnp.zeros((ROWS, LANES), F32))
                y2s[half * 4 + zl] = jnp.concatenate(pieces, axis=0).astype(BF16)
        second_send(0, y2s, y2r, z, z_dev)

        def sum_z(rows):
            total = zb[z, 0:rows, :].astype(F32)
            for slot in (3, 4, 6, 5):
                part = zr.at[slot, pl.ds(0, rows)]
                wait_recv(part, g_ss.at[1, slot], g_rs.at[1, slot])
                total = total + part[...].astype(F32)
            for yy in range(8):
                pieces = [total[yy * ROWS : yy * ROWS + ROWS]]
                if rows > CH:
                    pieces.append(total[CH + yy * ROWS : CH + yy * ROWS + ROWS])
                else:
                    pieces.append(jnp.zeros((ROWS, LANES), F32))
                z2s[yy] = jnp.concatenate(pieces, axis=0).astype(BF16)

        sized(1, z, sum_z)
        second_send(1, z2s, z2r, y, y_dev)

    def second_send(n, src, dst, me, dev):
        for i in FAR_FIRST:
            peer = lax.rem(me + i, 8)
            pltpu.make_async_remote_copy(
                src_ref=src.at[peer], dst_ref=dst.at[me],
                send_sem=g2_ss.at[n, peer], recv_sem=g2_rs.at[n, me],
                device_id=dev(peer), device_id_type=MESH,
            ).start()
        pending.append(functools.partial(second_done, n, src, me, dev))

    def second_done(n, src, me, dev):
        def one(i, carry):
            peer = lax.rem(me + i, 8)
            pltpu.make_async_remote_copy(
                src_ref=src.at[peer], dst_ref=src.at[peer],
                send_sem=g2_ss.at[n, peer], recv_sem=g2_rs.at[n, peer],
                device_id=dev(peer), device_id_type=MESH,
            ).wait_send()
            return carry

        lax.fori_loop(1, 8, one, 0)

    def second_sum(n, src, dst, me):
        total = src[me].astype(F32)
        for i in (7, 1, 6, 2, 5, 3, 4):
            peer = lax.rem(me + i, 8)
            wait_recv(dst.at[peer], g2_ss.at[n, peer], g2_rs.at[n, peer])
            total = total + dst[peer].astype(F32)
        return total

    residual(0)
    residual(1)
    gather_forward(0, 0, r1)
    forward(0)
    gather_forward(0, 1, r1)
    scatter_mid(0, 0, sb1, q1, t1)
    forward(1)
    scatter_mid(0, 1, sb1, q1, t1)
    cotangent(0)
    cotangent(1)
    store(0, out_ref, out_hbm)
    grad_rank(x, c)
    for h in range(2):
        wait_recv(r2.at[h, x * 2 + other], sib_ss.at[1, 0, h], sib_rs.at[1, 0, h])
    grad_rank(x, other)
    gather_forward(1, 0, r2)
    backward(0)
    gather_forward(1, 1, r2)
    scatter_mid(1, 0, sb2, q2, t2)
    backward(1)
    for d in (1, 3, 2):
        grad_rank(chips[d], c)
    scatter_mid(1, 1, sb2, q2, t2)
    for d in (1, 3, 2):
        grad_rank(chips[d], other)
    earlier = list(pending)
    pending.clear()
    grad_first()
    d_residual(0)
    d_residual(1)
    grad_middle()
    for wait in earlier:
        wait()

    all_to_all_wait(2, a3s, a3r)
    weighted = (a3r[...].reshape(TOK, CH).astype(F32) * tout).astype(BF16)
    a4s[...] = mm(kronT[...], weighted).astype(BF16).reshape(NSEQ, POS, CH)
    all_to_all_send(3, a4s, a4r)
    grad_second()
    drain()

    all_to_all_wait(3, a4s, a4r)
    scaled = (a4r[...].reshape(TOK, CH).astype(F32) * tin).astype(BF16)
    d_mix = mm(scaled, bm_ref[...], 0, 1)
    din_ref[...] = (dres_s[...].astype(F32) + d_mix).astype(BF16)

    store(1, din_ref, din_hbm)

    rows_y = second_sum(0, y2s, y2r, z)
    rows_z = second_sum(1, z2s, z2r, y)
    gd_ref[:, 0:LANES] = rows_y[0:ROWS]
    gd_ref[:, LANES : 2 * LANES] = rows_z[0:ROWS]
    gd_ref[:, 2 * LANES : HID] = rows_y[ROWS:48] + rows_z[ROWS:48]
    store(2, gd_ref, gd_hbm)

    drain()


def finish(*refs):
    came, gone, held, sems = refs[0:3], refs[3:6], refs[6:9], refs[9]
    reads = [pltpu.make_async_copy(came[n], held[n], sems.at[0, n]) for n in range(3)]
    writes = [pltpu.make_async_copy(held[n], gone[n], sems.at[1, n]) for n in range(3)]
    for cp in reads:
        cp.start()
    for n in range(3):
        reads[n].wait()
        writes[n].start()
    for cp in writes:
        cp.wait()


def body(
    inputs, targets, block_mix, cross_mix, twiddle_in, twiddle_out, norm_gain, w_gate, w_up, w_down
):
    hbm = pl.BlockSpec(memory_space=pltpu.HBM)
    dma = pltpu.SemaphoreType.DMA
    chunks = pltpu.VMEM((NSEQ, POS, CH), BF16)
    blocks4 = pltpu.VMEM((2, 4, CH, HT), BF16)
    results = (
        jax.ShapeDtypeStruct((CH, TOK), BF16),
        jax.ShapeDtypeStruct((CH, TOK), BF16),
        jax.ShapeDtypeStruct((ROWS, HID), F32),
    )
    made = pl.pallas_call(
        kernel,
        out_shape=results,
        in_specs=[hbm] * 10,
        out_specs=(hbm, hbm, hbm),
        scratch_shapes=[
            pltpu.VMEM((CH, TOK), BF16),
            pltpu.VMEM((CH, TOK), BF16),
            pltpu.VMEM((ROWS, HID), F32),
            pltpu.VMEM((CH, TOK), BF16),
            pltpu.VMEM((CH, TOK), BF16),
            pltpu.VMEM((TOK, TOK), BF16),
            pltpu.VMEM((NSEQ, NSEQ), BF16),
            pltpu.VMEM((1, TOK), F32),
            pltpu.VMEM((NSEQ, POS), F32),
            pltpu.VMEM((D // 128, 128), F32),
            pltpu.VMEM((D, HID), BF16),
            pltpu.VMEM((D, HID), BF16),
            pltpu.VMEM((D, HID), BF16),
            pltpu.VMEM((NTEN, 2 * HID, CH), BF16),
            pltpu.VMEM((NTEN, HID, CH), BF16),
            pltpu.VMEM((NSEQ * LINE, TOK), BF16),
            pltpu.VMEM((TOK, TOK), BF16),
        ]
        + [pltpu.VMEM((8, LINE, CH), BF16)] * 2
        + [pltpu.VMEM((NSEQ, PACKED, LANES), BF16)] * 2
        + [chunks] * 4
        + [
            pltpu.VMEM((2, NTEN, CH, HT), BF16),
            pltpu.VMEM((2, NTEN, CH, HT), BF16),
            pltpu.VMEM((2, NTEN, 8, HT), F32),
            pltpu.VMEM((2, NTEN, 8, HT), F32),
        ]
        + [blocks4] * 8
        + [
            pltpu.VMEM((2, 4, CH, HT), F32),
            pltpu.VMEM((2, HID, HT), F32),
            pltpu.VMEM((2, HID, HT), F32),
            pltpu.VMEM((2, HID, HT), BF16),
            pltpu.VMEM((2, CH, HT), F32),
            pltpu.VMEM((CH, TOK), BF16),
            pltpu.VMEM((8, CH + 96, LANES), BF16),
            pltpu.VMEM((7, CH + 96, LANES), BF16),
            pltpu.VMEM((8, 2 * CH, LANES), BF16),
            pltpu.VMEM((7, 2 * CH, LANES), BF16),
            pltpu.VMEM((8, 48, LANES), BF16),
            pltpu.VMEM((8, 48, LANES), BF16),
            pltpu.VMEM((8, 48, LANES), BF16),
            pltpu.VMEM((8, 48, LANES), BF16),
            pltpu.VMEM((2, NSEQ, POS), F32),
            pltpu.SemaphoreType.REGULAR,
            dma((2,)),
            dma((3,)),
            dma((10,)),
            dma((4, NSEQ)),
            dma((4, NSEQ)),
            dma((2, 4, 2)),
            dma((2, 4, 2)),
            dma((2, 4, 2)),
            dma((2, 4, 2)),
            dma((2, 2, NTEN)),
            dma((2, 2, NTEN)),
            dma((2, 2, 4)),
            dma((2, 2, 4)),
            dma((2, 2, 4)),
            dma((2, 2, 4)),
            dma((2, 7)),
            dma((2, 7)),
            dma((2, 8)),
            dma((2, 8)),
        ],
        compiler_params=pltpu.CompilerParams(
            collective_id=0, has_side_effects=True, vmem_limit_bytes=64 * 1024 * 1024
        ),
        name="monarch_block",
    )(
        inputs[0].T,
        targets[0].T,
        block_mix,
        cross_mix,
        twiddle_in,
        twiddle_out,
        norm_gain.reshape(D // 128, 128),
        w_gate,
        w_up,
        w_down,
    )
    output, d_input, grad_down = pl.pallas_call(
        finish,
        out_shape=results,
        in_specs=[hbm] * 3,
        out_specs=(hbm, hbm, hbm),
        scratch_shapes=[
            pltpu.VMEM((CH, TOK), BF16),
            pltpu.VMEM((CH, TOK), BF16),
            pltpu.VMEM((ROWS, HID), F32),
            dma((2, 3)),
        ],
        compiler_params=pltpu.CompilerParams(vmem_limit_bytes=64 * 1024 * 1024),
        name="hand_over",
    )(*made)
    return output.T[None], d_input.T[None], grad_down


def solution(mesh):
    return jax.shard_map(
        body,
        mesh=mesh,
        in_specs=(
            P("dp", "seq", "tensor"),
            P("dp", "seq", "tensor"),
            P(),
            P(),
            P("seq", None),
            P(None, "seq"),
            P(),
            P(None, "tensor"),
            P(None, "tensor"),
            P(None, "tensor"),
        ),
        out_specs=(P("dp", "seq", "tensor"), P("dp", "seq", "tensor"), P(("dp", "seq"), "tensor")),
        check_vma=False,
    )
```

```python
import functools

import jax
import jax.numpy as jnp
from jax import lax
from jax.experimental import pallas as pl
from jax.experimental.pallas import tpu as pltpu
from jax.sharding import PartitionSpec as P

F32 = jnp.float32
BF16 = jnp.bfloat16
MESH = pl.DeviceIdType.MESH

TOK = 256
HT = TOK // 2
CH = 192
HID = 384
NSEQ = 16
NTEN = 8
POS = 16
PACKED = 48
LINE = 32
FAR_FIRST = (4, 3, 5, 2, 6, 1, 7)
D = 1536
LANES = 128
ROWS = 24
EPS = 1e-05


def mm(a, b, ca=1, cb=0):
    return lax.dot_general(a, b, (((ca,), (cb,)), ((), ())), preferred_element_type=F32)


def eye(n, dtype=BF16):
    rows = lax.broadcasted_iota(jnp.int32, (n, n), 0)
    cols = lax.broadcasted_iota(jnp.int32, (n, n), 1)
    return jnp.where(rows == cols, 1.0, 0.0).astype(dtype)


def column_of(row):
    n = row.shape[1]
    return jnp.sum(eye(n, F32) * row, axis=1, keepdims=True)


def kernel(
    x_hbm, tgt_hbm, bm_hbm, cm_hbm, ti_hbm, to_hbm, gain_hbm, wg_hbm, wu_hbm, wd_hbm,
    out_hbm, din_hbm, gd_hbm,
    out_ref, din_ref, gd_ref, x_ref, tgt_ref, bm_ref, cm_ref, ti_ref, to_ref, gain_ref,
    wg, wu, wd, wguT, wdT, kron, kronT,
    a1s, a1r, a2s, a2r, a3s, a3r, a4s, a4r,
    r1, r2, v1, v2,
    p1, p2, sb1, sb2, q1, q2, t1, t2, own, pre_s, back_s, gate_s, up_s, hid_s, res_s, dres_s,
    ya, yr, zb, zr, y2s, y2r, z2s, z2r,
    to_pair, cross_sem, tw_sem, osem, wsem, a_ss, a_rs, ag_ss, ag_rs, sib_ss, sib_rs, v_ss, v_rs,
    rsib_ss, rsib_rs, rs_ss, rs_rs, g_ss, g_rs, g2_ss, g2_rs,
):
    dp = lax.axis_index("dp")
    sq = lax.axis_index("seq")
    tn = lax.axis_index("tensor")
    x, c = tn // 2, tn % 2
    y, zh = sq // 2, sq % 2
    z = zh * 4 + dp

    def seq_dev(s):
        return (dp, s, tn)

    def ten_dev(t):
        return (dp, sq, t)

    def y_dev(yy):
        return (dp, yy * 2 + zh, tn)

    def z_dev(zz):
        return (lax.rem(zz, 4), y * 2 + zz // 4, tn)

    pending = []

    def drain():
        while pending:
            pending.pop(0)()


    def send(src, dst, ss, rs, dev):
        cp = pltpu.make_async_remote_copy(
            src_ref=src, dst_ref=dst, send_sem=ss, recv_sem=rs, device_id=dev, device_id_type=MESH
        )
        cp.start()
        pending.append(cp.wait_send)

    def wait_recv(buf, ss, rs):
        pltpu.make_async_remote_copy(
            src_ref=buf, dst_ref=buf, send_sem=ss, recv_sem=rs,
            device_id=(dp, sq, tn), device_id_type=MESH,
        ).wait_recv()

    loads = []
    for n, (src, dst) in enumerate(
        (
            (x_hbm, x_ref), (bm_hbm, bm_ref), (ti_hbm, ti_ref), (cm_hbm, cm_ref), (to_hbm, to_ref),
            (gain_hbm, gain_ref), (wg_hbm, wg), (wu_hbm, wu), (wd_hbm, wd), (tgt_hbm, tgt_ref),
        )
    ):
        cp = pltpu.make_async_copy(src, dst, wsem.at[n])
        loads.append(cp)
    for cp in loads[0:3]:
        cp.start()

    barrier = pltpu.get_barrier_semaphore()

    def greet(dev):
        pl.semaphore_signal(barrier, inc=1, device_id=dev, device_id_type=MESH)

    for i in FAR_FIRST:
        greet(y_dev(lax.rem(y + i, 8)))
        greet(z_dev(lax.rem(z + i, 8)))
    for i in (4, 5, 3, 6, 2, 7, 1):
        greet(ten_dev(lax.rem(tn + i, NTEN)))
    for cp in loads[3:]:
        cp.start()

    def store(n, src, dst):
        cp = pltpu.make_async_copy(src, dst, osem.at[n])
        cp.start()
        pending.append(cp.wait)

    def a2a_copy(n, src, dst, peer):
        return pltpu.make_async_remote_copy(
            src_ref=src.at[peer], dst_ref=dst.at[sq],
            send_sem=a_ss.at[n, peer], recv_sem=a_rs.at[n, sq],
            device_id=seq_dev(peer), device_id_type=MESH,
        )

    def all_to_all_send(n, src, dst):
        for i in FAR_FIRST + (0,):
            yy = lax.rem(y + i, 8)
            a2a_copy(n, src, dst, yy * 2 + 1 - zh).start()
            if i:
                a2a_copy(n, src, dst, yy * 2 + zh).start()
        dst[sq] = src[sq]
        pending.append(functools.partial(all_to_all_done, n, src, dst))

    def all_to_all_send_half(n, src, dst, h):
        for i in (2, 1, 3, 0):
            yy = h * 4 + lax.rem(y + i, 4)
            a2a_copy(n, src, dst, yy * 2 + 1 - zh).start()

            @pl.when(yy != y)
            def _():
                a2a_copy(n, src, dst, yy * 2 + zh).start()

        if h:
            dst[sq] = src[sq]
            pending.append(functools.partial(all_to_all_done, n, src, dst))

    def all_to_all_wait(n, src, dst):
        for i in (0, 7, 1, 6, 2, 5, 3, 4):
            for other_line in range(2):
                if i or other_line:
                    peer = lax.rem(y + i, 8) * 2 + (1 - zh if other_line else zh)
                    wait_recv(dst.at[peer], a_ss.at[n, peer], a_rs.at[n, peer])

    def all_to_all_wait_half(n, src, dst, h):
        for i in (0, 3, 1, 2):
            yy = h * 4 + lax.rem(y + i, 4)

            @pl.when(yy != y)
            def _():
                peer = yy * 2 + zh
                wait_recv(dst.at[peer], a_ss.at[n, peer], a_rs.at[n, peer])

            peer = yy * 2 + 1 - zh
            wait_recv(dst.at[peer], a_ss.at[n, peer], a_rs.at[n, peer])

    def all_to_all_done(n, src, dst):
        def one(i, carry):
            a2a_copy(n, src, dst, lax.rem(sq + i, NSEQ)).wait_send()
            return carry

        lax.fori_loop(1, NSEQ, one, 0)

    def line_copy(peer):
        return pltpu.make_async_remote_copy(
            src_ref=a1s.at[peer], dst_ref=a1r.at[y],
            send_sem=a_ss.at[0, peer], recv_sem=a_rs.at[0, y],
            device_id=y_dev(peer), device_id_type=MESH,
        )

    def line_done():
        for i in FAR_FIRST:
            line_copy(lax.rem(y + i, 8)).wait_send()

    for cp in loads[0:3]:
        cp.wait()
    tin = column_of(ti_ref[...])
    section = mm(bm_ref[...], x_ref[...], 0, 1) * tin
    a1s[...] = section.astype(BF16).reshape(8, LINE, CH)

    rows = lax.broadcasted_iota(jnp.int32, (TOK, NSEQ), 0)
    cols = lax.broadcasted_iota(jnp.int32, (TOK, NSEQ), 1)
    for cp in loads[3:6]:
        cp.wait()
    cross = cm_ref[...]

    def iota(shape, dim):
        return lax.broadcasted_iota(jnp.int32, shape, dim)

    def flags(hit):
        return jnp.where(hit, 1.0, 0.0).astype(BF16)

    rows_here = flags(iota((8, NSEQ), 1) == 2 * iota((8, NSEQ), 0) + zh)
    cross_here = mm(rows_here, cross).astype(BF16)
    wide = mm(flags(iota((NSEQ * LINE, NSEQ), 0) // LINE == iota((NSEQ * LINE, NSEQ), 1)), cross_here, 1, 1)
    wide = mm(wide.astype(BF16), flags(iota((8, TOK), 1) // LINE == iota((8, TOK), 0)))
    same_pos = iota((NSEQ * LINE, TOK), 0) % LINE == iota((NSEQ * LINE, TOK), 1) % LINE
    kron[...] = jnp.where(same_pos, wide, 0.0).astype(BF16)
    pick_block = flags(rows // POS == cols)
    pick_pos = jnp.where(rows % POS == cols, 1.0, 0.0)
    wide = mm(mm(pick_block, cross).astype(BF16), pick_block, 1, 1)
    same_pos = iota((TOK, TOK), 0) % POS == iota((TOK, TOK), 1) % POS
    kronT[...] = jnp.where(same_pos, wide, 0.0).astype(BF16)
    tout_all = jnp.broadcast_to(to_ref[...][:, None, :], (NSEQ, POS, POS)).reshape(TOK, POS)
    tout = jnp.sum(tout_all * pick_pos, axis=1, keepdims=True)
    flat = tn * CH + lax.broadcasted_iota(jnp.int32, (CH, 128), 0)
    lane = lax.broadcasted_iota(jnp.int32, (CH, 128), 1)
    gain = jnp.zeros((CH, 128), F32)
    for k in range(D // 128):
        gain = gain + jnp.where(flat == k * 128 + lane, gain_ref[k : k + 1, :], 0.0)
    gain = jnp.sum(gain, axis=1, keepdims=True)

    pl.semaphore_wait(barrier, 7 + 7 + (NTEN - 1))
    partner = (dp, y * 2 + 1 - zh, tn)
    for i in FAR_FIRST:
        line_copy(lax.rem(y + i, 8)).start()
    pending.append(line_done)
    a1r[y] = a1s[y]
    pl.semaphore_signal(cross_sem, inc=1, device_id=partner, device_id_type=MESH)
    to_pair[zh] = to_ref[...]
    send(to_pair.at[zh], to_pair.at[zh], tw_sem.at[0], tw_sem.at[1], partner)

    for cp in loads[6:]:
        cp.wait()
    eye_h = eye(HID)
    for r in range(NTEN):
        block = slice(r * CH, (r + 1) * CH)
        wguT[r, 0:HID, :] = mm(eye_h, wg[block, :], 1, 1).astype(BF16)
        wguT[r, HID : 2 * HID, :] = mm(eye_h, wu[block, :], 1, 1).astype(BF16)
        wdT[r] = mm(eye_h, wd[block, :], 1, 1).astype(BF16)
    eye_c = eye(CH)

    wait_recv(to_pair.at[1 - zh], tw_sem.at[0], tw_sem.at[1])
    tline = jnp.zeros((NSEQ * LINE, 1), F32)
    for half in range(2):
        spread = jnp.broadcast_to(to_pair[half][:, None, :], (NSEQ, LINE, POS)).reshape(NSEQ * LINE, POS)
        here = iota((NSEQ * LINE, POS), 0) % LINE == half * POS + iota((NSEQ * LINE, POS), 1)
        tline = tline + jnp.sum(jnp.where(here, spread, 0.0), axis=1, keepdims=True)
    pl.semaphore_wait(cross_sem, 1)
    for i in FAR_FIRST:
        peer = lax.rem(y + i, 8)
        wait_recv(a1r.at[peer], a_ss.at[0, peer], a_rs.at[0, peer])

    mixed = mm(kron[...], a1r[...].reshape(TOK, CH)) * tline
    mixed = mixed.reshape(NSEQ, LINE, CH)
    a2s[:, 0:LINE, :] = mixed[:, :, 0:LANES].astype(BF16)
    rest = mixed[:, :, LANES:CH]
    rest = jnp.concatenate([rest[:, 0:POS], rest[:, POS:LINE]], axis=2)
    a2s[:, LINE:PACKED, :] = rest.astype(BF16)
    all_to_all_send(1, a2s, a2r)

    halves = [slice(0, HT), slice(HT, TOK)]

    def residual(h):
        all_to_all_wait_half(1, a2s, a2r, h)
        terms = a2r[h * 8 : h * 8 + 8].astype(F32).reshape(4, 2, PACKED, LANES)
        terms = terms[:, 0] + terms[:, 1]
        rest = terms[:, LINE:PACKED]
        rest = jnp.concatenate([rest[:, :, 0 : CH - LANES], rest[:, :, CH - LANES : LANES]], axis=1)
        mixed = jnp.concatenate([terms[:, 0:LINE], rest], axis=2).astype(BF16).reshape(HT, CH)
        mixed = mm(eye_c, mixed, 1, 1)
        res = (x_ref[:, halves[h]].astype(F32) + mixed).astype(BF16).astype(F32)
        res_s[h] = res
        r1[h, tn] = (res * gain).astype(BF16)
        gather_start(0, h, r1)
        share_row(0, h, v1, jnp.sum(res * res, axis=0, keepdims=True))

    def share_row(n, h, buf, row):
        buf[h, tn] = jnp.broadcast_to(row, (8, HT))

        for i in (4, 5, 3, 6, 2, 7, 1):
            peer = lax.rem(tn + i, NTEN)
            pltpu.make_async_remote_copy(
                src_ref=buf.at[h, tn], dst_ref=buf.at[h, tn],
                send_sem=v_ss.at[n, h, peer], recv_sem=v_rs.at[n, h, tn],
                device_id=ten_dev(peer), device_id_type=MESH,
            ).start()
        pending.append(functools.partial(rows_done, n, h, buf))

    def sum_rows(n, h, buf):
        for i in range(1, NTEN):
            peer = lax.rem(tn + i, NTEN)
            wait_recv(buf.at[h, peer], v_ss.at[n, h, peer], v_rs.at[n, h, peer])
        return jnp.sum(buf[h, :, 0:1, :], axis=0)

    def rows_done(n, h, buf):
        def one(i, carry):
            peer = lax.rem(tn + i, NTEN)
            pltpu.make_async_remote_copy(
                src_ref=buf.at[h, tn], dst_ref=buf.at[h, tn],
                send_sem=v_ss.at[n, h, peer], recv_sem=v_rs.at[n, h, peer],
                device_id=ten_dev(peer), device_id_type=MESH,
            ).wait_send()
            return carry

        lax.fori_loop(1, NTEN, one, 0)

    chips = [lax.rem(x + d, 4) for d in range(4)]
    other = 1 - c

    def gather_start(n, h, buf):
        part = buf.at[h, tn]
        for d in (2, 1, 3):
            send(part, part, ag_ss.at[n, d, h], ag_rs.at[n, d, h], ten_dev(chips[d] * 2 + c))
        send(part, part, sib_ss.at[n, 0, h], sib_rs.at[n, 0, h], ten_dev(x * 2 + other))

    def gather_forward(n, h, buf, then=None):
        for d in (1, 3, 2):
            src = lax.rem(x + 4 - d, 4) * 2 + c
            part = buf.at[h, src]
            wait_recv(part, ag_ss.at[n, d, h], ag_rs.at[n, d, h])
            send(part, part, sib_ss.at[n, d, h], sib_rs.at[n, d, h], ten_dev(x * 2 + other))
            if then is not None:
                then(src // 2, c)

    def gather_own(n, h, buf, weights, acc):
        rank = x * 2 + other
        first = mm(weights[tn], buf[h, tn])
        wait_recv(buf.at[h, rank], sib_ss.at[n, 0, h], sib_rs.at[n, 0, h])
        acc[h] = first + mm(weights[rank], buf[h, rank])

    def gather_matmul(n, h, buf, weights, acc):
        total = acc[h]
        for d in (1, 3, 2):
            rank = lax.rem(x + 4 - d, 4) * 2 + c
            total = total + mm(weights[rank], buf[h, rank])
        for d in (1, 3, 2):
            rank = lax.rem(x + 4 - d, 4) * 2 + other
            wait_recv(buf.at[h, rank], sib_ss.at[n, d, h], sib_rs.at[n, d, h])
            total = total + mm(weights[rank], buf[h, rank])
        return total

    def scatter_start(n, h, part_of, p, sb):
        for d in (2, 1, 3, 0):
            p[h, d] = part_of(chips[d] * 2 + other).astype(BF16)
            send(p.at[h, d], sb.at[h, d], rsib_ss.at[n, h, d], rsib_rs.at[n, h, d], ten_dev(x * 2 + other))
        for d in (2, 1, 3, 0):
            own[h, d] = part_of(chips[d] * 2 + c)

    def scatter_mid(n, h, sb, q, t):
        for d in (2, 1, 3):
            wait_recv(sb.at[h, d], rsib_ss.at[n, h, d], rsib_rs.at[n, h, d])
            q[h, d] = (own[h, d] + sb[h, d].astype(F32)).astype(BF16)
            send(q.at[h, d], t.at[h, d], rs_ss.at[n, h, d], rs_rs.at[n, h, d], ten_dev(chips[d] * 2 + c))

    def scatter_end(n, h, sb, t):
        wait_recv(sb.at[h, 0], rsib_ss.at[n, h, 0], rsib_rs.at[n, h, 0])
        total = own[h, 0] + sb[h, 0].astype(F32)
        for d in (1, 3, 2):
            wait_recv(t.at[h, d], rs_ss.at[n, h, d], rs_rs.at[n, h, d])
            total = total + t[h, d].astype(F32)
        return total

    def rows_of(ref, r):
        return ref[pl.ds(pl.multiple_of(r * CH, CH), CH), :]

    inv = [None, None]

    def forward(h):
        pre = gather_matmul(0, h, r1, wguT, pre_s)
        inv[h] = lax.rsqrt(sum_rows(0, h, v1) / D + EPS)
        gate_pre = pre[0:HID] * inv[h]
        up_pre = pre[HID : 2 * HID] * inv[h]
        sig = jax.nn.sigmoid(gate_pre)
        hid_s[h] = (gate_pre * sig * up_pre).astype(BF16)
        gate_s[h] = gate_pre
        up_s[h] = up_pre
        scatter_start(0, h, lambda r: mm(rows_of(wd, r), hid_s[h]), p1, sb1)

    def cotangent(h):
        summed = res_s[h] + scatter_end(0, h, sb1, t1)
        r2[h, tn] = (summed - tgt_ref[:, halves[h]].astype(F32)).astype(BF16)
        gather_start(1, h, r2)
        out_ref[:, halves[h]] = summed.astype(BF16)

    def backward(h):
        d_hidden = gather_matmul(1, h, r2, wdT, back_s)
        gate_pre = gate_s[h]
        up_pre = up_s[h]
        sig = jax.nn.sigmoid(gate_pre)
        d_gate = (d_hidden * up_pre * sig * (1.0 + gate_pre * (1.0 - sig))).astype(BF16)
        d_up = (d_hidden * gate_pre * sig).astype(BF16)
        inner = d_gate.astype(F32) * gate_pre + d_up.astype(F32) * up_pre
        share_row(1, h, v2, jnp.sum(inner, axis=0, keepdims=True))
        scatter_start(1, h, lambda r: mm(rows_of(wg, r), d_gate) + mm(rows_of(wu, r), d_up), p2, sb2)

    def d_residual(h):
        d_normed = scatter_end(1, h, sb2, t2)
        corr = sum_rows(1, h, v2) / D
        d_res = r2[h, tn].astype(F32) + inv[h] * (gain * d_normed - res_s[h] * inv[h] * corr)
        dres_s[:, halves[h]] = d_res.astype(BF16)
        d_tok = mm(eye_h[0:HT, 0:HT], d_res.astype(BF16), 1, 1)
        a3s[h * 8 : h * 8 + 8] = d_tok.astype(BF16).reshape(8, POS, CH)
        all_to_all_send_half(2, a3s, a3r, h)

    sign = 1 - 2 * c

    def grad_rank(chip, yhi):
        cots = jnp.concatenate([r2[h, chip * 2 + yhi] for h in range(2)], axis=1)
        hids = jnp.concatenate([hid_s[h] for h in range(2)], axis=1)
        g = mm(cots, hids, 1, 1)
        first, second, third = (g[:, n * LANES : (n + 1) * LANES] for n in range(3))
        at = pl.multiple_of(chip * 48, 16)
        for m in range(4):
            ya[yhi * 4 + m, pl.ds(at, 48), :] = first[m * 48 : m * 48 + 48].astype(BF16)
        zat = pl.multiple_of(yhi * 96, 16)
        for half in range(2):
            pieces = [second[m * 48 + half * ROWS : m * 48 + half * ROWS + ROWS] for m in range(4)]
            zb[half * 4 + chip, pl.ds(zat, 96), :] = jnp.concatenate(pieces, axis=0).astype(BF16)

        @pl.when(chip < 2)
        def _():
            for m in range(4):
                ya[yhi * 4 + m, pl.ds(CH + at, 48), :] = third[m * 48 : m * 48 + 48].astype(BF16)

        @pl.when(chip >= 2)
        def _():
            for half in range(2):
                pieces = [third[m * 48 + half * ROWS : m * 48 + half * ROWS + ROWS] for m in range(4)]
                zb[half * 4 + chip, pl.ds(CH + zat, 96), :] = jnp.concatenate(pieces, axis=0).astype(BF16)

    def away(me, k):
        return lax.rem(me + sign * k + 8, 8)

    def sized(axis, target, work):
        if axis == 0:
            work(CH + 96)
            return

        @pl.when(lax.rem(target, 4) < 2)
        def _():
            work(CH)

        @pl.when(lax.rem(target, 4) >= 2)
        def _():
            work(2 * CH)

    AXES = ((ya, yr, y, y_dev), (zb, zr, z, z_dev))

    def grad_copy(axis, slot, to, target, rows):
        src, dst, me, dev = AXES[axis]
        return pltpu.make_async_remote_copy(
            src_ref=src.at[target, pl.ds(0, rows)], dst_ref=dst.at[slot, pl.ds(0, rows)],
            send_sem=g_ss.at[axis, slot], recv_sem=g_rs.at[axis, slot],
            device_id=dev(away(me, to)), device_id_type=MESH,
        )

    STEP1 = ((0, 2, 4), (1, 1, 3), (2, -1, -3))
    STEP2 = ((3, 1, 1), (4, -1, -1))
    STEP3 = ((5, 2, 2), (6, -2, -2))

    def grad_step(axis, sends):
        me = AXES[axis][2]
        for slot, to, place in sends:
            target = away(me, place)
            sized(axis, target, lambda rows: grad_copy(axis, slot, to, target, rows).start())

            def done(slot=slot, to=to, target=target):
                sized(axis, target, lambda rows: grad_copy(axis, slot, to, target, rows).wait_send())

            pending.append(done)

    def grad_add(axis, target, slots):
        buf, got, me, dev = AXES[axis]

        def work(rows):
            total = buf[target, 0:rows, :].astype(F32)
            for slot in slots:
                part = got.at[slot, pl.ds(0, rows)]
                wait_recv(part, g_ss.at[axis, slot], g_rs.at[axis, slot])
                total = total + part[...].astype(F32)
            buf[target, 0:rows, :] = total.astype(BF16)

        sized(axis, target, work)

    def grad_first():
        for axis in range(2):
            grad_step(axis, STEP1)

    def grad_middle():
        for axis in range(2):
            grad_step(axis, STEP2)
        for axis in range(2):
            me = AXES[axis][2]
            grad_add(axis, away(me, 2), (0, 1))
            grad_add(axis, away(me, -2), (2,))
            grad_step(axis, STEP3)

    def grad_second():
        total = ya[y].astype(F32)
        for slot in (3, 4, 6, 5):
            wait_recv(yr.at[slot], g_ss.at[0, slot], g_rs.at[0, slot])
            total = total + yr[slot].astype(F32)
        for zl in range(4):
            for half in range(2):
                at = zl * 48 + half * ROWS
                pieces = [total[at : at + ROWS]]
                if zl < 2:
                    pieces.append(total[CH + at : CH + at + ROWS])
                else:
                    pieces.append(jnp.zeros((ROWS, LANES), F32))
                y2s[half * 4 + zl] = jnp.concatenate(pieces, axis=0).astype(BF16)
        second_send(0, y2s, y2r, z, z_dev)

        def sum_z(rows):
            total = zb[z, 0:rows, :].astype(F32)
            for slot in (3, 4, 6, 5):
                part = zr.at[slot, pl.ds(0, rows)]
                wait_recv(part, g_ss.at[1, slot], g_rs.at[1, slot])
                total = total + part[...].astype(F32)
            for yy in range(8):
                pieces = [total[yy * ROWS : yy * ROWS + ROWS]]
                if rows > CH:
                    pieces.append(total[CH + yy * ROWS : CH + yy * ROWS + ROWS])
                else:
                    pieces.append(jnp.zeros((ROWS, LANES), F32))
                z2s[yy] = jnp.concatenate(pieces, axis=0).astype(BF16)

        sized(1, z, sum_z)
        second_send(1, z2s, z2r, y, y_dev)

    def second_send(n, src, dst, me, dev):
        for i in FAR_FIRST:
            peer = lax.rem(me + i, 8)
            pltpu.make_async_remote_copy(
                src_ref=src.at[peer], dst_ref=dst.at[me],
                send_sem=g2_ss.at[n, peer], recv_sem=g2_rs.at[n, me],
                device_id=dev(peer), device_id_type=MESH,
            ).start()
        pending.append(functools.partial(second_done, n, src, me, dev))

    def second_done(n, src, me, dev):
        def one(i, carry):
            peer = lax.rem(me + i, 8)
            pltpu.make_async_remote_copy(
                src_ref=src.at[peer], dst_ref=src.at[peer],
                send_sem=g2_ss.at[n, peer], recv_sem=g2_rs.at[n, peer],
                device_id=dev(peer), device_id_type=MESH,
            ).wait_send()
            return carry

        lax.fori_loop(1, 8, one, 0)

    def second_sum(n, src, dst, me):
        total = src[me].astype(F32)
        for i in (7, 1, 6, 2, 5, 3, 4):
            peer = lax.rem(me + i, 8)
            wait_recv(dst.at[peer], g2_ss.at[n, peer], g2_rs.at[n, peer])
            total = total + dst[peer].astype(F32)
        return total

    residual(0)
    residual(1)
    gather_own(0, 0, r1, wguT, pre_s)
    gather_own(0, 1, r1, wguT, pre_s)
    gather_forward(0, 0, r1)
    forward(0)
    gather_forward(0, 1, r1)
    scatter_mid(0, 0, sb1, q1, t1)
    forward(1)
    scatter_mid(0, 1, sb1, q1, t1)
    cotangent(0)
    cotangent(1)
    store(0, out_ref, out_hbm)
    grad_rank(x, c)
    gather_own(1, 0, r2, wdT, back_s)
    gather_own(1, 1, r2, wdT, back_s)
    grad_rank(x, other)
    gather_forward(1, 0, r2)
    backward(0)
    gather_forward(1, 1, r2)
    scatter_mid(1, 0, sb2, q2, t2)
    backward(1)
    for d in (1, 3, 2):
        grad_rank(chips[d], c)
    scatter_mid(1, 1, sb2, q2, t2)
    for d in (1, 3, 2):
        grad_rank(chips[d], other)
    earlier = list(pending)
    pending.clear()
    grad_first()
    d_residual(0)
    d_residual(1)
    grad_middle()
    for wait in earlier:
        wait()

    all_to_all_wait(2, a3s, a3r)
    weighted = (a3r[...].reshape(TOK, CH).astype(F32) * tout).astype(BF16)
    a4s[...] = mm(kronT[...], weighted).astype(BF16).reshape(NSEQ, POS, CH)
    all_to_all_send(3, a4s, a4r)
    grad_second()
    drain()

    all_to_all_wait(3, a4s, a4r)
    scaled = (a4r[...].reshape(TOK, CH).astype(F32) * tin).astype(BF16)
    d_mix = mm(scaled, bm_ref[...], 0, 1)
    din_ref[...] = (dres_s[...].astype(F32) + d_mix).astype(BF16)

    store(1, din_ref, din_hbm)

    rows_y = second_sum(0, y2s, y2r, z)
    rows_z = second_sum(1, z2s, z2r, y)
    gd_ref[:, 0:LANES] = rows_y[0:ROWS]
    gd_ref[:, LANES : 2 * LANES] = rows_z[0:ROWS]
    gd_ref[:, 2 * LANES : HID] = rows_y[ROWS:48] + rows_z[ROWS:48]
    store(2, gd_ref, gd_hbm)

    drain()


def finish(*refs):
    came, gone, held, sems = refs[0:3], refs[3:6], refs[6:9], refs[9]
    reads = [pltpu.make_async_copy(came[n], held[n], sems.at[0, n]) for n in range(3)]
    writes = [pltpu.make_async_copy(held[n], gone[n], sems.at[1, n]) for n in range(3)]
    for cp in reads:
        cp.start()
    for n in range(3):
        reads[n].wait()
        writes[n].start()
    for cp in writes:
        cp.wait()


def body(
    inputs, targets, block_mix, cross_mix, twiddle_in, twiddle_out, norm_gain, w_gate, w_up, w_down
):
    hbm = pl.BlockSpec(memory_space=pltpu.HBM)
    dma = pltpu.SemaphoreType.DMA
    chunks = pltpu.VMEM((NSEQ, POS, CH), BF16)
    blocks4 = pltpu.VMEM((2, 4, CH, HT), BF16)
    results = (
        jax.ShapeDtypeStruct((CH, TOK), BF16),
        jax.ShapeDtypeStruct((CH, TOK), BF16),
        jax.ShapeDtypeStruct((ROWS, HID), F32),
    )
    made = pl.pallas_call(
        kernel,
        out_shape=results,
        in_specs=[hbm] * 10,
        out_specs=(hbm, hbm, hbm),
        scratch_shapes=[
            pltpu.VMEM((CH, TOK), BF16),
            pltpu.VMEM((CH, TOK), BF16),
            pltpu.VMEM((ROWS, HID), F32),
            pltpu.VMEM((CH, TOK), BF16),
            pltpu.VMEM((CH, TOK), BF16),
            pltpu.VMEM((TOK, TOK), BF16),
            pltpu.VMEM((NSEQ, NSEQ), BF16),
            pltpu.VMEM((1, TOK), F32),
            pltpu.VMEM((NSEQ, POS), F32),
            pltpu.VMEM((D // 128, 128), F32),
            pltpu.VMEM((D, HID), BF16),
            pltpu.VMEM((D, HID), BF16),
            pltpu.VMEM((D, HID), BF16),
            pltpu.VMEM((NTEN, 2 * HID, CH), BF16),
            pltpu.VMEM((NTEN, HID, CH), BF16),
            pltpu.VMEM((NSEQ * LINE, TOK), BF16),
            pltpu.VMEM((TOK, TOK), BF16),
        ]
        + [pltpu.VMEM((8, LINE, CH), BF16)] * 2
        + [pltpu.VMEM((NSEQ, PACKED, LANES), BF16)] * 2
        + [chunks] * 4
        + [
            pltpu.VMEM((2, NTEN, CH, HT), BF16),
            pltpu.VMEM((2, NTEN, CH, HT), BF16),
            pltpu.VMEM((2, NTEN, 8, HT), F32),
            pltpu.VMEM((2, NTEN, 8, HT), F32),
        ]
        + [blocks4] * 8
        + [
            pltpu.VMEM((2, 4, CH, HT), F32),
            pltpu.VMEM((2, 2 * HID, HT), F32),
            pltpu.VMEM((2, HID, HT), F32),
            pltpu.VMEM((2, HID, HT), F32),
            pltpu.VMEM((2, HID, HT), F32),
            pltpu.VMEM((2, HID, HT), BF16),
            pltpu.VMEM((2, CH, HT), F32),
            pltpu.VMEM((CH, TOK), BF16),
            pltpu.VMEM((8, CH + 96, LANES), BF16),
            pltpu.VMEM((7, CH + 96, LANES), BF16),
            pltpu.VMEM((8, 2 * CH, LANES), BF16),
            pltpu.VMEM((7, 2 * CH, LANES), BF16),
            pltpu.VMEM((8, 48, LANES), BF16),
            pltpu.VMEM((8, 48, LANES), BF16),
            pltpu.VMEM((8, 48, LANES), BF16),
            pltpu.VMEM((8, 48, LANES), BF16),
            pltpu.VMEM((2, NSEQ, POS), F32),
            pltpu.SemaphoreType.REGULAR,
            dma((2,)),
            dma((3,)),
            dma((10,)),
            dma((4, NSEQ)),
            dma((4, NSEQ)),
            dma((2, 4, 2)),
            dma((2, 4, 2)),
            dma((2, 4, 2)),
            dma((2, 4, 2)),
            dma((2, 2, NTEN)),
            dma((2, 2, NTEN)),
            dma((2, 2, 4)),
            dma((2, 2, 4)),
            dma((2, 2, 4)),
            dma((2, 2, 4)),
            dma((2, 7)),
            dma((2, 7)),
            dma((2, 8)),
            dma((2, 8)),
        ],
        compiler_params=pltpu.CompilerParams(
            collective_id=0, has_side_effects=True, vmem_limit_bytes=64 * 1024 * 1024
        ),
        name="monarch_block",
    )(
        inputs[0].T,
        targets[0].T,
        block_mix,
        cross_mix,
        twiddle_in,
        twiddle_out,
        norm_gain.reshape(D // 128, 128),
        w_gate,
        w_up,
        w_down,
    )
    output, d_input, grad_down = pl.pallas_call(
        finish,
        out_shape=results,
        in_specs=[hbm] * 3,
        out_specs=(hbm, hbm, hbm),
        scratch_shapes=[
            pltpu.VMEM((CH, TOK), BF16),
            pltpu.VMEM((CH, TOK), BF16),
            pltpu.VMEM((ROWS, HID), F32),
            dma((2, 3)),
        ],
        compiler_params=pltpu.CompilerParams(vmem_limit_bytes=64 * 1024 * 1024),
        name="hand_over",
    )(*made)
    return output.T[None], d_input.T[None], grad_down


def solution(mesh):
    return jax.shard_map(
        body,
        mesh=mesh,
        in_specs=(
            P("dp", "seq", "tensor"),
            P("dp", "seq", "tensor"),
            P(),
            P(),
            P("seq", None),
            P(None, "seq"),
            P(),
            P(None, "tensor"),
            P(None, "tensor"),
            P(None, "tensor"),
        ),
        out_specs=(P("dp", "seq", "tensor"), P("dp", "seq", "tensor"), P(("dp", "seq"), "tensor")),
        check_vma=False,
    )
```

```python
import functools

import jax
import jax.numpy as jnp
from jax import lax
from jax.experimental import pallas as pl
from jax.experimental.pallas import tpu as pltpu
from jax.sharding import PartitionSpec as P

F32 = jnp.float32
BF16 = jnp.bfloat16
MESH = pl.DeviceIdType.MESH

TOK = 256
HT = TOK // 2
CH = 192
HID = 384
NSEQ = 16
NTEN = 8
POS = 16
PACKED = 48
LINE = 32
FAR_FIRST = (4, 3, 5, 2, 6, 1, 7)
D = 1536
LANES = 128
ROWS = 24
EPS = 1e-05


def mm(a, b, ca=1, cb=0):
    return lax.dot_general(a, b, (((ca,), (cb,)), ((), ())), preferred_element_type=F32)


def eye(n, dtype=BF16):
    rows = lax.broadcasted_iota(jnp.int32, (n, n), 0)
    cols = lax.broadcasted_iota(jnp.int32, (n, n), 1)
    return jnp.where(rows == cols, 1.0, 0.0).astype(dtype)


def column_of(row):
    n = row.shape[1]
    return jnp.sum(eye(n, F32) * row, axis=1, keepdims=True)


def kernel(
    x_hbm, tgt_hbm, bm_hbm, cm_hbm, ti_hbm, to_hbm, gain_hbm, wg_hbm, wu_hbm, wd_hbm,
    out_hbm, din_hbm, gd_hbm,
    out_ref, din_ref, gd_ref, x_ref, tgt_ref, bm_ref, cm_ref, ti_ref, to_ref, gain_ref,
    wg, wu, wd, wguT, wdT, kron, kronT,
    a1s, a1r, a2s, a2r, a3s, a3r, a4s, a4r,
    r1, r2, v1, v2,
    p1, p2, sb1, sb2, q1, q2, t1, t2, own, pre_s, back_s, gate_s, up_s, hid_s, res_s, dres_s,
    ya, yr, zb, zr, y2s, y2r, z2s, z2r,
    to_pair, cross_sem, tw_sem, osem, wsem, a_ss, a_rs, ag_ss, ag_rs, sib_ss, sib_rs, v_ss, v_rs,
    rsib_ss, rsib_rs, rs_ss, rs_rs, g_ss, g_rs, g2_ss, g2_rs,
):
    dp = lax.axis_index("dp")
    sq = lax.axis_index("seq")
    tn = lax.axis_index("tensor")
    x, c = tn // 2, tn % 2
    y, zh = sq // 2, sq % 2
    z = zh * 4 + dp

    def seq_dev(s):
        return (dp, s, tn)

    def ten_dev(t):
        return (dp, sq, t)

    def y_dev(yy):
        return (dp, yy * 2 + zh, tn)

    def z_dev(zz):
        return (lax.rem(zz, 4), y * 2 + zz // 4, tn)

    pending = []

    def drain():
        while pending:
            pending.pop(0)()


    def send(src, dst, ss, rs, dev):
        cp = pltpu.make_async_remote_copy(
            src_ref=src, dst_ref=dst, send_sem=ss, recv_sem=rs, device_id=dev, device_id_type=MESH
        )
        cp.start()
        pending.append(cp.wait_send)

    def wait_recv(buf, ss, rs):
        pltpu.make_async_remote_copy(
            src_ref=buf, dst_ref=buf, send_sem=ss, recv_sem=rs,
            device_id=(dp, sq, tn), device_id_type=MESH,
        ).wait_recv()

    loads = []
    for n, (src, dst) in enumerate(
        (
            (x_hbm, x_ref), (bm_hbm, bm_ref), (ti_hbm, ti_ref), (cm_hbm, cm_ref), (to_hbm, to_ref),
            (gain_hbm, gain_ref), (wg_hbm, wg), (wu_hbm, wu), (wd_hbm, wd), (tgt_hbm, tgt_ref),
        )
    ):
        cp = pltpu.make_async_copy(src, dst, wsem.at[n])
        loads.append(cp)
    for cp in loads[0:3]:
        cp.start()

    barrier = pltpu.get_barrier_semaphore()

    def greet(dev):
        pl.semaphore_signal(barrier, inc=1, device_id=dev, device_id_type=MESH)

    for i in FAR_FIRST:
        greet(y_dev(lax.rem(y + i, 8)))
        greet(z_dev(lax.rem(z + i, 8)))
    for i in (4, 5, 3, 6, 2, 7, 1):
        greet(ten_dev(lax.rem(tn + i, NTEN)))
    for cp in loads[3:]:
        cp.start()

    def store(n, src, dst):
        cp = pltpu.make_async_copy(src, dst, osem.at[n])
        cp.start()
        pending.append(cp.wait)

    def a2a_copy(n, src, dst, peer):
        return pltpu.make_async_remote_copy(
            src_ref=src.at[peer], dst_ref=dst.at[sq],
            send_sem=a_ss.at[n, peer], recv_sem=a_rs.at[n, sq],
            device_id=seq_dev(peer), device_id_type=MESH,
        )

    def all_to_all_send(n, src, dst):
        for i in FAR_FIRST + (0,):
            yy = lax.rem(y + i, 8)
            a2a_copy(n, src, dst, yy * 2 + 1 - zh).start()
            if i:
                a2a_copy(n, src, dst, yy * 2 + zh).start()
        dst[sq] = src[sq]
        pending.append(functools.partial(all_to_all_done, n, src, dst))

    def all_to_all_send_half(n, src, dst, h):
        for i in (2, 1, 3, 0):
            yy = h * 4 + lax.rem(y + i, 4)
            a2a_copy(n, src, dst, yy * 2 + 1 - zh).start()

            @pl.when(yy != y)
            def _():
                a2a_copy(n, src, dst, yy * 2 + zh).start()

        if h:
            dst[sq] = src[sq]
            pending.append(functools.partial(all_to_all_done, n, src, dst))

    def all_to_all_wait(n, src, dst):
        for i in (0, 7, 1, 6, 2, 5, 3, 4):
            for other_line in range(2):
                if i or other_line:
                    peer = lax.rem(y + i, 8) * 2 + (1 - zh if other_line else zh)
                    wait_recv(dst.at[peer], a_ss.at[n, peer], a_rs.at[n, peer])

    def all_to_all_wait_half(n, src, dst, h):
        for i in (0, 3, 1, 2):
            yy = h * 4 + lax.rem(y + i, 4)

            @pl.when(yy != y)
            def _():
                peer = yy * 2 + zh
                wait_recv(dst.at[peer], a_ss.at[n, peer], a_rs.at[n, peer])

            peer = yy * 2 + 1 - zh
            wait_recv(dst.at[peer], a_ss.at[n, peer], a_rs.at[n, peer])

    def all_to_all_done(n, src, dst):
        def one(i, carry):
            a2a_copy(n, src, dst, lax.rem(sq + i, NSEQ)).wait_send()
            return carry

        lax.fori_loop(1, NSEQ, one, 0)

    def line_copy(peer):
        return pltpu.make_async_remote_copy(
            src_ref=a1s.at[peer], dst_ref=a1r.at[y],
            send_sem=a_ss.at[0, peer], recv_sem=a_rs.at[0, y],
            device_id=y_dev(peer), device_id_type=MESH,
        )

    def line_done():
        for i in FAR_FIRST:
            line_copy(lax.rem(y + i, 8)).wait_send()

    for cp in loads[0:3]:
        cp.wait()
    tin = column_of(ti_ref[...])
    section = mm(bm_ref[...], x_ref[...], 0, 1) * tin
    a1s[...] = section.astype(BF16).reshape(8, LINE, CH)

    rows = lax.broadcasted_iota(jnp.int32, (TOK, NSEQ), 0)
    cols = lax.broadcasted_iota(jnp.int32, (TOK, NSEQ), 1)
    for cp in loads[3:6]:
        cp.wait()
    cross = cm_ref[...]

    def iota(shape, dim):
        return lax.broadcasted_iota(jnp.int32, shape, dim)

    def flags(hit):
        return jnp.where(hit, 1.0, 0.0).astype(BF16)

    rows_here = flags(iota((8, NSEQ), 1) == 2 * iota((8, NSEQ), 0) + zh)
    cross_here = mm(rows_here, cross).astype(BF16)
    place = iota((NSEQ * LINE, NSEQ), 0)
    block = 2 * (place % TOK // LINE) + jnp.where(place < TOK, 1 - zh, zh)
    wide = mm(flags(block == iota((NSEQ * LINE, NSEQ), 1)), cross_here, 1, 1)
    wide = mm(wide.astype(BF16), flags(iota((8, TOK), 1) // LINE == iota((8, TOK), 0)))
    same_pos = iota((NSEQ * LINE, TOK), 0) % LINE == iota((NSEQ * LINE, TOK), 1) % LINE
    kron[...] = jnp.where(same_pos, wide, 0.0).astype(BF16)
    pick_block = flags(rows // POS == cols)
    pick_pos = jnp.where(rows % POS == cols, 1.0, 0.0)
    wide = mm(mm(pick_block, cross).astype(BF16), pick_block, 1, 1)
    same_pos = iota((TOK, TOK), 0) % POS == iota((TOK, TOK), 1) % POS
    kronT[...] = jnp.where(same_pos, wide, 0.0).astype(BF16)
    tout_all = jnp.broadcast_to(to_ref[...][:, None, :], (NSEQ, POS, POS)).reshape(TOK, POS)
    tout = jnp.sum(tout_all * pick_pos, axis=1, keepdims=True)
    flat = tn * CH + lax.broadcasted_iota(jnp.int32, (CH, 128), 0)
    lane = lax.broadcasted_iota(jnp.int32, (CH, 128), 1)
    gain = jnp.zeros((CH, 128), F32)
    for k in range(D // 128):
        gain = gain + jnp.where(flat == k * 128 + lane, gain_ref[k : k + 1, :], 0.0)
    gain = jnp.sum(gain, axis=1, keepdims=True)

    pl.semaphore_wait(barrier, 7 + 7 + (NTEN - 1))
    partner = (dp, y * 2 + 1 - zh, tn)
    for i in FAR_FIRST:
        line_copy(lax.rem(y + i, 8)).start()
    pending.append(line_done)
    a1r[y] = a1s[y]
    pl.semaphore_signal(cross_sem, inc=1, device_id=partner, device_id_type=MESH)
    to_pair[zh] = to_ref[...]
    send(to_pair.at[zh], to_pair.at[zh], tw_sem.at[0], tw_sem.at[1], partner)

    for cp in loads[6:]:
        cp.wait()
    eye_h = eye(HID)
    for r in range(NTEN):
        block = slice(r * CH, (r + 1) * CH)
        wguT[r, 0:HID, :] = mm(eye_h, wg[block, :], 1, 1).astype(BF16)
        wguT[r, HID : 2 * HID, :] = mm(eye_h, wu[block, :], 1, 1).astype(BF16)
        wdT[r] = mm(eye_h, wd[block, :], 1, 1).astype(BF16)
    eye_c = eye(CH)

    wait_recv(to_pair.at[1 - zh], tw_sem.at[0], tw_sem.at[1])
    tline = jnp.zeros((NSEQ * LINE, 1), F32)
    for half in range(2):
        spread = jnp.broadcast_to(to_pair[half][:, None, :], (NSEQ, LINE, POS)).reshape(NSEQ * LINE, POS)
        here = iota((NSEQ * LINE, POS), 0) % LINE == half * POS + iota((NSEQ * LINE, POS), 1)
        tline = tline + jnp.sum(jnp.where(here, spread, 0.0), axis=1, keepdims=True)
    pl.semaphore_wait(cross_sem, 1)
    for i in FAR_FIRST:
        peer = lax.rem(y + i, 8)
        wait_recv(a1r.at[peer], a_ss.at[0, peer], a_rs.at[0, peer])

    tline = tline.reshape(8, 2, LINE, 1)
    for own_line in range(2):
        part = zh if own_line else 1 - zh
        tw = jnp.where(part == 0, tline[:, 0], tline[:, 1]).reshape(TOK, 1)
        mixed = mm(kron[own_line * TOK : own_line * TOK + TOK, :], a1r[...].reshape(TOK, CH)) * tw
        mixed = mixed.reshape(8, LINE, CH)
        rest = mixed[:, :, LANES:CH]
        rest = jnp.concatenate([rest[:, 0:POS], rest[:, POS:LINE]], axis=2).astype(BF16)
        mixed = mixed[:, :, 0:LANES].astype(BF16)
        for ky in range(8):
            a2s[ky * 2 + part, 0:LINE, :] = mixed[ky]
            a2s[ky * 2 + part, LINE:PACKED, :] = rest[ky]
        for i in FAR_FIRST + (() if own_line else (0,)):
            a2a_copy(1, a2s, a2r, lax.rem(y + i, 8) * 2 + part).start()
    a2r[sq] = a2s[sq]
    pending.append(functools.partial(all_to_all_done, 1, a2s, a2r))

    halves = [slice(0, HT), slice(HT, TOK)]

    def residual(h):
        all_to_all_wait_half(1, a2s, a2r, h)
        terms = a2r[h * 8 : h * 8 + 8].astype(F32).reshape(4, 2, PACKED, LANES)
        terms = terms[:, 0] + terms[:, 1]
        rest = terms[:, LINE:PACKED]
        rest = jnp.concatenate([rest[:, :, 0 : CH - LANES], rest[:, :, CH - LANES : LANES]], axis=1)
        mixed = jnp.concatenate([terms[:, 0:LINE], rest], axis=2).astype(BF16).reshape(HT, CH)
        mixed = mm(eye_c, mixed, 1, 1)
        res = (x_ref[:, halves[h]].astype(F32) + mixed).astype(BF16).astype(F32)
        res_s[h] = res
        r1[h, tn] = (res * gain).astype(BF16)
        gather_start(0, h, r1)
        share_row(0, h, v1, jnp.sum(res * res, axis=0, keepdims=True))

    def share_row(n, h, buf, row):
        buf[h, tn] = jnp.broadcast_to(row, (8, HT))

        for i in (4, 5, 3, 6, 2, 7, 1):
            peer = lax.rem(tn + i, NTEN)
            pltpu.make_async_remote_copy(
                src_ref=buf.at[h, tn], dst_ref=buf.at[h, tn],
                send_sem=v_ss.at[n, h, peer], recv_sem=v_rs.at[n, h, tn],
                device_id=ten_dev(peer), device_id_type=MESH,
            ).start()
        pending.append(functools.partial(rows_done, n, h, buf))

    def sum_rows(n, h, buf):
        for i in range(1, NTEN):
            peer = lax.rem(tn + i, NTEN)
            wait_recv(buf.at[h, peer], v_ss.at[n, h, peer], v_rs.at[n, h, peer])
        return jnp.sum(buf[h, :, 0:1, :], axis=0)

    def rows_done(n, h, buf):
        def one(i, carry):
            peer = lax.rem(tn + i, NTEN)
            pltpu.make_async_remote_copy(
                src_ref=buf.at[h, tn], dst_ref=buf.at[h, tn],
                send_sem=v_ss.at[n, h, peer], recv_sem=v_rs.at[n, h, peer],
                device_id=ten_dev(peer), device_id_type=MESH,
            ).wait_send()
            return carry

        lax.fori_loop(1, NTEN, one, 0)

    chips = [lax.rem(x + d, 4) for d in range(4)]
    other = 1 - c

    def gather_start(n, h, buf):
        part = buf.at[h, tn]
        for d in (2, 1, 3):
            send(part, part, ag_ss.at[n, d, h], ag_rs.at[n, d, h], ten_dev(chips[d] * 2 + c))
        send(part, part, sib_ss.at[n, 0, h], sib_rs.at[n, 0, h], ten_dev(x * 2 + other))

    def gather_forward(n, h, buf, then=None):
        for d in (1, 3, 2):
            src = lax.rem(x + 4 - d, 4) * 2 + c
            part = buf.at[h, src]
            wait_recv(part, ag_ss.at[n, d, h], ag_rs.at[n, d, h])
            send(part, part, sib_ss.at[n, d, h], sib_rs.at[n, d, h], ten_dev(x * 2 + other))
            if then is not None:
                then(src // 2, c)

    def gather_own(n, h, buf, weights, acc):
        rank = x * 2 + other
        first = mm(weights[tn], buf[h, tn])
        wait_recv(buf.at[h, rank], sib_ss.at[n, 0, h], sib_rs.at[n, 0, h])
        acc[h] = first + mm(weights[rank], buf[h, rank])

    def gather_matmul(n, h, buf, weights, acc):
        total = acc[h]
        for d in (1, 3, 2):
            rank = lax.rem(x + 4 - d, 4) * 2 + c
            total = total + mm(weights[rank], buf[h, rank])
        for d in (1, 3, 2):
            rank = lax.rem(x + 4 - d, 4) * 2 + other
            wait_recv(buf.at[h, rank], sib_ss.at[n, d, h], sib_rs.at[n, d, h])
            total = total + mm(weights[rank], buf[h, rank])
        return total

    def scatter_start(n, h, part_of, p, sb):
        for d in (2, 1, 3, 0):
            p[h, d] = part_of(chips[d] * 2 + other).astype(BF16)
            send(p.at[h, d], sb.at[h, d], rsib_ss.at[n, h, d], rsib_rs.at[n, h, d], ten_dev(x * 2 + other))
        for d in (2, 1, 3, 0):
            own[h, d] = part_of(chips[d] * 2 + c)

    def scatter_mid(n, h, sb, q, t):
        for d in (2, 1, 3):
            wait_recv(sb.at[h, d], rsib_ss.at[n, h, d], rsib_rs.at[n, h, d])
            q[h, d] = (own[h, d] + sb[h, d].astype(F32)).astype(BF16)
            send(q.at[h, d], t.at[h, d], rs_ss.at[n, h, d], rs_rs.at[n, h, d], ten_dev(chips[d] * 2 + c))

    def scatter_end(n, h, sb, t):
        wait_recv(sb.at[h, 0], rsib_ss.at[n, h, 0], rsib_rs.at[n, h, 0])
        total = own[h, 0] + sb[h, 0].astype(F32)
        for d in (1, 3, 2):
            wait_recv(t.at[h, d], rs_ss.at[n, h, d], rs_rs.at[n, h, d])
            total = total + t[h, d].astype(F32)
        return total

    def rows_of(ref, r):
        return ref[pl.ds(pl.multiple_of(r * CH, CH), CH), :]

    inv = [None, None]

    def forward(h):
        pre = gather_matmul(0, h, r1, wguT, pre_s)
        inv[h] = lax.rsqrt(sum_rows(0, h, v1) / D + EPS)
        gate_pre = pre[0:HID] * inv[h]
        up_pre = pre[HID : 2 * HID] * inv[h]
        sig = jax.nn.sigmoid(gate_pre)
        hid_s[h] = (gate_pre * sig * up_pre).astype(BF16)
        gate_s[h] = gate_pre
        up_s[h] = up_pre
        scatter_start(0, h, lambda r: mm(rows_of(wd, r), hid_s[h]), p1, sb1)

    def cotangent(h):
        summed = res_s[h] + scatter_end(0, h, sb1, t1)
        r2[h, tn] = (summed - tgt_ref[:, halves[h]].astype(F32)).astype(BF16)
        gather_start(1, h, r2)
        out_ref[:, halves[h]] = summed.astype(BF16)

    def backward(h):
        d_hidden = gather_matmul(1, h, r2, wdT, back_s)
        gate_pre = gate_s[h]
        up_pre = up_s[h]
        sig = jax.nn.sigmoid(gate_pre)
        d_gate = (d_hidden * up_pre * sig * (1.0 + gate_pre * (1.0 - sig))).astype(BF16)
        d_up = (d_hidden * gate_pre * sig).astype(BF16)
        inner = d_gate.astype(F32) * gate_pre + d_up.astype(F32) * up_pre
        share_row(1, h, v2, jnp.sum(inner, axis=0, keepdims=True))
        scatter_start(1, h, lambda r: mm(rows_of(wg, r), d_gate) + mm(rows_of(wu, r), d_up), p2, sb2)

    def d_residual(h):
        d_normed = scatter_end(1, h, sb2, t2)
        corr = sum_rows(1, h, v2) / D
        d_res = r2[h, tn].astype(F32) + inv[h] * (gain * d_normed - res_s[h] * inv[h] * corr)
        dres_s[:, halves[h]] = d_res.astype(BF16)
        d_tok = mm(eye_h[0:HT, 0:HT], d_res.astype(BF16), 1, 1)
        a3s[h * 8 : h * 8 + 8] = d_tok.astype(BF16).reshape(8, POS, CH)
        all_to_all_send_half(2, a3s, a3r, h)

    sign = 1 - 2 * c

    def grad_rank(chip, yhi):
        cots = jnp.concatenate([r2[h, chip * 2 + yhi] for h in range(2)], axis=1)
        hids = jnp.concatenate([hid_s[h] for h in range(2)], axis=1)
        g = mm(cots, hids, 1, 1)
        first, second, third = (g[:, n * LANES : (n + 1) * LANES] for n in range(3))
        at = pl.multiple_of(chip * 48, 16)
        for m in range(4):
            ya[yhi * 4 + m, pl.ds(at, 48), :] = first[m * 48 : m * 48 + 48].astype(BF16)
        zat = pl.multiple_of(yhi * 96, 16)
        for half in range(2):
            pieces = [second[m * 48 + half * ROWS : m * 48 + half * ROWS + ROWS] for m in range(4)]
            zb[half * 4 + chip, pl.ds(zat, 96), :] = jnp.concatenate(pieces, axis=0).astype(BF16)

        @pl.when(chip < 2)
        def _():
            for m in range(4):
                ya[yhi * 4 + m, pl.ds(CH + at, 48), :] = third[m * 48 : m * 48 + 48].astype(BF16)

        @pl.when(chip >= 2)
        def _():
            for half in range(2):
                pieces = [third[m * 48 + half * ROWS : m * 48 + half * ROWS + ROWS] for m in range(4)]
                zb[half * 4 + chip, pl.ds(CH + zat, 96), :] = jnp.concatenate(pieces, axis=0).astype(BF16)

    def away(me, k):
        return lax.rem(me + sign * k + 8, 8)

    def sized(axis, target, work):
        if axis == 0:
            work(CH + 96)
            return

        @pl.when(lax.rem(target, 4) < 2)
        def _():
            work(CH)

        @pl.when(lax.rem(target, 4) >= 2)
        def _():
            work(2 * CH)

    AXES = ((ya, yr, y, y_dev), (zb, zr, z, z_dev))

    def grad_copy(axis, slot, to, target, rows):
        src, dst, me, dev = AXES[axis]
        return pltpu.make_async_remote_copy(
            src_ref=src.at[target, pl.ds(0, rows)], dst_ref=dst.at[slot, pl.ds(0, rows)],
            send_sem=g_ss.at[axis, slot], recv_sem=g_rs.at[axis, slot],
            device_id=dev(away(me, to)), device_id_type=MESH,
        )

    STEP1 = ((0, 2, 4), (1, 1, 3), (2, -1, -3))
    STEP2 = ((3, 1, 1), (4, -1, -1))
    STEP3 = ((5, 2, 2), (6, -2, -2))

    def grad_step(axis, sends):
        me = AXES[axis][2]
        for slot, to, place in sends:
            target = away(me, place)
            sized(axis, target, lambda rows: grad_copy(axis, slot, to, target, rows).start())

            def done(slot=slot, to=to, target=target):
                sized(axis, target, lambda rows: grad_copy(axis, slot, to, target, rows).wait_send())

            pending.append(done)

    def grad_add(axis, target, slots):
        buf, got, me, dev = AXES[axis]

        def work(rows):
            total = buf[target, 0:rows, :].astype(F32)
            for slot in slots:
                part = got.at[slot, pl.ds(0, rows)]
                wait_recv(part, g_ss.at[axis, slot], g_rs.at[axis, slot])
                total = total + part[...].astype(F32)
            buf[target, 0:rows, :] = total.astype(BF16)

        sized(axis, target, work)

    def grad_first():
        for axis in range(2):
            grad_step(axis, STEP1)

    def grad_middle():
        for axis in range(2):
            grad_step(axis, STEP2)
        for axis in range(2):
            me = AXES[axis][2]
            grad_add(axis, away(me, 2), (0, 1))
            grad_add(axis, away(me, -2), (2,))
            grad_step(axis, STEP3)

    def grad_second():
        total = ya[y].astype(F32)
        for slot in (3, 4, 6, 5):
            wait_recv(yr.at[slot], g_ss.at[0, slot], g_rs.at[0, slot])
            total = total + yr[slot].astype(F32)
        for zl in range(4):
            for half in range(2):
                at = zl * 48 + half * ROWS
                pieces = [total[at : at + ROWS]]
                if zl < 2:
                    pieces.append(total[CH + at : CH + at + ROWS])
                else:
                    pieces.append(jnp.zeros((ROWS, LANES), F32))
                y2s[half * 4 + zl] = jnp.concatenate(pieces, axis=0).astype(BF16)
        second_send(0, y2s, y2r, z, z_dev)

        def sum_z(rows):
            total = zb[z, 0:rows, :].astype(F32)
            for slot in (3, 4, 6, 5):
                part = zr.at[slot, pl.ds(0, rows)]
                wait_recv(part, g_ss.at[1, slot], g_rs.at[1, slot])
                total = total + part[...].astype(F32)
            for yy in range(8):
                pieces = [total[yy * ROWS : yy * ROWS + ROWS]]
                if rows > CH:
                    pieces.append(total[CH + yy * ROWS : CH + yy * ROWS + ROWS])
                else:
                    pieces.append(jnp.zeros((ROWS, LANES), F32))
                z2s[yy] = jnp.concatenate(pieces, axis=0).astype(BF16)

        sized(1, z, sum_z)
        second_send(1, z2s, z2r, y, y_dev)

    def second_send(n, src, dst, me, dev):
        for i in FAR_FIRST:
            peer = lax.rem(me + i, 8)
            pltpu.make_async_remote_copy(
                src_ref=src.at[peer], dst_ref=dst.at[me],
                send_sem=g2_ss.at[n, peer], recv_sem=g2_rs.at[n, me],
                device_id=dev(peer), device_id_type=MESH,
            ).start()
        pending.append(functools.partial(second_done, n, src, me, dev))

    def second_done(n, src, me, dev):
        def one(i, carry):
            peer = lax.rem(me + i, 8)
            pltpu.make_async_remote_copy(
                src_ref=src.at[peer], dst_ref=src.at[peer],
                send_sem=g2_ss.at[n, peer], recv_sem=g2_rs.at[n, peer],
                device_id=dev(peer), device_id_type=MESH,
            ).wait_send()
            return carry

        lax.fori_loop(1, 8, one, 0)

    def second_sum(n, src, dst, me):
        total = src[me].astype(F32)
        for i in (7, 1, 6, 2, 5, 3, 4):
            peer = lax.rem(me + i, 8)
            wait_recv(dst.at[peer], g2_ss.at[n, peer], g2_rs.at[n, peer])
            total = total + dst[peer].astype(F32)
        return total

    residual(0)
    residual(1)
    gather_own(0, 0, r1, wguT, pre_s)
    gather_own(0, 1, r1, wguT, pre_s)
    gather_forward(0, 0, r1)
    forward(0)
    gather_forward(0, 1, r1)
    scatter_mid(0, 0, sb1, q1, t1)
    forward(1)
    scatter_mid(0, 1, sb1, q1, t1)
    cotangent(0)
    cotangent(1)
    store(0, out_ref, out_hbm)
    grad_rank(x, c)
    gather_own(1, 0, r2, wdT, back_s)
    gather_own(1, 1, r2, wdT, back_s)
    grad_rank(x, other)
    gather_forward(1, 0, r2)
    backward(0)
    gather_forward(1, 1, r2)
    scatter_mid(1, 0, sb2, q2, t2)
    backward(1)
    for d in (1, 3, 2):
        grad_rank(chips[d], c)
    scatter_mid(1, 1, sb2, q2, t2)
    for d in (1, 3, 2):
        grad_rank(chips[d], other)
    earlier = list(pending)
    pending.clear()
    grad_first()
    d_residual(0)
    d_residual(1)
    grad_middle()
    for wait in earlier:
        wait()

    all_to_all_wait(2, a3s, a3r)
    weighted = (a3r[...].reshape(TOK, CH).astype(F32) * tout).astype(BF16)
    a4s[...] = mm(kronT[...], weighted).astype(BF16).reshape(NSEQ, POS, CH)
    all_to_all_send(3, a4s, a4r)
    grad_second()
    drain()

    all_to_all_wait(3, a4s, a4r)
    scaled = (a4r[...].reshape(TOK, CH).astype(F32) * tin).astype(BF16)
    d_mix = mm(scaled, bm_ref[...], 0, 1)
    din_ref[...] = (dres_s[...].astype(F32) + d_mix).astype(BF16)

    store(1, din_ref, din_hbm)

    rows_y = second_sum(0, y2s, y2r, z)
    rows_z = second_sum(1, z2s, z2r, y)
    gd_ref[:, 0:LANES] = rows_y[0:ROWS]
    gd_ref[:, LANES : 2 * LANES] = rows_z[0:ROWS]
    gd_ref[:, 2 * LANES : HID] = rows_y[ROWS:48] + rows_z[ROWS:48]
    store(2, gd_ref, gd_hbm)

    drain()


def finish(*refs):
    came, gone, held, sems = refs[0:3], refs[3:6], refs[6:9], refs[9]
    reads = [pltpu.make_async_copy(came[n], held[n], sems.at[0, n]) for n in range(3)]
    writes = [pltpu.make_async_copy(held[n], gone[n], sems.at[1, n]) for n in range(3)]
    for cp in reads:
        cp.start()
    for n in range(3):
        reads[n].wait()
        writes[n].start()
    for cp in writes:
        cp.wait()


def body(
    inputs, targets, block_mix, cross_mix, twiddle_in, twiddle_out, norm_gain, w_gate, w_up, w_down
):
    hbm = pl.BlockSpec(memory_space=pltpu.HBM)
    dma = pltpu.SemaphoreType.DMA
    chunks = pltpu.VMEM((NSEQ, POS, CH), BF16)
    blocks4 = pltpu.VMEM((2, 4, CH, HT), BF16)
    results = (
        jax.ShapeDtypeStruct((CH, TOK), BF16),
        jax.ShapeDtypeStruct((CH, TOK), BF16),
        jax.ShapeDtypeStruct((ROWS, HID), F32),
    )
    made = pl.pallas_call(
        kernel,
        out_shape=results,
        in_specs=[hbm] * 10,
        out_specs=(hbm, hbm, hbm),
        scratch_shapes=[
            pltpu.VMEM((CH, TOK), BF16),
            pltpu.VMEM((CH, TOK), BF16),
            pltpu.VMEM((ROWS, HID), F32),
            pltpu.VMEM((CH, TOK), BF16),
            pltpu.VMEM((CH, TOK), BF16),
            pltpu.VMEM((TOK, TOK), BF16),
            pltpu.VMEM((NSEQ, NSEQ), BF16),
            pltpu.VMEM((1, TOK), F32),
            pltpu.VMEM((NSEQ, POS), F32),
            pltpu.VMEM((D // 128, 128), F32),
            pltpu.VMEM((D, HID), BF16),
            pltpu.VMEM((D, HID), BF16),
            pltpu.VMEM((D, HID), BF16),
            pltpu.VMEM((NTEN, 2 * HID, CH), BF16),
            pltpu.VMEM((NTEN, HID, CH), BF16),
            pltpu.VMEM((NSEQ * LINE, TOK), BF16),
            pltpu.VMEM((TOK, TOK), BF16),
        ]
        + [pltpu.VMEM((8, LINE, CH), BF16)] * 2
        + [pltpu.VMEM((NSEQ, PACKED, LANES), BF16)] * 2
        + [chunks] * 4
        + [
            pltpu.VMEM((2, NTEN, CH, HT), BF16),
            pltpu.VMEM((2, NTEN, CH, HT), BF16),
            pltpu.VMEM((2, NTEN, 8, HT), F32),
            pltpu.VMEM((2, NTEN, 8, HT), F32),
        ]
        + [blocks4] * 8
        + [
            pltpu.VMEM((2, 4, CH, HT), F32),
            pltpu.VMEM((2, 2 * HID, HT), F32),
            pltpu.VMEM((2, HID, HT), F32),
            pltpu.VMEM((2, HID, HT), F32),
            pltpu.VMEM((2, HID, HT), F32),
            pltpu.VMEM((2, HID, HT), BF16),
            pltpu.VMEM((2, CH, HT), F32),
            pltpu.VMEM((CH, TOK), BF16),
            pltpu.VMEM((8, CH + 96, LANES), BF16),
            pltpu.VMEM((7, CH + 96, LANES), BF16),
            pltpu.VMEM((8, 2 * CH, LANES), BF16),
            pltpu.VMEM((7, 2 * CH, LANES), BF16),
            pltpu.VMEM((8, 48, LANES), BF16),
            pltpu.VMEM((8, 48, LANES), BF16),
            pltpu.VMEM((8, 48, LANES), BF16),
            pltpu.VMEM((8, 48, LANES), BF16),
            pltpu.VMEM((2, NSEQ, POS), F32),
            pltpu.SemaphoreType.REGULAR,
            dma((2,)),
            dma((3,)),
            dma((10,)),
            dma((4, NSEQ)),
            dma((4, NSEQ)),
            dma((2, 4, 2)),
            dma((2, 4, 2)),
            dma((2, 4, 2)),
            dma((2, 4, 2)),
            dma((2, 2, NTEN)),
            dma((2, 2, NTEN)),
            dma((2, 2, 4)),
            dma((2, 2, 4)),
            dma((2, 2, 4)),
            dma((2, 2, 4)),
            dma((2, 7)),
            dma((2, 7)),
            dma((2, 8)),
            dma((2, 8)),
        ],
        compiler_params=pltpu.CompilerParams(
            collective_id=0, has_side_effects=True, vmem_limit_bytes=64 * 1024 * 1024
        ),
        name="monarch_block",
    )(
        inputs[0].T,
        targets[0].T,
        block_mix,
        cross_mix,
        twiddle_in,
        twiddle_out,
        norm_gain.reshape(D // 128, 128),
        w_gate,
        w_up,
        w_down,
    )
    output, d_input, grad_down = pl.pallas_call(
        finish,
        out_shape=results,
        in_specs=[hbm] * 3,
        out_specs=(hbm, hbm, hbm),
        scratch_shapes=[
            pltpu.VMEM((CH, TOK), BF16),
            pltpu.VMEM((CH, TOK), BF16),
            pltpu.VMEM((ROWS, HID), F32),
            dma((2, 3)),
        ],
        compiler_params=pltpu.CompilerParams(vmem_limit_bytes=64 * 1024 * 1024),
        name="hand_over",
    )(*made)
    return output.T[None], d_input.T[None], grad_down


def solution(mesh):
    return jax.shard_map(
        body,
        mesh=mesh,
        in_specs=(
            P("dp", "seq", "tensor"),
            P("dp", "seq", "tensor"),
            P(),
            P(),
            P("seq", None),
            P(None, "seq"),
            P(),
            P(None, "tensor"),
            P(None, "tensor"),
            P(None, "tensor"),
        ),
        out_specs=(P("dp", "seq", "tensor"), P("dp", "seq", "tensor"), P(("dp", "seq"), "tensor")),
        check_vma=False,
    )
```
